32 devices in a mesh: fsdp: 4 (over y, x), ctx: 2 (over core), tp: 4 (over z).
Axes of the slice: x: 2, y: 2, z: 4, core: 2. Of those that a mesh axis runs over, the one named last changes fastest.
Arguments:
- hidden: bfloat16 [4, 4096, 1024], P('fsdp', 'ctx'), may hold values from -6 to 6
- segments: int32 [4, 4096], P('fsdp', 'ctx'), may hold values from 0 to 8, as said below
- out_grad: bfloat16 [4, 4096, 1024], P('fsdp', 'ctx'), may hold values from -6 to 6
- norm_gain: bfloat16 [1024], P(('fsdp', 'ctx')), may hold values from 0.25 to 1.75
- w_zx: bfloat16 [1024, 2, 2048], P(('fsdp', 'ctx'), None, 'tp'), may hold values from -0.1875 to 0.1875
- w_dt: bfloat16 [1024, 32], P(('fsdp', 'ctx'), 'tp'), may hold values from -0.1875 to 0.1875
- w_bc: bfloat16 [1024, 2, 128], P(('fsdp', 'ctx')), may hold values from -0.1875 to 0.1875
- conv_x_w: float32 [4, 2048], P(None, 'tp'), may hold values from -3 to 3
- conv_x_b: float32 [2048], P('tp'), may hold values from -2 to 2
- conv_bc_w: float32 [4, 2, 128], replicated, may hold values from -3 to 3
- conv_bc_b: float32 [2, 128], replicated, may hold values from -2 to 2
- dt_bias: float32 [32], P('tp'), may hold values from -5 to -2
- a_log: float32 [32], P('tp'), may hold values from -3 to 1.4
- skip_d: float32 [32], P('tp'), may hold values from 0.5 to 1.5
- out_gain: float32 [2048], P('tp'), may hold values from 0.25 to 1.75
- w_out: bfloat16 [2048, 1024], P('tp', ('fsdp', 'ctx')), may hold values from -0.125 to 0.125
Outputs:
- block_out: bfloat16 [4, 4096, 1024], P('fsdp', 'ctx')
- hidden_grad: float32 [4, 4096, 1024], P('fsdp', 'ctx')
- norm_gain_grad: float32 [1024], P(('fsdp', 'ctx'))
- w_zx_grad: float32 [1024, 2, 2048], P(('fsdp', 'ctx'), None, 'tp')
- w_dt_grad: float32 [1024, 32], P(('fsdp', 'ctx'), 'tp')
- w_bc_grad: float32 [1024, 2, 128], P(('fsdp', 'ctx'))
- conv_x_w_grad: float32 [4, 2048], P(None, 'tp')
- conv_x_b_grad: float32 [2048], P('tp')
- conv_bc_w_grad: float32 [4, 2, 128], replicated
- conv_bc_b_grad: float32 [2, 128], replicated
- dt_bias_grad: float32 [32], P('tp')
- a_log_grad: float32 [32], P('tp')
- skip_d_grad: float32 [32], P('tp')
- out_gain_grad: float32 [2048], P('tp')
- w_out_grad: float32 [2048, 1024], P('tp', ('fsdp', 'ctx'))
The draws below stay inside these ranges and needn't reach their ends.
Inputs may be any that keep to these rules, and one draw needn't show every extreme that they name: `segments`: in every sequence the segment numbers start at 0 and rise by 0 or 1 from one token to the next; every piece of 2048 tokens holds exactly 4 document starts, none at its first or last token, so that at every boundary between pieces the tokens on both sides lie in one document.
All inputs are finite; a program needn't handle non-finite values.
Results may differ from the reference program's by a relative error of at most 0.0099.
Values may be sent and summed in bfloat16 or wider, within the bound.
No kernel may reach another device: no remote copies, remote signals or barrier semaphores. Data moves between devices by JAX's collectives and lax.ppermute only.
A program may use at most 192 MiB of HBM per device.

```python
import jax
import jax.numpy as jnp
from jax import lax

D = 1024
HEADS = 32
HEADDIM = 64
STATE = 128
CONV = 4
BLOCK = 256
PIECE = 2048
SEQS = 4
LEN = 4096
INNER = 2048


def draw_segments(key, part):
    key = jax.random.fold_in(key, 7)
    pieces = LEN // PIECE
    per_piece = max(1, PIECE // 512)
    margin = max(4, min(LEN // 32, PIECE // 4))
    window = PIECE - 2 * margin
    scores = jax.random.randint(key, (SEQS, pieces, window), 0, 65536) * window + jnp.arange(window, dtype=jnp.int32)
    _, chosen = lax.top_k(scores, per_piece)
    starts = (jnp.arange(pieces, dtype=jnp.int32) * PIECE)[None, :, None] + margin + chosen.astype(jnp.int32)
    starts = starts.reshape(SEQS, pieces * per_piece)
    places = jnp.arange(LEN, dtype=jnp.int32)
    passed = starts[:, None, :] <= places[None, :, None]
    return jnp.sum(passed.astype(jnp.int32), axis=2)


def steps_of(stream_key, shape, split, low, top_value):
    def one(axis_at, blocks):
        heights = jax.random.uniform(jax.random.fold_in(jax.random.fold_in(stream_key, 6), axis_at), (blocks,), jnp.float32, low / len(split), top_value / len(split))
        return jnp.repeat(jnp.exp(heights), shape[axis_at] // blocks).reshape((-1,) + (1,) * (len(shape) - axis_at - 1))

    factor_of = one(*split[0])
    for cut in split[1:]:
        factor_of = factor_of * one(*cut)
    return factor_of


def normal_values(key, extent, deviation, bound, shards=(), held_as=jnp.bfloat16):
    factor_of = steps_of(key, extent, shards, -0.22, 0.18) if shards else 1.0
    array = jax.random.normal(key, extent, jnp.float32) * deviation * factor_of
    return jnp.minimum(jnp.maximum(array, -bound), bound).astype(held_as)


def setup_inputs(seed: int = 0) -> dict:
    splits = jax.random.split(jax.random.key(seed), 17)
    return {
        "hidden": normal_values(splits[0], (SEQS, LEN, D), 1.0, 6.0, ((0, 4), (1, 2))),
        "segments": draw_segments(jax.random.fold_in(splits[16], 71), 0),
        "out_grad": normal_values(splits[2], (SEQS, LEN, D), 1.0, 6.0, ((0, 4), (1, 2))),
        "norm_gain": jnp.clip(1.0 + 0.15 * jax.random.normal(splits[3], (D,), jnp.float32), 0.25, 1.75).astype(jnp.bfloat16),
        "w_zx": normal_values(splits[4], (D, 2, INNER), D ** -0.5, 0.1875, ((0, 8), (2, 4))),
        "w_dt": normal_values(splits[5], (D, HEADS), D ** -0.5, 0.1875, ((0, 8), (1, 4))),
        "w_bc": normal_values(splits[6], (D, 2, STATE), D ** -0.5, 0.1875, ((0, 8),)),
        "conv_x_w": normal_values(splits[7], (CONV, INNER), 0.5, 3.0, ((1, 4),), jnp.float32),
        "conv_x_b": normal_values(splits[8], (INNER,), 0.3, 2.0, ((0, 4),), jnp.float32),
        "conv_bc_w": normal_values(splits[9], (CONV, 2, STATE), 0.5, 3.0, (), jnp.float32),
        "conv_bc_b": normal_values(splits[10], (2, STATE), 0.3, 2.0, (), jnp.float32),
        "dt_bias": jnp.clip(-5.0 + 3.0 * jax.random.uniform(splits[11], (HEADS,), jnp.float32) ** steps_of(splits[11], (HEADS,), ((0, 4),), -0.2, 0.2), -5.0, -2.0),
        "a_log": jnp.clip(-3.0 + 4.4 * jax.random.uniform(splits[12], (HEADS,), jnp.float32) ** steps_of(splits[12], (HEADS,), ((0, 4),), -0.2, 0.2), -3.0, 1.4),
        "skip_d": jnp.clip(0.5 + 1.0 * jax.random.uniform(splits[13], (HEADS,), jnp.float32) ** steps_of(splits[13], (HEADS,), ((0, 4),), -0.2, 0.2), 0.5, 1.5),
        "out_gain": jnp.clip(1.0 + 0.15 * jax.random.normal(splits[14], (INNER,), jnp.float32), 0.25, 1.75),
        "w_out": normal_values(splits[15], (INNER, D), INNER ** -0.5, 0.125, ((0, 4), (1, 8))),
    }


EPSILON = 1e-05
PRECISE = lax.Precision.HIGHEST

@jax.custom_vjp
def low(v):
    return lax.optimization_barrier(v.astype(jnp.bfloat16)).astype(jnp.float32)

@jax.custom_vjp
def low_back(v):
    return v

def low_keep(v):
    return (low(v), None)

def low_pass(kept, grad):
    return (grad,)

def back_keep(v):
    return (v, None)

def back_low(kept, grad):
    return (low(grad),)
low.defvjp(low_keep, low_pass)
low_back.defvjp(back_keep, back_low)

def product(left, right):
    return jnp.dot(left, right, precision=PRECISE, preferred_element_type=jnp.float32)

def causal_conv(values, weight, offset_bias, segment, edge_values, edge_segment):
    joined = jnp.concatenate([edge_values, values], 0)
    joined_segment = jnp.concatenate([edge_segment, segment], 0)
    length = values.shape[0]
    summed = jnp.zeros_like(values) + offset_bias
    for offset in range(weight.shape[0]):
        source = joined[offset:offset + length]
        same_doc = (joined_segment[offset:offset + length] == segment).astype(values.dtype)
        summed = summed + weight[offset] * source * same_doc[:, None]
    return summed

def block_step(carried_in, block_data):
    ssm_state, last_segment = carried_in
    values, input_b, input_c, step_size, decay_rate, segment = block_data
    cumulative = jnp.cumsum(decay_rate, axis=0)
    places = jnp.arange(segment.shape[0])
    linked = (segment[:, None] == segment[None, :]) & (places[:, None] >= places[None, :])
    gap_values = jnp.where(linked[:, :, None], cumulative[:, None, :] - cumulative[None, :, :], 0.0)
    decay_mask = jnp.where(linked[:, :, None], jnp.exp(gap_values), 0.0)
    scores = product(input_c, input_b.T)
    weights = scores[:, :, None] * decay_mask * step_size[None, :, :]
    inside = jnp.einsum('tsh,shp->thp', weights, values, precision=PRECISE)
    entry_mask = (segment == last_segment).astype(decay_rate.dtype)[:, None] * jnp.exp(cumulative)
    carried = jnp.einsum('tn,hpn->thp', input_c, ssm_state, precision=PRECISE) * entry_mask[:, :, None]
    linked_end = linked[-1].astype(decay_rate.dtype)[:, None]
    tail_weight = linked_end * jnp.exp(cumulative[-1][None, :] - cumulative) * step_size
    new_state = entry_mask[-1][:, None, None] * ssm_state + jnp.einsum('sh,shp,sn->hpn', tail_weight, values, input_b, precision=PRECISE)
    return ((new_state, segment[-1]), inside + carried)

def mamba_mixer(hidden_row, segment, params):
    norm_gain, w_zx, w_dt, w_bc, conv_x_w, conv_x_b, conv_bc_w, conv_bc_b, dt_bias, a_log, skip_d, out_gain, w_out = params
    normed = hidden_row * lax.rsqrt(lax.optimization_barrier(jnp.mean(hidden_row * hidden_row, -1, keepdims=True)) + EPSILON) * norm_gain
    normed_low = low(normed)
    gate_raw = low_back(product(normed_low, w_zx[:, 0]))
    inner_pre = low_back(product(normed_low, w_zx[:, 1]))
    step_raw = low_back(product(normed_low, w_dt))
    state_pre = low_back(product(normed_low, w_bc.reshape(w_bc.shape[0], -1)))
    edge_count = conv_x_w.shape[0] - 1
    edge_segment = jnp.zeros((edge_count,), jnp.int32)
    inner_act = jax.nn.silu(causal_conv(inner_pre, conv_x_w, conv_x_b, segment, jnp.zeros((edge_count, INNER), jnp.float32), edge_segment))
    state_act = jax.nn.silu(causal_conv(state_pre, conv_bc_w.reshape(conv_bc_w.shape[0], -1), conv_bc_b.reshape(-1), segment, jnp.zeros((edge_count, 2 * STATE), jnp.float32), edge_segment))
    step_size = jax.nn.softplus(step_raw + dt_bias)
    decay_rate = -jnp.exp(a_log) * step_size
    blocks = LEN // BLOCK
    values = inner_act.reshape(LEN, HEADS, HEADDIM)
    stacked = (values.reshape(blocks, BLOCK, HEADS, HEADDIM), state_act[:, :STATE].reshape(blocks, BLOCK, STATE), state_act[:, STATE:].reshape(blocks, BLOCK, STATE), step_size.reshape(blocks, BLOCK, HEADS), decay_rate.reshape(blocks, BLOCK, HEADS), segment.reshape(blocks, BLOCK))
    initial = (jnp.zeros((HEADS, HEADDIM, STATE), jnp.float32), segment[0])
    _, outputs = lax.scan(jax.checkpoint(block_step), initial, stacked)
    scan_out = outputs.reshape(LEN, HEADS, HEADDIM) + skip_d[:, None] * values
    gated_inner = scan_out.reshape(LEN, INNER) * jax.nn.silu(gate_raw)
    normed_gate = gated_inner * lax.rsqrt(lax.optimization_barrier(jnp.mean(gated_inner * gated_inner, -1, keepdims=True)) + EPSILON) * out_gain
    return hidden_row + product(low(normed_gate), w_out)

def reference(hidden, segments, out_grad, norm_gain, w_zx, w_dt, w_bc, conv_x_w, conv_x_b, conv_bc_w, conv_bc_b, dt_bias, a_log, skip_d, out_gain, w_out):
    params = tuple((weight.astype(jnp.float32) for weight in (norm_gain, w_zx, w_dt, w_bc, conv_x_w, conv_x_b, conv_bc_w, conv_bc_b, dt_bias, a_log, skip_d, out_gain, w_out)))

    def one_sequence(totals, sequence_item):
        hidden_row, segment, cotangent = sequence_item
        result, pullback = jax.vjp(lambda row, weights: mamba_mixer(row, segment, weights), hidden_row.astype(jnp.float32), params)
        row_grad, weight_grads = pullback(cotangent.astype(jnp.float32))
        return (jax.tree.map(jnp.add, totals, weight_grads), (result.astype(jnp.bfloat16), row_grad))
    zero_grads = jax.tree.map(jnp.zeros_like, params)
    totals, (block_out, hidden_grad) = lax.scan(one_sequence, zero_grads, (hidden, segments, out_grad))
    return (block_out, hidden_grad, totals[0], totals[1], totals[2], totals[3], totals[4], totals[5], totals[6], totals[7], totals[8], totals[9], totals[10], totals[11], totals[12])
```

```python
import functools

import jax
import jax.numpy as jnp
from jax import lax
from jax.experimental import pallas as pl
from jax.experimental.pallas import tpu as pltpu
from jax.sharding import PartitionSpec as P

CHUNK = 128
STEP = 256
SUB = STEP // CHUNK
LANES = 128
EDGE = 16
GROUPS = 4
EPSILON = 1e-05
EXACT = lax.Precision.HIGHEST
F32 = jnp.float32
BF16 = jnp.bfloat16
NEGATIVE = -1e30
M1, M2, M3, ENTRY, TAIL, SEG, RAW = 16, 17, 18, 19, 20, 21, 24
VMEM_LIMIT = 56 * 1024 * 1024


def nn(a, b):
    return lax.dot_general(a, b, (((1,), (0,)), ((), ())), preferred_element_type=F32)


def nt(a, b):
    return lax.dot_general(a, b, (((1,), (1,)), ((), ())), preferred_element_type=F32)


def tn(a, b):
    return nn(a.T, b)


def exact(a, b):
    return lax.dot_general(
        a, b, (((1,), (0,)), ((), ())), precision=EXACT, preferred_element_type=F32
    )


def iota(shape, dim):
    return lax.broadcasted_iota(jnp.int32, shape, dim)


def spread(per_head, pairs):
    rows = per_head.shape[0]
    low = iota((rows, LANES), 1) < LANES // 2
    parts = []
    for j in range(pairs):
        left = jnp.broadcast_to(per_head[:, 2 * j : 2 * j + 1], (rows, LANES))
        right = jnp.broadcast_to(per_head[:, 2 * j + 1 : 2 * j + 2], (rows, LANES))
        parts.append(jnp.where(low, left, right))
    return jnp.concatenate(parts, 1)


def halves(block):
    low = iota(block.shape, 1) < LANES // 2
    zero = jnp.zeros_like(block)
    return jnp.where(low, block, zero), jnp.where(low, zero, block)


def silu(v):
    return v * jax.nn.sigmoid(v)


def rms_unit(x):
    return x * lax.rsqrt(jnp.mean(x * x, -1, keepdims=True) + EPSILON)


def front_kernel(
    hid, edge, tok, w, gain, cw, dtp,
    normed, gate, pre_out, u_out, rec, st, pdx, fin, pdfin,
    buf, state, decay,
):
    inner = gate.shape[1]
    wide = pre_out.shape[1]
    pairs = inner // LANES
    at = pl.program_id(0)

    @pl.when(at == 0)
    def _():
        edge_low = (rms_unit(edge[...].astype(F32)) * gain[...]).astype(BF16)
        edge_pre = nn(edge_low, w[:, inner : inner + wide])
        buf[0:8, :] = edge_pre[EDGE - 8 :, :]
        state[...] = jnp.zeros_like(state)
        decay[...] = jnp.ones_like(decay)

    @pl.when(at > 0)
    def _():
        buf[0:8, :] = buf[STEP : STEP + 8, :]

    low = (rms_unit(hid[...].astype(F32)) * gain[...]).astype(BF16)
    normed[...] = low
    gate[...] = nn(low, w[:, :inner])
    pre = nn(low, w[:, inner : inner + wide])
    pre_out[...] = pre
    buf[8 : 8 + STEP, :] = pre
    raw_all = nn(low, w[:, inner + wide :]) + dtp[0:1, :]
    marks = tok[...]
    u = cw[3:4, :] * pre + cw[4:5, :]
    u = u + cw[2:3, :] * (buf[7 : 7 + STEP, :] * marks[:, M1 : M1 + 1])
    u = u + cw[1:2, :] * (buf[6 : 6 + STEP, :] * marks[:, M2 : M2 + 1])
    u = u + cw[0:1, :] * (buf[5 : 5 + STEP, :] * marks[:, M3 : M3 + 1])
    u_out[...] = u
    act = silu(u)
    step_all = jax.nn.softplus(raw_all)
    lane = iota((CHUNK, LANES), 1)
    lower = (iota((CHUNK, CHUNK), 0) >= iota((CHUNK, CHUNK), 1)).astype(F32)
    for i in range(SUB):
        rows = slice(i * CHUNK, (i + 1) * CHUNK)
        step = step_all[rows]
        cum = exact(lower, step * dtp[1:2, :])
        mark = marks[rows]
        rec[rows, :] = jnp.where(
            lane < 8, cum, jnp.where(lane < 16, step, jnp.where(lane < 24, mark, raw_all[rows]))
        )
        last = cum[CHUNK - 1 :, :]
        tail = mark[:, TAIL : TAIL + 1] * jnp.exp(last - cum) * step
        fed = (act[rows, :inner] * spread(tail, pairs)).astype(BF16)
        st[i] = state[...]
        pdx[8 * i : 8 * i + 8, :] = decay[...]
        passed = spread(mark[CHUNK - 1 :, ENTRY : ENTRY + 1] * jnp.exp(last), pairs)
        input_b = act[rows, inner : inner + LANES].T.astype(BF16)
        state[...] = passed * state[...] + nn(input_b, fed)
        decay[...] = decay[...] * passed
    fin[...] = state[...]
    pdfin[...] = decay[...]


def front(hidden, edge, tok, w, gain, cw, dtp, inner, wide):
    rows, width = hidden.shape
    steps = rows // STEP
    state_size = LANES

    def whole(a):
        return pl.BlockSpec(a.shape, lambda i: (0,) * a.ndim)

    def tall(cols):
        return pl.BlockSpec((STEP, cols), lambda i: (i, 0))

    chunks = rows // CHUNK
    return pl.pallas_call(
        front_kernel,
        grid=(steps,),
        in_specs=[tall(width), whole(edge), tall(LANES), whole(w), whole(gain), whole(cw), whole(dtp)],
        out_specs=[
            tall(width),
            tall(inner),
            tall(wide),
            tall(wide),
            tall(LANES),
            pl.BlockSpec((SUB, state_size, inner), lambda i: (i, 0, 0)),
            pl.BlockSpec((8 * SUB, inner), lambda i: (i, 0)),
            pl.BlockSpec((state_size, inner), lambda i: (0, 0)),
            pl.BlockSpec((8, inner), lambda i: (0, 0)),
        ],
        out_shape=[
            jax.ShapeDtypeStruct((rows, width), BF16),
            jax.ShapeDtypeStruct((rows, inner), F32),
            jax.ShapeDtypeStruct((rows, wide), F32),
            jax.ShapeDtypeStruct((rows, wide), F32),
            jax.ShapeDtypeStruct((rows, LANES), F32),
            jax.ShapeDtypeStruct((chunks, state_size, inner), F32),
            jax.ShapeDtypeStruct((8 * chunks, inner), F32),
            jax.ShapeDtypeStruct((state_size, inner), F32),
            jax.ShapeDtypeStruct((8, inner), F32),
        ],
        scratch_shapes=[
            pltpu.VMEM((STEP + 8, wide), F32),
            pltpu.VMEM((state_size, inner), F32),
            pltpu.VMEM((8, inner), F32),
        ],
        compiler_params=pltpu.CompilerParams(
            dimension_semantics=("arbitrary",), vmem_limit_bytes=VMEM_LIMIT
        ),
        name="front",
    )(hidden, edge, tok, w, gain, cw, dtp)


def middle_kernel(
    u, rec, gate, st, pdx, sin, og, wo, prm,
    scan, dgate, sums, part,
):
    inner = gate.shape[1]
    pairs = inner // LANES
    d_gate = nn(og[...], wo[...])
    dgate[...] = d_gate
    act = silu(u[...])
    below = iota((CHUNK, CHUNK), 0) >= iota((CHUNK, CHUNK), 1)
    for i in range(SUB):
        rows = slice(i * CHUNK, (i + 1) * CHUNK)
        record = rec[rows, :]
        turned = record.T
        state = (st[i] + pdx[8 * i : 8 * i + 1, :] * sin[...]).astype(BF16)
        x = act[rows, :inner]
        input_b = act[rows, inner : inner + LANES].astype(BF16)
        input_c = act[rows, inner + LANES :].astype(BF16)
        scores = nt(input_c, input_b)
        barred = jnp.where(
            below & (record[:, SEG : SEG + 1] == turned[SEG : SEG + 1, :]), 0.0, NEGATIVE
        )
        entry = record[:, ENTRY : ENTRY + 1] * jnp.exp(record)
        outs = []
        for j in range(pairs):
            block = x[:, j * LANES : (j + 1) * LANES].astype(BF16)
            total = None
            for k, side in enumerate(halves(block)):
                h = 2 * j + k
                link = jnp.exp(record[:, h : h + 1] - turned[h : h + 1, :] + barred)
                weight = (scores * link * turned[8 + h : 9 + h, :]).astype(BF16)
                term = nn(weight, side)
                total = term if total is None else total + term
            outs.append(total)
        y = jnp.concatenate(outs, 1)
        y = y + nn(input_c, state) * spread(entry, pairs) + prm[0:1, :] * x
        scan[rows, :] = y
    gated = scan[...] * silu(gate[...])
    scaled = gated * prm[1:2, :]
    squares = jnp.sum(gated * gated, -1, keepdims=True)
    crosses = jnp.sum(scaled * d_gate, -1, keepdims=True)
    lane = iota((STEP, LANES), 1)
    both = jnp.where(lane == 0, squares, jnp.where(lane == 1, crosses, 0.0))
    sums[...] = both.T[0:8, :]
    part[...] = nt(scaled.astype(BF16), wo[...]).astype(BF16)


def middle(u, rec, gate, st, pdx, sin, og, wo, prm):
    rows, inner = gate.shape
    width = og.shape[1]

    def whole(a):
        return pl.BlockSpec(a.shape, lambda i: (0,) * a.ndim)

    def tall(cols):
        return pl.BlockSpec((STEP, cols), lambda i: (i, 0))

    return pl.pallas_call(
        middle_kernel,
        grid=(rows // STEP,),
        in_specs=[
            tall(u.shape[1]),
            tall(LANES),
            tall(inner),
            pl.BlockSpec((SUB,) + st.shape[1:], lambda i: (i, 0, 0)),
            pl.BlockSpec((8 * SUB, inner), lambda i: (i, 0)),
            whole(sin),
            tall(width),
            whole(wo),
            whole(prm),
        ],
        out_specs=[
            tall(inner),
            tall(inner),
            pl.BlockSpec((8, STEP), lambda i: (0, i)),
            tall(width),
        ],
        out_shape=[
            jax.ShapeDtypeStruct((rows, inner), F32),
            jax.ShapeDtypeStruct((rows, inner), F32),
            jax.ShapeDtypeStruct((8, rows), F32),
            jax.ShapeDtypeStruct((rows, width), BF16),
        ],
        compiler_params=pltpu.CompilerParams(
            dimension_semantics=("arbitrary",), vmem_limit_bytes=VMEM_LIMIT
        ),
        name="middle",
    )(u, rec, gate, st, pdx, sin, og, wo, prm)


def turn_kernel(
    inner_total, scan, gate, dgate, sums, upre_c, rec, prm,
    dscan, dgr, glow, adj, psx, fin, gain_grad,
    state, decay,
):
    inner = gate.shape[1]
    pairs = inner // LANES
    at = pl.program_id(0)

    @pl.when(at == 0)
    def _():
        state[...] = jnp.zeros_like(state)
        decay[...] = jnp.ones_like(decay)
        gain_grad[...] = jnp.zeros_like(gain_grad)

    head = sums[...]
    column = jnp.concatenate([head, jnp.zeros((LANES - 8, STEP), F32)], 0).T
    inv = lax.rsqrt(column[:, 0:1] / inner_total + EPSILON)
    cube = inv * inv * inv * (column[:, 1:2] / inner_total)
    raw = gate[...]
    sig = jax.nn.sigmoid(raw)
    sil = raw * sig
    y = scan[...]
    gated = y * sil
    unit = gated * inv
    d_gate = dgate[...]
    gain = prm[1:2, :]
    glow[...] = (unit * gain).astype(BF16)
    gain_grad[...] += jnp.broadcast_to(jnp.sum(d_gate * unit, 0, keepdims=True), gain_grad.shape)
    d_gated = inv * gain * d_gate - gated * cube
    d_scan = d_gated * sil
    dscan[...] = d_scan
    dgr[...] = (d_gated * y * (sig * (1.0 + raw * (1.0 - sig)))).astype(BF16)
    input_c = silu(upre_c[...])
    for i in reversed(range(SUB)):
        rows = slice(i * CHUNK, (i + 1) * CHUNK)
        record = rec[rows, :]
        entry = record[:, ENTRY : ENTRY + 1] * jnp.exp(record)
        adj[i] = state[...]
        psx[8 * i : 8 * i + 8, :] = decay[...]
        passed = spread(entry[CHUNK - 1 :, :], pairs)
        fed = (d_scan[rows] * spread(entry, pairs)).astype(BF16)
        state[...] = passed * state[...] + nn(input_c[rows].T.astype(BF16), fed)
        decay[...] = decay[...] * passed
    fin[...] = state[...]


def turn(scan, gate, dgate, sums, u, rec, prm, inner_total):
    rows, inner = gate.shape
    steps = rows // STEP
    chunks = rows // CHUNK
    state_size = LANES
    c_block = u.shape[1] // LANES - 1

    def whole(a):
        return pl.BlockSpec(a.shape, lambda i: (0,) * a.ndim)

    def tall(cols):
        return pl.BlockSpec((STEP, cols), lambda i: (steps - 1 - i, 0))

    return pl.pallas_call(
        functools.partial(turn_kernel, float(inner_total)),
        grid=(steps,),
        in_specs=[
            tall(inner),
            tall(inner),
            tall(inner),
            pl.BlockSpec((8, STEP), lambda i: (0, steps - 1 - i)),
            pl.BlockSpec((STEP, LANES), lambda i: (steps - 1 - i, c_block)),
            tall(LANES),
            whole(prm),
        ],
        out_specs=[
            tall(inner),
            tall(inner),
            tall(inner),
            pl.BlockSpec((SUB, state_size, inner), lambda i: (steps - 1 - i, 0, 0)),
            pl.BlockSpec((8 * SUB, inner), lambda i: (steps - 1 - i, 0)),
            pl.BlockSpec((state_size, inner), lambda i: (0, 0)),
            pl.BlockSpec((8, inner), lambda i: (0, 0)),
        ],
        out_shape=[
            jax.ShapeDtypeStruct((rows, inner), F32),
            jax.ShapeDtypeStruct((rows, inner), BF16),
            jax.ShapeDtypeStruct((rows, inner), BF16),
            jax.ShapeDtypeStruct((chunks, state_size, inner), F32),
            jax.ShapeDtypeStruct((8 * chunks, inner), F32),
            jax.ShapeDtypeStruct((state_size, inner), F32),
            jax.ShapeDtypeStruct((8, inner), F32),
        ],
        scratch_shapes=[pltpu.VMEM((state_size, inner), F32), pltpu.VMEM((8, inner), F32)],
        compiler_params=pltpu.CompilerParams(
            dimension_semantics=("arbitrary",), vmem_limit_bytes=VMEM_LIMIT
        ),
        name="turn",
    )(scan, gate, dgate, sums, u, rec, prm)


def back_kernel(
    u, rec, dscan, st, pdx, sin, adj, psx, ain, prm, dtp,
    dpre, dstep, skip_acc, head_acc,
):
    inner = dscan.shape[1]
    pairs = inner // LANES
    heads = 2 * pairs

    @pl.when(pl.program_id(0) == 0)
    def _():
        skip_acc[...] = jnp.zeros_like(skip_acc)
        head_acc[...] = jnp.zeros_like(head_acc)

    raw = u[...]
    sig = jax.nn.sigmoid(raw)
    act = raw * sig
    slope = sig * (1.0 + raw * (1.0 - sig))
    above = iota((CHUNK, CHUNK), 0) <= iota((CHUNK, CHUNK), 1)
    upper = above.astype(F32)
    lane = iota((CHUNK, LANES), 1)
    gather_heads = (iota((inner, LANES), 0) // (LANES // 2) == iota((inner, LANES), 1)).astype(BF16)
    nega = dtp[1:2, :]
    for i in range(SUB):
        rows = slice(i * CHUNK, (i + 1) * CHUNK)
        record = rec[rows, :]
        turned = record.T
        state = st[i] + pdx[8 * i : 8 * i + 1, :] * sin[...]
        state_low = state.astype(BF16)
        later = adj[i] + psx[8 * i : 8 * i + 1, :] * ain[...]
        later_low = later.astype(BF16)
        x = act[rows, :inner]
        b_wide = act[rows, inner : inner + LANES]
        c_wide = act[rows, inner + LANES :]
        input_b = b_wide.astype(BF16)
        input_c = c_wide.astype(BF16)
        dy = dscan[rows, :]
        scores = nt(input_b, input_c)
        barred = jnp.where(
            above & (record[:, SEG : SEG + 1] == turned[SEG : SEG + 1, :]), 0.0, NEGATIVE
        )
        step = pltpu.roll(record, LANES - 8, axis=1)
        z = pltpu.roll(record, LANES - RAW, axis=1)
        d_scores = jnp.zeros((CHUNK, CHUNK), F32)
        direct = jnp.zeros((CHUNK, LANES), F32)
        arrivals = []
        dxs = []
        for j in range(pairs):
            cols = slice(j * LANES, (j + 1) * LANES)
            x_sides = halves(x[:, cols].astype(BF16))
            dy_pair = dy[:, cols].astype(BF16)
            dy_sides = halves(dy_pair)
            total = None
            for k in range(2):
                h = 2 * j + k
                step_col = record[:, 8 + h : 9 + h]
                link = jnp.exp(turned[h : h + 1, :] - record[:, h : h + 1] + barred)
                d_link = nt(x_sides[k], dy_pair) * link
                d_scaled = d_link * step_col
                d_scores = d_scores + d_scaled
                flow = d_scaled * scores
                arrivals.append(jnp.sum(flow, 0, keepdims=True))
                given = jnp.sum(d_link * scores, 1, keepdims=True)
                direct = jnp.where(lane == h, given, direct)
                weight = (scores * link * step_col).astype(BF16)
                term = nn(weight, dy_sides[k])
                total = term if total is None else total + term
            dxs.append(total)
        dx = jnp.concatenate(dxs, 1)
        arrived = jnp.concatenate(arrivals + [jnp.zeros((CHUNK - heads, CHUNK), F32)], 0).T
        decay_in = record[:, ENTRY : ENTRY + 1] * jnp.exp(record)
        last = record[CHUNK - 1 :, :]
        tail_exp = record[:, TAIL : TAIL + 1] * jnp.exp(last - record)
        tail = tail_exp * step
        tail_wide = spread(jnp.where(lane < 8, tail, 0.0), pairs)
        fed_back = (dy * spread(decay_in, pairs)).astype(BF16)
        fed = (x * tail_wide).astype(BF16)
        from_state = nn(input_c, state_low)
        d_fed = nn(input_b, later_low)
        d_score_low = d_scores.astype(BF16)
        d_c = nt(fed_back, state_low) + nn(d_scores.T.astype(BF16), input_b)
        d_b = nt(fed, later_low) + nn(d_score_low, input_c)
        d_entry = nn((dy * from_state).astype(BF16), gather_heads)
        d_tail = nn((x * d_fed).astype(BF16), gather_heads)
        through = jnp.broadcast_to(jnp.sum(later * state, 0, keepdims=True), (16, inner))
        d_through = nn(through.astype(BF16), gather_heads)[0:1, :]
        dx = dx + d_fed * tail_wide + prm[0:1, :] * dy
        tail_flow = d_tail * tail
        d_cum = arrived - direct * step + d_entry * decay_in - tail_flow
        d_cum = jnp.where(lane < 8, d_cum, 0.0)
        d_last = jnp.sum(tail_flow, 0, keepdims=True) + decay_in[CHUNK - 1 :, :] * d_through
        d_rate = exact(upper, d_cum) + jnp.where(lane < 8, d_last, 0.0)
        d_step = direct + d_tail * tail_exp + nega * d_rate
        d_z = jnp.where(lane < 8, d_step * jax.nn.sigmoid(z), 0.0)
        dstep[rows, :] = d_z.astype(BF16)
        dpre[rows, :] = jnp.concatenate([dx, d_b, d_c], 1) * slope[rows]
        skip_acc[...] += jnp.broadcast_to(jnp.sum(dy * x, 0, keepdims=True), skip_acc.shape)
        head_acc[0:1, :] += jnp.sum(d_z, 0, keepdims=True)
        head_acc[1:2, :] += jnp.sum(
            jnp.where(lane < 8, d_rate * (nega * step), 0.0), 0, keepdims=True
        )


def back(u, rec, dscan, st, pdx, sin, adj, psx, ain, prm, dtp, group):
    rows, inner = dscan.shape
    steps = rows // STEP // GROUPS
    wide = u.shape[1]
    first = group * steps

    def whole(a):
        return pl.BlockSpec(a.shape, lambda i: (0,) * a.ndim)

    def tall(cols):
        return pl.BlockSpec((STEP, cols), lambda i: (first + i, 0))

    def out_tall(cols):
        return pl.BlockSpec((STEP, cols), lambda i: (i, 0))

    states = pl.BlockSpec((SUB,) + st.shape[1:], lambda i: (first + i, 0, 0))
    decays = pl.BlockSpec((8 * SUB, inner), lambda i: (first + i, 0))
    return pl.pallas_call(
        back_kernel,
        grid=(steps,),
        in_specs=[
            tall(wide), tall(LANES), tall(inner), states, decays, whole(sin),
            states, decays, whole(ain), whole(prm), whole(dtp),
        ],
        out_specs=[
            out_tall(wide),
            out_tall(LANES),
            pl.BlockSpec((8, inner), lambda i: (0, 0)),
            pl.BlockSpec((8, LANES), lambda i: (0, 0)),
        ],
        out_shape=[
            jax.ShapeDtypeStruct((steps * STEP, wide), F32),
            jax.ShapeDtypeStruct((steps * STEP, LANES), BF16),
            jax.ShapeDtypeStruct((8, inner), F32),
            jax.ShapeDtypeStruct((8, LANES), F32),
        ],
        compiler_params=pltpu.CompilerParams(
            dimension_semantics=("arbitrary",), vmem_limit_bytes=VMEM_LIMIT
        ),
        name="back",
    )(u, rec, dscan, st, pdx, sin, adj, psx, ain, prm, dtp)


def rear_kernel(
    dpre, rec, pre, dgr, dstep, follow, hid, w, cw,
    dproj, dnorm, conv_acc, gain_acc,
    buf, mbuf,
):
    wide = dpre.shape[1]
    inner = dgr.shape[1]

    @pl.when(pl.program_id(0) == 0)
    def _():
        buf[STEP : STEP + 8, :] = follow[:, :wide]
        mbuf[STEP : STEP + 8, :] = follow[:, wide:]
        conv_acc[...] = jnp.zeros_like(conv_acc)
        gain_acc[...] = jnp.zeros_like(gain_acc)

    @pl.when(pl.program_id(0) > 0)
    def _():
        buf[STEP : STEP + 8, :] = buf[0:8, :]
        mbuf[STEP : STEP + 8, :] = mbuf[0:8, :]

    grad = dpre[...]
    buf[0:STEP, :] = grad
    mbuf[0:STEP, :] = rec[...]
    value = pre[...]
    total = cw[3:4, :] * grad
    conv_acc[3:4, :] += jnp.sum(value * grad, 0, keepdims=True)
    conv_acc[4:5, :] += jnp.sum(grad, 0, keepdims=True)
    for shift in (1, 2, 3):
        mark = mbuf[shift : shift + STEP, :][:, M1 + shift - 1 : M1 + shift]
        moved = buf[shift : shift + STEP, :] * mark
        total = total + cw[3 - shift : 4 - shift, :] * moved
        conv_acc[3 - shift : 4 - shift, :] += jnp.sum(value * moved, 0, keepdims=True)
    dproj[:, :inner] = dgr[...]
    dproj[:, inner : inner + wide] = total.astype(BF16)
    dproj[:, inner + wide :] = dstep[...]
    grad_in = nt(dproj[...], w[...])
    dnorm[...] = grad_in.astype(BF16)
    unit = rms_unit(hid[...].astype(F32))
    gain_acc[...] += jnp.broadcast_to(jnp.sum(grad_in * unit, 0, keepdims=True), gain_acc.shape)


def rear(dpre, rec, pre, dgr, dstep, follow, hid, w, cw, group):
    rows, wide = dpre.shape
    steps = rows // STEP
    inner = dgr.shape[1]
    width, packed = w.shape
    first = group * steps

    def whole(a):
        return pl.BlockSpec(a.shape, lambda i: (0,) * a.ndim)

    def tall(cols):
        return pl.BlockSpec((STEP, cols), lambda i: (first + steps - 1 - i, 0))

    def own(cols):
        return pl.BlockSpec((STEP, cols), lambda i: (steps - 1 - i, 0))

    return pl.pallas_call(
        rear_kernel,
        grid=(steps,),
        in_specs=[
            own(wide), tall(LANES), tall(wide), tall(inner), own(LANES), whole(follow),
            tall(width), whole(w), whole(cw),
        ],
        out_specs=[
            own(packed),
            own(width),
            pl.BlockSpec((8, wide), lambda i: (0, 0)),
            pl.BlockSpec((8, width), lambda i: (0, 0)),
        ],
        out_shape=[
            jax.ShapeDtypeStruct((rows, packed), BF16),
            jax.ShapeDtypeStruct((rows, width), BF16),
            jax.ShapeDtypeStruct((8, wide), F32),
            jax.ShapeDtypeStruct((8, width), F32),
        ],
        scratch_shapes=[
            pltpu.VMEM((STEP + 8, wide), F32),
            pltpu.VMEM((STEP + 8, LANES), F32),
        ],
        compiler_params=pltpu.CompilerParams(
            dimension_semantics=("arbitrary",), vmem_limit_bytes=VMEM_LIMIT
        ),
        name="rear",
    )(dpre, rec, pre, dgr, dstep, follow, hid, w, cw)


def passed_along(value, axis, steps):
    count = lax.axis_size(axis)
    leading, last = (max(0, -steps), min(count, count - steps))
    return lax.ppermute(value, axis, [(source, source + steps) for source in range(leading, last)])


def chained(own, decay, axis, steps):
    entering = jnp.zeros_like(own)
    for turn_at in range(lax.axis_size(axis) - 1):
        leaving = own if turn_at == 0 else own + decay * entering
        entering = passed_along(leaving, axis, steps)
    return entering


def token_marks(segment, before):
    rows = segment.shape[0]
    joined = jnp.concatenate([before, segment])
    marks = [joined[3 - j : 3 - j + rows] == segment for j in (1, 2, 3)]
    blocks = segment.reshape(-1, CHUNK)
    previous = jnp.concatenate([before[2:], blocks[:-1, -1]])
    marks.append((blocks == previous[:, None]).reshape(-1))
    marks.append((blocks == blocks[:, -1:]).reshape(-1))
    marks.append(segment)
    table = jnp.stack([mark.astype(F32) for mark in marks], 1)
    return jnp.pad(table, ((0, 0), (M1, LANES - M1 - len(marks))))


def body(
    hidden, segments, out_grad, norm_gain, w_zx, w_dt, w_bc, conv_x_w, conv_x_b,
    conv_bc_w, conv_bc_b, dt_bias, a_log, skip_d, out_gain, w_out,
):
    _, rows, width = hidden.shape
    inner = w_zx.shape[2]
    heads = w_dt.shape[1]
    head_size = inner // heads
    state_size = w_bc.shape[2]
    wide = inner + 2 * state_size
    taps = conv_x_w.shape[0]
    owned = w_zx.shape[0]
    shards = ("fsdp", "ctx")
    hid = hidden[0]
    cot = out_grad[0]
    segment = segments[0]

    packed = jnp.concatenate(
        [
            w_zx.reshape(owned, 2 * inner),
            w_bc.reshape(owned, 2 * state_size),
            w_dt, w_dt, w_dt, w_dt,
            norm_gain[:, None],
            jnp.zeros((owned, LANES - 4 * heads - 1), BF16),
        ],
        1,
    )
    w_in = lax.all_gather(packed, shards, axis=0, tiled=True)
    wo = lax.all_gather(w_out.T, shards, axis=0, tiled=True)
    gain_at = 2 * inner + 2 * state_size + 4 * heads
    gain = w_in[:, gain_at].astype(F32)[None, :]

    edge, edge_segment = passed_along((hid[rows - EDGE :], segment[rows - 3 :]), "ctx", 1)
    tok = token_marks(segment, edge_segment)
    conv_rows = jnp.concatenate(
        [
            jnp.concatenate([conv_x_w, conv_bc_w.reshape(taps, -1)], 1),
            jnp.concatenate([conv_x_b, conv_bc_b.reshape(-1)])[None],
            jnp.zeros((8 - taps - 1, wide), F32),
        ],
        0,
    )
    spare = jnp.zeros((LANES - 4 * heads,), F32)
    rate = -jnp.exp(a_log)
    dtp = jnp.concatenate(
        [
            jnp.concatenate([dt_bias] * 4 + [spare])[None],
            jnp.concatenate([rate] * 4 + [spare])[None],
            jnp.zeros((6, LANES), F32),
        ],
        0,
    )
    prm = jnp.concatenate(
        [jnp.repeat(skip_d, head_size)[None], out_gain[None], jnp.zeros((6, inner), F32)], 0
    )

    normed, gate, pre, u, rec, st, pdx, state_end, decay_end = front(
        hid, edge, tok, w_in, gain, conv_rows, dtp, inner, wide
    )
    sin = chained(state_end, decay_end[:1], "ctx", 1)
    scan, dgate, sums, part = middle(u, rec, gate, st, pdx, sin, cot, wo, prm)
    sums = lax.psum(sums, "tp")
    out_sum = lax.psum(part, "tp")
    inner_total = inner * lax.axis_size("tp")
    dscan, dgr, glow, adj, psx, adj_start, out_gain_acc = turn(
        scan, gate, dgate, sums, u, rec, prm, inner_total
    )
    ain = chained(adj_start, decay_end[:1], "ctx", -1)
    inv_gate = lax.rsqrt(sums[0] / inner_total + EPSILON)[:, None]
    block_out = (hid.astype(F32) + inv_gate * out_sum.astype(F32)).astype(BF16)

    backs = []
    for group in range(GROUPS):
        backs.append(back(u, rec, dscan, st, pdx, sin, adj, psx, ain, prm, dtp, group))
    group_rows = rows // GROUPS
    heads_of = [
        jnp.concatenate([backs[g][0][:8], rec[g * group_rows : g * group_rows + 8]], 1)
        for g in range(GROUPS)
    ]
    follows = heads_of[1:] + [passed_along(heads_of[0], "ctx", -1)]
    rears = []
    d_normed = []
    for group in range(GROUPS):
        rears.append(
            rear(
                backs[group][0], rec, pre, dgr, backs[group][1], follows[group], hid, w_in,
                conv_rows, group,
            )
        )
        d_normed.append(lax.psum(rears[-1][1], "tp"))
    dproj = jnp.concatenate([r[0] for r in rears], 0)
    conv_acc = sum(r[2] for r in rears)
    gain_acc = sum(r[3][0] for r in rears)
    skip_acc = sum(b[2][0] for b in backs)
    head_acc = sum(b[3] for b in backs)

    contract_rows = (((0,), (0,)), ((), ()))
    w_grad = lax.dot_general(normed, dproj, contract_rows, preferred_element_type=F32)
    wo_grad = lax.dot_general(cot, glow, contract_rows, preferred_element_type=F32)
    w_grad = w_grad.at[:, gain_at].set(gain_acc)
    w_owned = lax.psum_scatter(w_grad, shards, scatter_dimension=0, tiled=True)
    wo_owned = lax.psum_scatter(wo_grad, shards, scatter_dimension=0, tiled=True)

    small = jnp.concatenate(
        [
            conv_acc[: taps + 1].reshape(-1),
            out_gain_acc[0],
            skip_acc,
            head_acc[:2].reshape(-1),
        ]
    )
    small = lax.psum(small, shards)
    conv_sum = small[: (taps + 1) * wide].reshape(taps + 1, wide)
    rest = small[(taps + 1) * wide :]
    shared = jnp.concatenate(
        [
            w_owned[:, 2 * inner : 2 * inner + 2 * state_size].reshape(-1),
            w_owned[:, gain_at],
            conv_sum[:, inner:].reshape(-1),
        ]
    )
    shared = lax.psum(shared, "tp")
    bc_size = owned * 2 * state_size
    bc_owned = shared[:bc_size].reshape(owned, 2, state_size)
    gain_owned = shared[bc_size : bc_size + owned]
    conv_bc = shared[bc_size + owned :].reshape(taps + 1, 2, state_size)

    tokens = hid.astype(F32)
    inv_rms = lax.rsqrt(jnp.mean(tokens * tokens, -1, keepdims=True) + EPSILON)
    grads = []
    for group in range(GROUPS):
        span = slice(group * group_rows, (group + 1) * group_rows)
        scaled = d_normed[group].astype(F32) * gain
        inv = inv_rms[span]
        cross = jnp.sum(scaled * tokens[span], -1, keepdims=True) / width
        grads.append(
            cot[span].astype(F32) + inv * scaled - tokens[span] * (inv * inv * inv * cross)
        )
    hidden_grad = jnp.concatenate(grads, 0)

    return (
        block_out[None],
        hidden_grad[None],
        gain_owned,
        w_owned[:, : 2 * inner].reshape(owned, 2, inner),
        w_owned[:, 2 * inner + 2 * state_size : 2 * inner + 2 * state_size + heads],
        bc_owned,
        conv_sum[:taps, :inner],
        conv_sum[taps, :inner],
        conv_bc[:taps],
        conv_bc[taps],
        rest[2 * inner : 2 * inner + heads],
        rest[2 * inner + LANES : 2 * inner + LANES + heads],
        jnp.sum(rest[inner : 2 * inner].reshape(heads, head_size), 1),
        rest[:inner],
        wo_owned.T,
    )


def solution(mesh):
    placed = (
        P("fsdp", "ctx", None),
        P("fsdp", "ctx"),
        P("fsdp", "ctx", None),
        P(("fsdp", "ctx")),
        P(("fsdp", "ctx"), None, "tp"),
        P(("fsdp", "ctx"), "tp"),
        P(("fsdp", "ctx"), None, None),
        P(None, "tp"),
        P("tp"),
        P(),
        P(),
        P("tp"),
        P("tp"),
        P("tp"),
        P("tp"),
        P("tp", ("fsdp", "ctx")),
    )
    return jax.shard_map(
        body,
        mesh=mesh,
        in_specs=placed,
        out_specs=(
            P("fsdp", "ctx", None),
            P("fsdp", "ctx", None),
            P(("fsdp", "ctx")),
            P(("fsdp", "ctx"), None, "tp"),
            P(("fsdp", "ctx"), "tp"),
            P(("fsdp", "ctx"), None, None),
            P(None, "tp"),
            P("tp"),
            P(),
            P(),
            P("tp"),
            P("tp"),
            P("tp"),
            P("tp"),
            P("tp", ("fsdp", "ctx")),
        ),
        check_vma=False,
    )
```

```python
import functools

import jax
import jax.numpy as jnp
from jax import lax
from jax.experimental import pallas as pl
from jax.experimental.pallas import tpu as pltpu
from jax.sharding import PartitionSpec as P

CHUNK = 128
STEP = 256
SUB = STEP // CHUNK
LANES = 128
EDGE = 16
GROUPS = 4
EPSILON = 1e-05
EXACT = lax.Precision.HIGHEST
F32 = jnp.float32
BF16 = jnp.bfloat16
NEGATIVE = -1e30
M1, M2, M3, ENTRY, TAIL, SEG, RAW = 16, 17, 18, 19, 20, 21, 24
VMEM_LIMIT = 56 * 1024 * 1024


def nn(a, b):
    return lax.dot_general(a, b, (((1,), (0,)), ((), ())), preferred_element_type=F32)


def nt(a, b):
    return lax.dot_general(a, b, (((1,), (1,)), ((), ())), preferred_element_type=F32)


def tn(a, b):
    return nn(a.T, b)


def exact(a, b):
    return lax.dot_general(
        a, b, (((1,), (0,)), ((), ())), precision=EXACT, preferred_element_type=F32
    )


def lasts(microseconds):
    return pl.CostEstimate(
        flops=0, bytes_accessed=int(microseconds * 3.69e6), transcendentals=0
    )


ANYWHERE = pl.BlockSpec(memory_space=pl.ANY)


def ordered(kernel, inputs, after):
    def run(*refs):
        kernel(*refs[:inputs], *refs[inputs + after :])

    return run


def iota(shape, dim):
    return lax.broadcasted_iota(jnp.int32, shape, dim)


def spread(per_head, pairs):
    rows = per_head.shape[0]
    low = iota((rows, LANES), 1) < LANES // 2
    parts = []
    for j in range(pairs):
        left = jnp.broadcast_to(per_head[:, 2 * j : 2 * j + 1], (rows, LANES))
        right = jnp.broadcast_to(per_head[:, 2 * j + 1 : 2 * j + 2], (rows, LANES))
        parts.append(jnp.where(low, left, right))
    return jnp.concatenate(parts, 1)


def halves(block):
    low = iota(block.shape, 1) < LANES // 2
    zero = jnp.zeros_like(block)
    return jnp.where(low, block, zero), jnp.where(low, zero, block)


def silu(v):
    return v * jax.nn.sigmoid(v)


def rms_unit(x):
    return x * lax.rsqrt(jnp.mean(x * x, -1, keepdims=True) + EPSILON)


def front_kernel(
    gain_lane, starts, hid, edge, tok, cw, dtp, *refs
):
    (normed, gate, pre_out, u_out, rec, st, pdx, fin, pdfin, w, gain_out,
     buf, state, decay) = refs[-14:]
    shards = refs[:-14]
    inner = gate.shape[1]
    wide = pre_out.shape[1]
    pairs = inner // LANES
    at = pl.program_id(0)

    @pl.when(at == 0)
    def _():
        for k, shard in enumerate(shards):
            size = shard.shape[0]
            w[pl.ds(pl.multiple_of(starts[k], 16), size), :] = shard[...]
        for k in range(w.shape[0] // LANES):
            tile = w[k * LANES : (k + 1) * LANES, inner + wide :].astype(F32).T
            gain_out[:, k * LANES : (k + 1) * LANES] = jnp.broadcast_to(
                tile[gain_lane : gain_lane + 1, :], (8, LANES)
            )
        edge_low = (rms_unit(edge[...].astype(F32)) * gain_out[0:1, :]).astype(BF16)
        edge_pre = nn(edge_low, w[:, inner : inner + wide])
        buf[0:8, :] = edge_pre[EDGE - 8 :, :]
        state[...] = jnp.zeros_like(state)
        decay[...] = jnp.ones_like(decay)

    @pl.when(at > 0)
    def _():
        buf[0:8, :] = buf[STEP : STEP + 8, :]

    low = (rms_unit(hid[...].astype(F32)) * gain_out[0:1, :]).astype(BF16)
    normed[...] = low
    gate[...] = nn(low, w[:, :inner])
    pre = nn(low, w[:, inner : inner + wide])
    pre_out[...] = pre
    buf[8 : 8 + STEP, :] = pre
    raw_all = nn(low, w[:, inner + wide :]) + dtp[0:1, :]
    marks = tok[...]
    u = cw[3:4, :] * pre + cw[4:5, :]
    u = u + cw[2:3, :] * (buf[7 : 7 + STEP, :] * marks[:, M1 : M1 + 1])
    u = u + cw[1:2, :] * (buf[6 : 6 + STEP, :] * marks[:, M2 : M2 + 1])
    u = u + cw[0:1, :] * (buf[5 : 5 + STEP, :] * marks[:, M3 : M3 + 1])
    u_out[...] = u
    act = silu(u)
    step_all = jax.nn.softplus(raw_all)
    lane = iota((CHUNK, LANES), 1)
    lower = (iota((CHUNK, CHUNK), 0) >= iota((CHUNK, CHUNK), 1)).astype(F32)
    for i in range(SUB):
        rows = slice(i * CHUNK, (i + 1) * CHUNK)
        step = step_all[rows]
        cum = exact(lower, step * dtp[1:2, :])
        mark = marks[rows]
        rec[rows, :] = jnp.where(
            lane < 8, cum, jnp.where(lane < 16, step, jnp.where(lane < 24, mark, raw_all[rows]))
        )
        last = cum[CHUNK - 1 :, :]
        tail = mark[:, TAIL : TAIL + 1] * jnp.exp(last - cum) * step
        fed = (act[rows, :inner] * spread(tail, pairs)).astype(BF16)
        st[i] = state[...]
        pdx[8 * i : 8 * i + 8, :] = decay[...]
        passed = spread(mark[CHUNK - 1 :, ENTRY : ENTRY + 1] * jnp.exp(last), pairs)
        input_b = act[rows, inner : inner + LANES].T.astype(BF16)
        state[...] = passed * state[...] + nn(input_b, fed)
        decay[...] = decay[...] * passed
    fin[...] = state[...]
    pdfin[...] = decay[...]


def front(hidden, edge, tok, shards, starts, gain_lane, cw, dtp, inner, wide):
    rows, width = hidden.shape
    packed = shards[0].shape[1]
    steps = rows // STEP
    state_size = LANES

    def whole(a):
        return pl.BlockSpec(a.shape, lambda i: (0,) * a.ndim)

    def tall(cols):
        return pl.BlockSpec((STEP, cols), lambda i: (i, 0))

    chunks = rows // CHUNK
    return pl.pallas_call(
        functools.partial(front_kernel, gain_lane),
        grid=(steps,),
        in_specs=[
            pl.BlockSpec(memory_space=pltpu.SMEM),
            tall(width),
            whole(edge),
            tall(LANES),
            whole(cw),
            whole(dtp),
        ]
        + [whole(shard) for shard in shards],
        out_specs=[
            tall(width),
            tall(inner),
            tall(wide),
            tall(wide),
            tall(LANES),
            pl.BlockSpec((SUB, state_size, inner), lambda i: (i, 0, 0)),
            pl.BlockSpec((8 * SUB, inner), lambda i: (i, 0)),
            pl.BlockSpec((state_size, inner), lambda i: (0, 0)),
            pl.BlockSpec((8, inner), lambda i: (0, 0)),
            pl.BlockSpec((width, packed), lambda i: (0, 0)),
            pl.BlockSpec((8, width), lambda i: (0, 0)),
        ],
        out_shape=[
            jax.ShapeDtypeStruct((rows, width), BF16),
            jax.ShapeDtypeStruct((rows, inner), F32),
            jax.ShapeDtypeStruct((rows, wide), F32),
            jax.ShapeDtypeStruct((rows, wide), F32),
            jax.ShapeDtypeStruct((rows, LANES), F32),
            jax.ShapeDtypeStruct((chunks, state_size, inner), F32),
            jax.ShapeDtypeStruct((8 * chunks, inner), F32),
            jax.ShapeDtypeStruct((state_size, inner), F32),
            jax.ShapeDtypeStruct((8, inner), F32),
            jax.ShapeDtypeStruct((width, packed), BF16),
            jax.ShapeDtypeStruct((8, width), F32),
        ],
        scratch_shapes=[
            pltpu.VMEM((STEP + 8, wide), F32),
            pltpu.VMEM((state_size, inner), F32),
            pltpu.VMEM((8, inner), F32),
        ],
        compiler_params=pltpu.CompilerParams(
            dimension_semantics=("arbitrary",), vmem_limit_bytes=VMEM_LIMIT
        ),
        cost_estimate=lasts(1),
        name="front",
    )(starts, hidden, edge, tok, cw, dtp, *shards)


def middle_kernel(
    u, rec, gate, st, pdx, sin, og, wo, prm,
    scan, dgate, sums, part_first, part_second,
):
    inner = gate.shape[1]
    pairs = inner // LANES
    d_gate = nn(og[...], wo[...])
    dgate[...] = d_gate
    act = silu(u[...])
    below = iota((CHUNK, CHUNK), 0) >= iota((CHUNK, CHUNK), 1)
    for i in range(SUB):
        rows = slice(i * CHUNK, (i + 1) * CHUNK)
        record = rec[rows, :]
        turned = record.T
        state = (st[i] + pdx[8 * i : 8 * i + 1, :] * sin[...]).astype(BF16)
        x = act[rows, :inner]
        input_b = act[rows, inner : inner + LANES].astype(BF16)
        input_c = act[rows, inner + LANES :].astype(BF16)
        scores = nt(input_c, input_b)
        barred = jnp.where(
            below & (record[:, SEG : SEG + 1] == turned[SEG : SEG + 1, :]), 0.0, NEGATIVE
        )
        entry = record[:, ENTRY : ENTRY + 1] * jnp.exp(record)
        outs = []
        for j in range(pairs):
            block = x[:, j * LANES : (j + 1) * LANES].astype(BF16)
            total = None
            for k, side in enumerate(halves(block)):
                h = 2 * j + k
                link = jnp.exp(record[:, h : h + 1] - turned[h : h + 1, :] + barred)
                weight = (scores * link * turned[8 + h : 9 + h, :]).astype(BF16)
                term = nn(weight, side)
                total = term if total is None else total + term
            outs.append(total)
        y = jnp.concatenate(outs, 1)
        y = y + nn(input_c, state) * spread(entry, pairs) + prm[0:1, :] * x
        scan[rows, :] = y
    gated = scan[...] * silu(gate[...])
    scaled = gated * prm[1:2, :]
    squares = jnp.sum(gated * gated, -1, keepdims=True)
    crosses = jnp.sum(scaled * d_gate, -1, keepdims=True)
    lane = iota((STEP, LANES), 1)
    both = jnp.where(lane == 0, squares, jnp.where(lane == 1, crosses, 0.0))
    sums[...] = both.T[0:8, :]
    part = nt(scaled.astype(BF16), wo[...]).astype(BF16)
    early = pl.program_id(0) < pl.num_programs(0) // 2

    @pl.when(early)
    def _():
        part_first[...] = part

    @pl.when(jnp.logical_not(early))
    def _():
        part_second[...] = part


def middle(u, rec, gate, st, pdx, sin, og, wo, prm, half):
    rows, inner = gate.shape
    width = og.shape[1]
    rows = rows // 2
    steps = rows // STEP
    first = half * steps

    def whole(a):
        return pl.BlockSpec(a.shape, lambda i: (0,) * a.ndim)

    def tall(cols):
        return pl.BlockSpec((STEP, cols), lambda i: (first + i, 0))

    def own(cols):
        return pl.BlockSpec((STEP, cols), lambda i: (i, 0))

    return pl.pallas_call(
        middle_kernel,
        grid=(steps,),
        in_specs=[
            tall(u.shape[1]),
            tall(LANES),
            tall(inner),
            pl.BlockSpec((SUB,) + st.shape[1:], lambda i: (first + i, 0, 0)),
            pl.BlockSpec((8 * SUB, inner), lambda i: (first + i, 0)),
            whole(sin),
            tall(width),
            whole(wo),
            whole(prm),
        ],
        out_specs=[
            own(inner),
            own(inner),
            pl.BlockSpec((8, STEP), lambda i: (0, i)),
            pl.BlockSpec((STEP, width), lambda i: (jnp.minimum(i, steps // 2 - 1), 0)),
            pl.BlockSpec((STEP, width), lambda i: (jnp.maximum(i - steps // 2, 0), 0)),
        ],
        out_shape=[
            jax.ShapeDtypeStruct((rows, inner), F32),
            jax.ShapeDtypeStruct((rows, inner), F32),
            jax.ShapeDtypeStruct((8, rows), F32),
            jax.ShapeDtypeStruct((rows // 2, width), BF16),
            jax.ShapeDtypeStruct((rows // 2, width), BF16),
        ],
        compiler_params=pltpu.CompilerParams(
            dimension_semantics=("arbitrary",), vmem_limit_bytes=VMEM_LIMIT
        ),
        cost_estimate=lasts(1),
        name="middle",
    )(u, rec, gate, st, pdx, sin, og, wo, prm)


def turn_kernel(
    inner_total, scan, gate, dgate, sums, upre_c, rec, prm, fin_before, decay_before,
    dscan, dgr, glow, adj, psx, fin, gain_grad, decay_end,
    state, decay,
):
    inner = gate.shape[1]
    pairs = inner // LANES
    at = pl.program_id(0)

    @pl.when(at == 0)
    def _():
        state[...] = fin_before[...]
        decay[...] = decay_before[...]
        gain_grad[...] = jnp.zeros_like(gain_grad)

    head = sums[...]
    column = jnp.concatenate([head, jnp.zeros((LANES - 8, STEP), F32)], 0).T
    inv = lax.rsqrt(column[:, 0:1] / inner_total + EPSILON)
    cube = inv * inv * inv * (column[:, 1:2] / inner_total)
    raw = gate[...]
    sig = jax.nn.sigmoid(raw)
    sil = raw * sig
    y = scan[...]
    gated = y * sil
    unit = gated * inv
    d_gate = dgate[...]
    gain = prm[1:2, :]
    glow[...] = (unit * gain).astype(BF16)
    gain_grad[...] += jnp.broadcast_to(jnp.sum(d_gate * unit, 0, keepdims=True), gain_grad.shape)
    d_gated = inv * gain * d_gate - gated * cube
    d_scan = d_gated * sil
    dscan[...] = d_scan
    dgr[...] = (d_gated * y * (sig * (1.0 + raw * (1.0 - sig)))).astype(BF16)
    input_c = silu(upre_c[...])
    for i in reversed(range(SUB)):
        rows = slice(i * CHUNK, (i + 1) * CHUNK)
        record = rec[rows, :]
        entry = record[:, ENTRY : ENTRY + 1] * jnp.exp(record)
        adj[i] = state[...]
        psx[8 * i : 8 * i + 8, :] = decay[...]
        passed = spread(entry[CHUNK - 1 :, :], pairs)
        fed = (d_scan[rows] * spread(entry, pairs)).astype(BF16)
        state[...] = passed * state[...] + nn(input_c[rows].T.astype(BF16), fed)
        decay[...] = decay[...] * passed
    fin[...] = state[...]
    decay_end[...] = decay[...]


def turn(scan, gate, dgate, sums, u, rec, prm, fin_before, decay_before, inner_total, half):
    rows, inner = scan.shape
    steps = rows // STEP
    chunks = rows // CHUNK
    first = half * steps
    state_size = LANES
    c_block = u.shape[1] // LANES - 1

    def whole(a):
        return pl.BlockSpec(a.shape, lambda i: (0,) * a.ndim)

    def tall(cols):
        return pl.BlockSpec((STEP, cols), lambda i: (first + steps - 1 - i, 0))

    def own(cols):
        return pl.BlockSpec((STEP, cols), lambda i: (steps - 1 - i, 0))

    return pl.pallas_call(
        functools.partial(turn_kernel, float(inner_total)),
        grid=(steps,),
        in_specs=[
            own(inner),
            tall(inner),
            own(inner),
            pl.BlockSpec((8, STEP), lambda i: (0, steps - 1 - i)),
            pl.BlockSpec((STEP, LANES), lambda i: (first + steps - 1 - i, c_block)),
            tall(LANES),
            whole(prm),
            whole(fin_before),
            whole(decay_before),
        ],
        out_specs=[
            own(inner),
            own(inner),
            own(inner),
            pl.BlockSpec((SUB, state_size, inner), lambda i: (steps - 1 - i, 0, 0)),
            pl.BlockSpec((8 * SUB, inner), lambda i: (steps - 1 - i, 0)),
            pl.BlockSpec((state_size, inner), lambda i: (0, 0)),
            pl.BlockSpec((8, inner), lambda i: (0, 0)),
            pl.BlockSpec((8, inner), lambda i: (0, 0)),
        ],
        out_shape=[
            jax.ShapeDtypeStruct((rows, inner), F32),
            jax.ShapeDtypeStruct((rows, inner), BF16),
            jax.ShapeDtypeStruct((rows, inner), BF16),
            jax.ShapeDtypeStruct((chunks, state_size, inner), F32),
            jax.ShapeDtypeStruct((8 * chunks, inner), F32),
            jax.ShapeDtypeStruct((state_size, inner), F32),
            jax.ShapeDtypeStruct((8, inner), F32),
            jax.ShapeDtypeStruct((8, inner), F32),
        ],
        scratch_shapes=[pltpu.VMEM((state_size, inner), F32), pltpu.VMEM((8, inner), F32)],
        compiler_params=pltpu.CompilerParams(
            dimension_semantics=("arbitrary",), vmem_limit_bytes=VMEM_LIMIT
        ),
        cost_estimate=lasts(1),
        name="turn",
    )(scan, gate, dgate, sums, u, rec, prm, fin_before, decay_before)


def back_kernel(
    u, rec, dscan, st, pdx, sin, adj, psx, ain, prm, dtp,
    dpre, dstep, skip_acc, head_acc,
):
    inner = dscan.shape[1]
    pairs = inner // LANES
    heads = 2 * pairs

    @pl.when(pl.program_id(0) == 0)
    def _():
        skip_acc[...] = jnp.zeros_like(skip_acc)
        head_acc[...] = jnp.zeros_like(head_acc)

    raw = u[...]
    sig = jax.nn.sigmoid(raw)
    act = raw * sig
    slope = sig * (1.0 + raw * (1.0 - sig))
    above = iota((CHUNK, CHUNK), 0) <= iota((CHUNK, CHUNK), 1)
    upper = above.astype(F32)
    lane = iota((CHUNK, LANES), 1)
    gather_heads = (iota((inner, LANES), 0) // (LANES // 2) == iota((inner, LANES), 1)).astype(BF16)
    nega = dtp[1:2, :]
    for i in range(SUB):
        rows = slice(i * CHUNK, (i + 1) * CHUNK)
        record = rec[rows, :]
        turned = record.T
        state = st[i] + pdx[8 * i : 8 * i + 1, :] * sin[...]
        state_low = state.astype(BF16)
        later = adj[i] + psx[8 * i : 8 * i + 1, :] * ain[...]
        later_low = later.astype(BF16)
        x = act[rows, :inner]
        b_wide = act[rows, inner : inner + LANES]
        c_wide = act[rows, inner + LANES :]
        input_b = b_wide.astype(BF16)
        input_c = c_wide.astype(BF16)
        dy = dscan[rows, :]
        scores = nt(input_b, input_c)
        barred = jnp.where(
            above & (record[:, SEG : SEG + 1] == turned[SEG : SEG + 1, :]), 0.0, NEGATIVE
        )
        step = pltpu.roll(record, LANES - 8, axis=1)
        z = pltpu.roll(record, LANES - RAW, axis=1)
        d_scores = jnp.zeros((CHUNK, CHUNK), F32)
        direct = jnp.zeros((CHUNK, LANES), F32)
        arrivals = []
        dxs = []
        for j in range(pairs):
            cols = slice(j * LANES, (j + 1) * LANES)
            x_sides = halves(x[:, cols].astype(BF16))
            dy_pair = dy[:, cols].astype(BF16)
            dy_sides = halves(dy_pair)
            total = None
            for k in range(2):
                h = 2 * j + k
                step_col = record[:, 8 + h : 9 + h]
                link = jnp.exp(turned[h : h + 1, :] - record[:, h : h + 1] + barred)
                d_link = nt(x_sides[k], dy_pair) * link
                d_scaled = d_link * step_col
                d_scores = d_scores + d_scaled
                flow = d_scaled * scores
                arrivals.append(jnp.sum(flow, 0, keepdims=True))
                given = jnp.sum(d_link * scores, 1, keepdims=True)
                direct = jnp.where(lane == h, given, direct)
                weight = (scores * link * step_col).astype(BF16)
                term = nn(weight, dy_sides[k])
                total = term if total is None else total + term
            dxs.append(total)
        dx = jnp.concatenate(dxs, 1)
        arrived = jnp.concatenate(arrivals + [jnp.zeros((CHUNK - heads, CHUNK), F32)], 0).T
        decay_in = record[:, ENTRY : ENTRY + 1] * jnp.exp(record)
        last = record[CHUNK - 1 :, :]
        tail_exp = record[:, TAIL : TAIL + 1] * jnp.exp(last - record)
        tail = tail_exp * step
        tail_wide = spread(jnp.where(lane < 8, tail, 0.0), pairs)
        fed_back = (dy * spread(decay_in, pairs)).astype(BF16)
        fed = (x * tail_wide).astype(BF16)
        from_state = nn(input_c, state_low)
        d_fed = nn(input_b, later_low)
        d_score_low = d_scores.astype(BF16)
        d_c = nt(fed_back, state_low) + nn(d_scores.T.astype(BF16), input_b)
        d_b = nt(fed, later_low) + nn(d_score_low, input_c)
        d_entry = nn((dy * from_state).astype(BF16), gather_heads)
        d_tail = nn((x * d_fed).astype(BF16), gather_heads)
        through = jnp.broadcast_to(jnp.sum(later * state, 0, keepdims=True), (16, inner))
        d_through = nn(through.astype(BF16), gather_heads)[0:1, :]
        dx = dx + d_fed * tail_wide + prm[0:1, :] * dy
        tail_flow = d_tail * tail
        d_cum = arrived - direct * step + d_entry * decay_in - tail_flow
        d_cum = jnp.where(lane < 8, d_cum, 0.0)
        d_last = jnp.sum(tail_flow, 0, keepdims=True) + decay_in[CHUNK - 1 :, :] * d_through
        d_rate = exact(upper, d_cum) + jnp.where(lane < 8, d_last, 0.0)
        d_step = direct + d_tail * tail_exp + nega * d_rate
        d_z = jnp.where(lane < 8, d_step * jax.nn.sigmoid(z), 0.0)
        dstep[rows, :] = d_z.astype(BF16)
        dpre[rows, :] = jnp.concatenate([dx, d_b, d_c], 1) * slope[rows]
        skip_acc[...] += jnp.broadcast_to(jnp.sum(dy * x, 0, keepdims=True), skip_acc.shape)
        head_acc[0:1, :] += jnp.sum(d_z, 0, keepdims=True)
        head_acc[1:2, :] += jnp.sum(
            jnp.where(lane < 8, d_rate * (nega * step), 0.0), 0, keepdims=True
        )


def back(u, rec, dscan, st, pdx, sin, adj, psx, ain, prm, dtp, after, group):
    rows, wide = u.shape
    inner = dscan.shape[1]
    steps = rows // STEP // GROUPS
    first = group * steps
    in_half = group % (GROUPS // 2) * steps

    def whole(a):
        return pl.BlockSpec(a.shape, lambda i: (0,) * a.ndim)

    def tall(cols):
        return pl.BlockSpec((STEP, cols), lambda i: (first + i, 0))

    def out_tall(cols):
        return pl.BlockSpec((STEP, cols), lambda i: (i, 0))

    def states(at):
        return pl.BlockSpec((SUB,) + st.shape[1:], lambda i: (at + i, 0, 0))

    def decays(at):
        return pl.BlockSpec((8 * SUB, inner), lambda i: (at + i, 0))

    return pl.pallas_call(
        ordered(back_kernel, 11, len(after)),
        grid=(steps,),
        in_specs=[
            tall(wide),
            tall(LANES),
            pl.BlockSpec((STEP, inner), lambda i: (in_half + i, 0)),
            states(first),
            decays(first),
            whole(sin),
            states(in_half),
            decays(in_half),
            whole(ain),
            whole(prm),
            whole(dtp),
        ]
        + [ANYWHERE] * len(after),
        out_specs=[
            out_tall(wide),
            out_tall(LANES),
            pl.BlockSpec((8, inner), lambda i: (0, 0)),
            pl.BlockSpec((8, LANES), lambda i: (0, 0)),
        ],
        out_shape=[
            jax.ShapeDtypeStruct((steps * STEP, wide), F32),
            jax.ShapeDtypeStruct((steps * STEP, LANES), BF16),
            jax.ShapeDtypeStruct((8, inner), F32),
            jax.ShapeDtypeStruct((8, LANES), F32),
        ],
        compiler_params=pltpu.CompilerParams(
            dimension_semantics=("arbitrary",), vmem_limit_bytes=VMEM_LIMIT
        ),
        cost_estimate=lasts(1),
        name="back",
    )(u, rec, dscan, st, pdx, sin, adj, psx, ain, prm, dtp, *after)


def rear_kernel(
    dpre, rec, pre, dgr, dstep, follow, hid, w, cw, filled,
    dproj, dnorm, conv_acc, gain_acc,
    buf, mbuf,
):
    wide = dpre.shape[1]
    inner = dgr.shape[1]

    @pl.when(pl.program_id(0) == 0)
    def _():
        buf[STEP : STEP + 8, :] = follow[:, :wide]
        mbuf[STEP : STEP + 8, :] = follow[:, wide:]
        conv_acc[...] = jnp.zeros_like(conv_acc)
        gain_acc[...] = jnp.zeros_like(gain_acc)

    @pl.when(pl.program_id(0) > 0)
    def _():
        buf[STEP : STEP + 8, :] = buf[0:8, :]
        mbuf[STEP : STEP + 8, :] = mbuf[0:8, :]

    grad = dpre[...]
    buf[0:STEP, :] = grad
    mbuf[0:STEP, :] = rec[...]
    value = pre[...]
    total = cw[3:4, :] * grad
    conv_acc[3:4, :] += jnp.sum(value * grad, 0, keepdims=True)
    conv_acc[4:5, :] += jnp.sum(grad, 0, keepdims=True)
    for shift in (1, 2, 3):
        mark = mbuf[shift : shift + STEP, :][:, M1 + shift - 1 : M1 + shift]
        moved = buf[shift : shift + STEP, :] * mark
        total = total + cw[3 - shift : 4 - shift, :] * moved
        conv_acc[3 - shift : 4 - shift, :] += jnp.sum(value * moved, 0, keepdims=True)
    dproj[:, :inner] = dgr[...]
    dproj[:, inner : inner + wide] = total.astype(BF16)
    dproj[:, inner + wide :] = dstep[...]
    grad_in = nt(dproj[...], w[...])
    dnorm[...] = grad_in.astype(BF16)
    unit = rms_unit(hid[...].astype(F32))
    gain_acc[...] += jnp.broadcast_to(jnp.sum(grad_in * unit, 0, keepdims=True), gain_acc.shape)


def rear(dpre, rec, pre, dgr, dstep, follow, hid, w, cw, filled, after, group):
    rows, wide = dpre.shape
    in_half = group % (GROUPS // 2) * (rows // STEP)
    steps = rows // STEP
    inner = dgr.shape[1]
    width, packed = w.shape
    first = group * steps

    def whole(a):
        return pl.BlockSpec(a.shape, lambda i: (0,) * a.ndim)

    def tall(cols):
        return pl.BlockSpec((STEP, cols), lambda i: (first + steps - 1 - i, 0))

    def own(cols):
        return pl.BlockSpec((STEP, cols), lambda i: (steps - 1 - i, 0))

    return pl.pallas_call(
        ordered(rear_kernel, 10, len(after)),
        grid=(steps,),
        in_specs=[
            own(wide),
            tall(LANES),
            tall(wide),
            pl.BlockSpec((STEP, inner), lambda i: (in_half + steps - 1 - i, 0)),
            own(LANES),
            whole(follow),
            tall(width),
            whole(w),
            whole(cw),
            ANYWHERE,
        ]
        + [ANYWHERE] * len(after),
        out_specs=[
            tall(packed),
            own(width),
            pl.BlockSpec((8, wide), lambda i: (0, 0)),
            pl.BlockSpec((8, width), lambda i: (0, 0)),
        ],
        out_shape=[
            jax.ShapeDtypeStruct((pre.shape[0], packed), BF16),
            jax.ShapeDtypeStruct((rows, width), BF16),
            jax.ShapeDtypeStruct((8, wide), F32),
            jax.ShapeDtypeStruct((8, width), F32),
        ],
        scratch_shapes=[
            pltpu.VMEM((STEP + 8, wide), F32),
            pltpu.VMEM((STEP + 8, LANES), F32),
        ],
        compiler_params=pltpu.CompilerParams(
            dimension_semantics=("arbitrary",), vmem_limit_bytes=VMEM_LIMIT
        ),
        cost_estimate=lasts(1),
        input_output_aliases={9: 0} if group else {},
        name="rear",
    )(dpre, rec, pre, dgr, dstep, follow, hid, w, cw, filled, *after)


def settle_kernel(inner_total, hid, sums, given, held, outer, filled, out):
    column = jnp.concatenate([sums[...], jnp.zeros((LANES - 8, STEP), F32)], 0).T
    inv = lax.rsqrt(column[:, 0:1] / inner_total + EPSILON)
    total = jnp.where(outer[0:1, 0:1] > 0.0, given[...].astype(F32), held[...].astype(F32))
    out[...] = (hid[...].astype(F32) + inv * total).astype(BF16)


def finish_kernel(hid, cot, gain, given, held, outer, filled, out):
    x = hid[...].astype(F32)
    inv = lax.rsqrt(jnp.mean(x * x, -1, keepdims=True) + EPSILON)
    total = jnp.where(outer[0:1, 0:1] > 0.0, given[...].astype(F32), held[...].astype(F32))
    scaled = total * gain[0:1, :]
    cross = jnp.mean(scaled * x, -1, keepdims=True)
    out[...] = cot[...].astype(F32) + inv * scaled - x * (inv * inv * inv * cross)


def by_group(kernel, out_like, dtype, group, fresh, operands, filled, after, name):
    rows, width = out_like.shape
    steps = rows // GROUPS // STEP
    first = group * steps
    in_half = group % (GROUPS // 2) * steps
    specs = {
        "all": lambda a: pl.BlockSpec((STEP, a.shape[1]), lambda i: (first + i, 0)),
        "group": lambda a: pl.BlockSpec((STEP, a.shape[1]), lambda i: (i, 0)),
        "half": lambda a: pl.BlockSpec((8, STEP), lambda i: (0, in_half + i)),
        "whole": lambda a: pl.BlockSpec(a.shape, lambda i: (0, 0)),
    }
    count = len(operands) + 1
    return pl.pallas_call(
        ordered(kernel, count, len(after)),
        grid=(steps,),
        in_specs=[specs[kind](a) for a, kind in operands] + [ANYWHERE] * (1 + len(after)),
        out_specs=pl.BlockSpec((STEP, width), lambda i: (first + i, 0)),
        out_shape=jax.ShapeDtypeStruct((rows, width), dtype),
        input_output_aliases={} if fresh else {count - 1: 0},
        compiler_params=pltpu.CompilerParams(
            dimension_semantics=("arbitrary",), vmem_limit_bytes=VMEM_LIMIT
        ),
        cost_estimate=lasts(1),
        name=name,
    )(*[a for a, _ in operands], filled, *after)


def passed_along(value, axis, steps):
    count = lax.axis_size(axis)
    leading, last = (max(0, -steps), min(count, count - steps))
    return lax.ppermute(value, axis, [(source, source + steps) for source in range(leading, last)])


def chained(own, decay, axis, steps):
    entering = jnp.zeros_like(own)
    for turn_at in range(lax.axis_size(axis) - 1):
        leaving = own if turn_at == 0 else own + decay * entering
        entering = passed_along(leaving, axis, steps)
    return entering


def butterfly_sum(value, axis):
    bit = 1
    while bit < lax.axis_size(axis):
        pairs = [(i, i ^ bit) for i in range(lax.axis_size(axis))]
        value = value + lax.ppermute(value, axis, pairs)
        bit *= 2
    return value


def join_kernel(a, b, out):
    out[...] = (a[...].astype(F32) + b[...].astype(F32)).astype(out.dtype)


def join(a, b, after):
    rows, width = a.shape
    spec = pl.BlockSpec((STEP, width), lambda i: (i, 0))
    return pl.pallas_call(
        ordered(join_kernel, 2, len(after)),
        grid=(rows // STEP,),
        in_specs=[spec, spec] + [ANYWHERE] * len(after),
        out_specs=spec,
        out_shape=jax.ShapeDtypeStruct(a.shape, a.dtype),
        compiler_params=pltpu.CompilerParams(
            dimension_semantics=("arbitrary",), vmem_limit_bytes=VMEM_LIMIT
        ),
        cost_estimate=lasts(1),
        name="join",
    )(a, b, *after)


class LineSum:
    def __init__(self, value, axis):
        self.axis = axis
        self.short = lax.axis_size(axis) != 4
        if self.short:
            self.near = self.across = self.given = lax.psum(value, axis)
        else:
            self.own = value
            self.come = lax.ppermute(value, axis, [(0, 1), (3, 2)])

    def inwards(self, after=()):
        if not self.short:
            self.near = join(self.own, self.come, after)
            self.come = lax.ppermute(self.near, self.axis, [(1, 2), (2, 1)])

    def middle(self, after=()):
        if not self.short:
            self.across = join(self.near, self.come, after)
            self.given = lax.ppermute(self.across, self.axis, [(1, 0), (2, 3)])


def gathered_shards(own):
    rows = own.shape[0]
    if lax.axis_size("fsdp") != 4 or lax.axis_size("ctx") != 2:
        return [lax.all_gather(own, ("fsdp", "ctx"), axis=0, tiled=True)], [0]

    def swapped(value, axis, bit):
        count = lax.axis_size(axis)
        return lax.ppermute(value, axis, [(i, i ^ bit) for i in range(count)])

    half = rows // 2
    by_one, by_two = swapped(own, "fsdp", 1), swapped(own, "fsdp", 2)
    upper = swapped(by_two[:half], "fsdp", 1)
    under = swapped(by_one[half:], "fsdp", 2)
    mine = [own, by_one, by_two, upper, under]
    place = lax.axis_index("fsdp")
    core = lax.axis_index("ctx")
    shards, starts = [], []
    for other in (0, 1):
        for value, bits, offset in zip(mine, (0, 1, 2, 3, 3), (0, 0, 0, 0, half)):
            shards.append(swapped(value, "ctx", 1) if other else value)
            starts.append(((place ^ bits) * 2 + (core ^ other)) * rows + offset)
    return shards, starts


def token_marks(segment, before):
    rows = segment.shape[0]
    joined = jnp.concatenate([before, segment])
    marks = [joined[3 - j : 3 - j + rows] == segment for j in (1, 2, 3)]
    blocks = segment.reshape(-1, CHUNK)
    previous = jnp.concatenate([before[2:], blocks[:-1, -1]])
    marks.append((blocks == previous[:, None]).reshape(-1))
    marks.append((blocks == blocks[:, -1:]).reshape(-1))
    marks.append(segment)
    table = jnp.stack([mark.astype(F32) for mark in marks], 1)
    return jnp.pad(table, ((0, 0), (M1, LANES - M1 - len(marks))))


def body(
    hidden, segments, out_grad, norm_gain, w_zx, w_dt, w_bc, conv_x_w, conv_x_b,
    conv_bc_w, conv_bc_b, dt_bias, a_log, skip_d, out_gain, w_out,
):
    _, rows, width = hidden.shape
    inner = w_zx.shape[2]
    heads = w_dt.shape[1]
    head_size = inner // heads
    state_size = w_bc.shape[2]
    wide = inner + 2 * state_size
    taps = conv_x_w.shape[0]
    owned = w_zx.shape[0]
    shards = ("fsdp", "ctx")
    hid = hidden[0]
    cot = out_grad[0]
    segment = segments[0]

    packed = jnp.concatenate(
        [
            w_zx.reshape(owned, 2 * inner),
            w_bc.reshape(owned, 2 * state_size),
            w_dt, w_dt, w_dt, w_dt,
            norm_gain[:, None],
            jnp.zeros((owned, LANES - 4 * heads - 1), BF16),
        ],
        1,
    )
    w_shards, w_starts = gathered_shards(packed)
    w_starts = jnp.stack([jnp.asarray(start, jnp.int32) for start in w_starts])
    wo = lax.all_gather(w_out.T, shards, axis=0, tiled=True)
    gain_at = 2 * inner + 2 * state_size + 4 * heads

    edge, edge_segment = passed_along((hid[rows - EDGE :], segment[rows - 3 :]), "ctx", 1)
    tok = token_marks(segment, edge_segment)
    conv_rows = jnp.concatenate(
        [
            jnp.concatenate([conv_x_w, conv_bc_w.reshape(taps, -1)], 1),
            jnp.concatenate([conv_x_b, conv_bc_b.reshape(-1)])[None],
            jnp.zeros((8 - taps - 1, wide), F32),
        ],
        0,
    )
    spare = jnp.zeros((LANES - 4 * heads,), F32)
    rate = -jnp.exp(a_log)
    dtp = jnp.concatenate(
        [
            jnp.concatenate([dt_bias] * 4 + [spare])[None],
            jnp.concatenate([rate] * 4 + [spare])[None],
            jnp.zeros((6, LANES), F32),
        ],
        0,
    )
    prm = jnp.concatenate(
        [jnp.repeat(skip_d, head_size)[None], out_gain[None], jnp.zeros((6, inner), F32)], 0
    )

    normed, gate, pre, u, rec, st, pdx, state_end, decay_end, w_in, gain = front(
        hid, edge, tok, w_shards, w_starts, 4 * heads, conv_rows, dtp, inner, wide
    )
    sin = chained(state_end, decay_end[:1], "ctx", 1)
    inner_total = inner * lax.axis_size("tp")
    halves_out = [None, None]
    parts = [None] * GROUPS
    for half in (1, 0):
        scan, dgate, sums, parts[2 * half], parts[2 * half + 1] = middle(
            u, rec, gate, st, pdx, sin, cot, wo, prm, half
        )
        halves_out[half] = (scan, dgate, butterfly_sum(sums, "tp"))
    me = lax.axis_index("tp")
    outer = jnp.full((8, LANES), (me == 0) | (me == lax.axis_size("tp") - 1), F32)
    out_sums = [LineSum(parts[group], "tp") for group in range(GROUPS)]
    turned = [None, None]
    adj_start, decay_start = jnp.zeros_like(state_end), jnp.ones_like(decay_end)
    out_gain_acc = 0.0
    for half in (1, 0):
        scan, dgate, sums = halves_out[half]
        *turned[half], adj_start, gain_part, decay_start = turn(
            scan, gate, dgate, sums, u, rec, prm, adj_start, decay_start, inner_total, half
        )
        out_gain_acc = out_gain_acc + gain_part
    ain = chained(adj_start, decay_end[:1], "ctx", -1)

    group_rows = rows // GROUPS
    backs = [None] * GROUPS
    rears = [None] * GROUPS
    d_normed = [None] * GROUPS
    follows = [None] * GROUPS
    dproj = rec[:8]

    def run_back(group, after):
        dscan, _, _, adj, psx = turned[group // (GROUPS // 2)]
        backs[group] = back(u, rec, dscan, st, pdx, sin, adj, psx, ain, prm, dtp, after, group)
        start = jnp.concatenate(
            [backs[group][0][:8], rec[group * group_rows : group * group_rows + 8]], 1
        )
        if group == 0:
            follows[GROUPS - 1] = passed_along(start, "ctx", -1)
        else:
            follows[group - 1] = start

    def run_rear(group, filled, after):
        dgr = turned[group // (GROUPS // 2)][1]
        rears[group] = rear(
            backs[group][0], rec, pre, dgr, backs[group][1], follows[group], hid, w_in,
            conv_rows, filled, after, group,
        )
        d_normed[group] = LineSum(rears[group][1], "tp")
        return rears[group][0]

    def settle(group, filled, after=()):
        total = out_sums[group]
        return by_group(
            functools.partial(settle_kernel, float(inner_total)), hid, BF16, group, filled is None,
            [
                (hid, "all"),
                (halves_out[group // (GROUPS // 2)][2], "half"),
                (total.given, "group"),
                (total.across, "group"),
                (outer, "whole"),
            ],
            outer if filled is None else filled, after, "settle",
        )

    def finish(group, filled, after):
        total = d_normed[group]
        return by_group(
            finish_kernel, hid, F32, group, filled is None,
            [
                (hid, "all"),
                (cot, "all"),
                (gain, "whole"),
                (total.given, "group"),
                (total.across, "group"),
                (outer, "whole"),
            ],
            outer if filled is None else filled, after, "finish",
        )

    sum_a, sum_b, sum_c, sum_d = (out_sums[group] for group in (2, 3, 0, 1))
    sum_a.inwards((decay_start,))
    run_back(0, (sum_a.near,))
    run_back(1, (backs[0][3],))
    sum_b.inwards((backs[1][3],))
    sum_a.middle((backs[1][3],))
    dproj = run_rear(0, dproj, (sum_b.near, sum_a.across))
    run_back(2, (rears[0][3],))
    sum_c.inwards((backs[2][3],))
    sum_b.middle((backs[2][3],))
    dproj = run_rear(1, dproj, (sum_c.near, sum_b.across))
    run_back(3, (rears[1][3],))
    sum_d.inwards((backs[3][3],))
    sum_c.middle((backs[3][3],))
    block_out = settle(2, None, (backs[3][3],))
    dproj = run_rear(2, dproj, (sum_d.near, sum_c.across, block_out))
    dproj = run_rear(3, dproj, (rears[2][3],))
    d_normed[0].inwards((rears[3][3],))
    sum_d.middle((rears[3][3],))
    block_out = settle(3, block_out, (rears[3][3],))

    glow = jnp.concatenate([turned[0][2], turned[1][2]], 0)
    conv_acc = sum(r[2] for r in rears)
    gain_acc = sum(r[3][0] for r in rears)
    skip_acc = sum(b[2][0] for b in backs)
    head_acc = sum(b[3] for b in backs)

    contract_rows = (((0,), (0,)), ((), ()))
    w_grad = lax.dot_general(normed, dproj, contract_rows, preferred_element_type=F32)
    wo_grad = lax.dot_general(cot, glow, contract_rows, preferred_element_type=F32)
    for group in range(GROUPS):
        if group:
            d_normed[group].inwards((w_grad[:8, :LANES],))
        d_normed[group].middle((w_grad[:8, :LANES],))
    w_grad = w_grad.at[:, gain_at].set(gain_acc)
    w_owned = lax.psum_scatter(w_grad, shards, scatter_dimension=0, tiled=True)
    wo_owned = lax.psum_scatter(wo_grad, shards, scatter_dimension=0, tiled=True)

    small = jnp.concatenate(
        [
            conv_acc[: taps + 1].reshape(-1),
            out_gain_acc[0],
            skip_acc,
            head_acc[:2].reshape(-1),
        ]
    )
    small = butterfly_sum(butterfly_sum(small, "ctx"), "fsdp")
    conv_sum = small[: (taps + 1) * wide].reshape(taps + 1, wide)
    rest = small[(taps + 1) * wide :]
    shared = jnp.concatenate(
        [
            w_owned[:, 2 * inner : 2 * inner + 2 * state_size].reshape(-1),
            w_owned[:, gain_at],
            conv_sum[:, inner:].reshape(-1),
        ]
    )
    shared = butterfly_sum(shared, "tp")
    bc_size = owned * 2 * state_size
    bc_owned = shared[:bc_size].reshape(owned, 2, state_size)
    gain_owned = shared[bc_size : bc_size + owned]
    conv_bc = shared[bc_size + owned :].reshape(taps + 1, 2, state_size)

    block_out = settle(0, block_out)
    block_out = settle(1, block_out)
    hidden_grad = None
    for group in range(GROUPS):
        hidden_grad = finish(group, hidden_grad, (block_out,))

    return (
        block_out[None],
        hidden_grad[None],
        gain_owned,
        w_owned[:, : 2 * inner].reshape(owned, 2, inner),
        w_owned[:, 2 * inner + 2 * state_size : 2 * inner + 2 * state_size + heads],
        bc_owned,
        conv_sum[:taps, :inner],
        conv_sum[taps, :inner],
        conv_bc[:taps],
        conv_bc[taps],
        rest[2 * inner : 2 * inner + heads],
        rest[2 * inner + LANES : 2 * inner + LANES + heads],
        jnp.sum(rest[inner : 2 * inner].reshape(heads, head_size), 1),
        rest[:inner],
        wo_owned.T,
    )


def solution(mesh):
    placed = (
        P("fsdp", "ctx", None),
        P("fsdp", "ctx"),
        P("fsdp", "ctx", None),
        P(("fsdp", "ctx")),
        P(("fsdp", "ctx"), None, "tp"),
        P(("fsdp", "ctx"), "tp"),
        P(("fsdp", "ctx"), None, None),
        P(None, "tp"),
        P("tp"),
        P(),
        P(),
        P("tp"),
        P("tp"),
        P("tp"),
        P("tp"),
        P("tp", ("fsdp", "ctx")),
    )
    return jax.shard_map(
        body,
        mesh=mesh,
        in_specs=placed,
        out_specs=(
            P("fsdp", "ctx", None),
            P("fsdp", "ctx", None),
            P(("fsdp", "ctx")),
            P(("fsdp", "ctx"), None, "tp"),
            P(("fsdp", "ctx"), "tp"),
            P(("fsdp", "ctx"), None, None),
            P(None, "tp"),
            P("tp"),
            P(),
            P(),
            P("tp"),
            P("tp"),
            P("tp"),
            P("tp"),
            P("tp", ("fsdp", "ctx")),
        ),
        check_vma=False,
    )
```

```python
import functools

import jax
import jax.numpy as jnp
from jax import lax
from jax.experimental import pallas as pl
from jax.experimental.pallas import tpu as pltpu
from jax.sharding import PartitionSpec as P

CHUNK = 128
STEP = 256
SUB = STEP // CHUNK
LANES = 128
EDGE = 16
GROUPS = 4
EPSILON = 1e-05
EXACT = lax.Precision.HIGHEST
F32 = jnp.float32
BF16 = jnp.bfloat16
NEGATIVE = -1e30
M1, M2, M3, ENTRY, TAIL, SEG, RAW = 16, 17, 18, 19, 20, 21, 24
VMEM_LIMIT = 56 * 1024 * 1024


def nn(a, b):
    return lax.dot_general(a, b, (((1,), (0,)), ((), ())), preferred_element_type=F32)


def nt(a, b):
    return lax.dot_general(a, b, (((1,), (1,)), ((), ())), preferred_element_type=F32)


def tn(a, b):
    return nn(a.T, b)


def exact(a, b):
    return lax.dot_general(
        a, b, (((1,), (0,)), ((), ())), precision=EXACT, preferred_element_type=F32
    )


def lasts(microseconds):
    return pl.CostEstimate(
        flops=0, bytes_accessed=int(microseconds * 3.69e6), transcendentals=0
    )


ANYWHERE = pl.BlockSpec(memory_space=pl.ANY)


def ordered(kernel, inputs, after):
    def run(*refs):
        kernel(*refs[:inputs], *refs[inputs + after :])

    return run


def iota(shape, dim):
    return lax.broadcasted_iota(jnp.int32, shape, dim)


def spread(per_head, pairs):
    rows = per_head.shape[0]
    low = iota((rows, LANES), 1) < LANES // 2
    parts = []
    for j in range(pairs):
        left = jnp.broadcast_to(per_head[:, 2 * j : 2 * j + 1], (rows, LANES))
        right = jnp.broadcast_to(per_head[:, 2 * j + 1 : 2 * j + 2], (rows, LANES))
        parts.append(jnp.where(low, left, right))
    return jnp.concatenate(parts, 1)


def halves(block):
    low = iota(block.shape, 1) < LANES // 2
    zero = jnp.zeros_like(block)
    return jnp.where(low, block, zero), jnp.where(low, zero, block)


def silu(v):
    return v * jax.nn.sigmoid(v)


def rms_unit(x):
    return x * lax.rsqrt(jnp.mean(x * x, -1, keepdims=True) + EPSILON)


def front_kernel(
    gain_lane, starts, hid, edge, tok, cw, dtp, *refs
):
    (normed, gate, pre_out, u_out, rec, st, pdx, fin, pdfin, w, gain_out,
     buf, state, decay) = refs[-14:]
    shards = refs[:-14]
    inner = gate.shape[1]
    wide = pre_out.shape[1]
    pairs = inner // LANES
    at = pl.program_id(0)

    @pl.when(at == 0)
    def _():
        for k, shard in enumerate(shards):
            size = shard.shape[0]
            w[pl.ds(pl.multiple_of(starts[k], 16), size), :] = shard[...]
        for k in range(w.shape[0] // LANES):
            tile = w[k * LANES : (k + 1) * LANES, inner + wide :].astype(F32).T
            gain_out[:, k * LANES : (k + 1) * LANES] = jnp.broadcast_to(
                tile[gain_lane : gain_lane + 1, :], (8, LANES)
            )
        edge_low = (rms_unit(edge[...].astype(F32)) * gain_out[0:1, :]).astype(BF16)
        edge_pre = nn(edge_low, w[:, inner : inner + wide])
        buf[0:8, :] = edge_pre[EDGE - 8 :, :]
        state[...] = jnp.zeros_like(state)
        decay[...] = jnp.ones_like(decay)

    @pl.when(at > 0)
    def _():
        buf[0:8, :] = buf[STEP : STEP + 8, :]

    low = (rms_unit(hid[...].astype(F32)) * gain_out[0:1, :]).astype(BF16)
    normed[...] = low
    gate[...] = nn(low, w[:, :inner])
    pre = nn(low, w[:, inner : inner + wide])
    pre_out[...] = pre
    buf[8 : 8 + STEP, :] = pre
    raw_all = nn(low, w[:, inner + wide :]) + dtp[0:1, :]
    marks = tok[...]
    u = cw[3:4, :] * pre + cw[4:5, :]
    u = u + cw[2:3, :] * (buf[7 : 7 + STEP, :] * marks[:, M1 : M1 + 1])
    u = u + cw[1:2, :] * (buf[6 : 6 + STEP, :] * marks[:, M2 : M2 + 1])
    u = u + cw[0:1, :] * (buf[5 : 5 + STEP, :] * marks[:, M3 : M3 + 1])
    u_out[...] = u
    act = silu(u)
    step_all = jax.nn.softplus(raw_all)
    lane = iota((CHUNK, LANES), 1)
    lower = (iota((CHUNK, CHUNK), 0) >= iota((CHUNK, CHUNK), 1)).astype(F32)
    for i in range(SUB):
        rows = slice(i * CHUNK, (i + 1) * CHUNK)
        step = step_all[rows]
        cum = exact(lower, step * dtp[1:2, :])
        mark = marks[rows]
        rec[rows, :] = jnp.where(
            lane < 8, cum, jnp.where(lane < 16, step, jnp.where(lane < 24, mark, raw_all[rows]))
        )
        last = cum[CHUNK - 1 :, :]
        tail = mark[:, TAIL : TAIL + 1] * jnp.exp(last - cum) * step
        fed = (act[rows, :inner] * spread(tail, pairs)).astype(BF16)
        st[i] = state[...]
        pdx[8 * i : 8 * i + 8, :] = decay[...]
        passed = spread(mark[CHUNK - 1 :, ENTRY : ENTRY + 1] * jnp.exp(last), pairs)
        input_b = act[rows, inner : inner + LANES].T.astype(BF16)
        state[...] = passed * state[...] + nn(input_b, fed)
        decay[...] = decay[...] * passed
    fin[...] = state[...]
    pdfin[...] = decay[...]


def front(hidden, edge, tok, shards, starts, gain_lane, cw, dtp, inner, wide):
    rows, width = hidden.shape
    packed = shards[0].shape[1]
    steps = rows // STEP
    state_size = LANES

    def whole(a):
        return pl.BlockSpec(a.shape, lambda i: (0,) * a.ndim)

    def tall(cols):
        return pl.BlockSpec((STEP, cols), lambda i: (i, 0))

    chunks = rows // CHUNK
    return pl.pallas_call(
        functools.partial(front_kernel, gain_lane),
        grid=(steps,),
        in_specs=[
            pl.BlockSpec(memory_space=pltpu.SMEM),
            tall(width),
            whole(edge),
            tall(LANES),
            whole(cw),
            whole(dtp),
        ]
        + [whole(shard) for shard in shards],
        out_specs=[
            tall(width),
            tall(inner),
            tall(wide),
            tall(wide),
            tall(LANES),
            pl.BlockSpec((SUB, state_size, inner), lambda i: (i, 0, 0)),
            pl.BlockSpec((8 * SUB, inner), lambda i: (i, 0)),
            pl.BlockSpec((state_size, inner), lambda i: (0, 0)),
            pl.BlockSpec((8, inner), lambda i: (0, 0)),
            pl.BlockSpec((width, packed), lambda i: (0, 0)),
            pl.BlockSpec((8, width), lambda i: (0, 0)),
        ],
        out_shape=[
            jax.ShapeDtypeStruct((rows, width), BF16),
            jax.ShapeDtypeStruct((rows, inner), F32),
            jax.ShapeDtypeStruct((rows, wide), F32),
            jax.ShapeDtypeStruct((rows, wide), F32),
            jax.ShapeDtypeStruct((rows, LANES), F32),
            jax.ShapeDtypeStruct((chunks, state_size, inner), F32),
            jax.ShapeDtypeStruct((8 * chunks, inner), F32),
            jax.ShapeDtypeStruct((state_size, inner), F32),
            jax.ShapeDtypeStruct((8, inner), F32),
            jax.ShapeDtypeStruct((width, packed), BF16),
            jax.ShapeDtypeStruct((8, width), F32),
        ],
        scratch_shapes=[
            pltpu.VMEM((STEP + 8, wide), F32),
            pltpu.VMEM((state_size, inner), F32),
            pltpu.VMEM((8, inner), F32),
        ],
        compiler_params=pltpu.CompilerParams(
            dimension_semantics=("arbitrary",), vmem_limit_bytes=VMEM_LIMIT
        ),
        cost_estimate=lasts(0.01),
        name="front",
    )(starts, hidden, edge, tok, cw, dtp, *shards)


def middle_kernel(
    u, rec, gate, st, pdx, sin, og, wo, prm,
    scan, dgate, sums, *parts,
):
    inner = gate.shape[1]
    pairs = inner // LANES
    d_gate = nn(og[...], wo[...])
    dgate[...] = d_gate
    act = silu(u[...])
    below = iota((CHUNK, CHUNK), 0) >= iota((CHUNK, CHUNK), 1)
    for i in range(SUB):
        rows = slice(i * CHUNK, (i + 1) * CHUNK)
        record = rec[rows, :]
        turned = record.T
        state = (st[i] + pdx[8 * i : 8 * i + 1, :] * sin[...]).astype(BF16)
        x = act[rows, :inner]
        input_b = act[rows, inner : inner + LANES].astype(BF16)
        input_c = act[rows, inner + LANES :].astype(BF16)
        scores = nt(input_c, input_b)
        barred = jnp.where(
            below & (record[:, SEG : SEG + 1] == turned[SEG : SEG + 1, :]), 0.0, NEGATIVE
        )
        entry = record[:, ENTRY : ENTRY + 1] * jnp.exp(record)
        outs = []
        for j in range(pairs):
            block = x[:, j * LANES : (j + 1) * LANES].astype(BF16)
            total = None
            for k, side in enumerate(halves(block)):
                h = 2 * j + k
                link = jnp.exp(record[:, h : h + 1] - turned[h : h + 1, :] + barred)
                weight = (scores * link * turned[8 + h : 9 + h, :]).astype(BF16)
                term = nn(weight, side)
                total = term if total is None else total + term
            outs.append(total)
        y = jnp.concatenate(outs, 1)
        y = y + nn(input_c, state) * spread(entry, pairs) + prm[0:1, :] * x
        scan[rows, :] = y
    gated = scan[...] * silu(gate[...])
    scaled = gated * prm[1:2, :]
    squares = jnp.sum(gated * gated, -1, keepdims=True)
    crosses = jnp.sum(scaled * d_gate, -1, keepdims=True)
    lane = iota((STEP, LANES), 1)
    both = jnp.where(lane == 0, squares, jnp.where(lane == 1, crosses, 0.0))
    sums[...] = both.T[0:8, :]
    for part in parts:

        @pl.when(pl.program_id(0) < pl.num_programs(0) // 2)
        def _():
            part[...] = nt(scaled.astype(BF16), wo[...]).astype(BF16)


def middle(u, rec, gate, st, pdx, sin, og, wo, prm, half, with_part):
    rows, inner = gate.shape
    width = og.shape[1]
    rows = rows // 2
    steps = rows // STEP
    first = half * steps

    def whole(a):
        return pl.BlockSpec(a.shape, lambda i: (0,) * a.ndim)

    def tall(cols):
        return pl.BlockSpec((STEP, cols), lambda i: (first + i, 0))

    def own(cols):
        return pl.BlockSpec((STEP, cols), lambda i: (i, 0))

    return pl.pallas_call(
        middle_kernel,
        grid=(steps,),
        in_specs=[
            tall(u.shape[1]),
            tall(LANES),
            tall(inner),
            pl.BlockSpec((SUB,) + st.shape[1:], lambda i: (first + i, 0, 0)),
            pl.BlockSpec((8 * SUB, inner), lambda i: (first + i, 0)),
            whole(sin),
            tall(width),
            whole(wo),
            whole(prm),
        ],
        out_specs=[
            own(inner),
            own(inner),
            pl.BlockSpec((8, STEP), lambda i: (0, i)),
        ]
        + [pl.BlockSpec((STEP, width), lambda i: (jnp.minimum(i, steps // 2 - 1), 0))] * with_part,
        out_shape=[
            jax.ShapeDtypeStruct((rows, inner), F32),
            jax.ShapeDtypeStruct((rows, inner), F32),
            jax.ShapeDtypeStruct((8, rows), F32),
        ]
        + [jax.ShapeDtypeStruct((rows // 2, width), BF16)] * with_part,
        compiler_params=pltpu.CompilerParams(
            dimension_semantics=("arbitrary",), vmem_limit_bytes=VMEM_LIMIT
        ),
        cost_estimate=lasts(0.01),
        name="middle",
    )(u, rec, gate, st, pdx, sin, og, wo, prm)


def turn_kernel(
    inner_total, scan, gate, dgate, sums, upre_c, rec, prm, fin_before, decay_before, wo,
    dscan, dgr, glow, adj, psx, fin, gain_grad, decay_end, *rest,
):
    state, decay = rest[-2:]
    inner = gate.shape[1]
    pairs = inner // LANES
    at = pl.program_id(0)

    @pl.when(at == 0)
    def _():
        state[...] = fin_before[...]
        decay[...] = decay_before[...]
        gain_grad[...] = jnp.zeros_like(gain_grad)

    head = sums[...]
    column = jnp.concatenate([head, jnp.zeros((LANES - 8, STEP), F32)], 0).T
    inv = lax.rsqrt(column[:, 0:1] / inner_total + EPSILON)
    cube = inv * inv * inv * (column[:, 1:2] / inner_total)
    raw = gate[...]
    sig = jax.nn.sigmoid(raw)
    sil = raw * sig
    y = scan[...]
    gated = y * sil
    unit = gated * inv
    d_gate = dgate[...]
    gain = prm[1:2, :]
    glow[...] = (unit * gain).astype(BF16)
    late = pl.program_id(0) >= pl.num_programs(0) // 2
    for k, part in enumerate(rest[:-2]):

        @pl.when(late if k else jnp.logical_not(late))
        def _():
            part[...] = nt((gated * gain).astype(BF16), wo[...]).astype(BF16)

    gain_grad[...] += jnp.broadcast_to(jnp.sum(d_gate * unit, 0, keepdims=True), gain_grad.shape)
    d_gated = inv * gain * d_gate - gated * cube
    d_scan = d_gated * sil
    dscan[...] = d_scan
    dgr[...] = (d_gated * y * (sig * (1.0 + raw * (1.0 - sig)))).astype(BF16)
    input_c = silu(upre_c[...])
    for i in reversed(range(SUB)):
        rows = slice(i * CHUNK, (i + 1) * CHUNK)
        record = rec[rows, :]
        entry = record[:, ENTRY : ENTRY + 1] * jnp.exp(record)
        adj[i] = state[...]
        psx[8 * i : 8 * i + 8, :] = decay[...]
        passed = spread(entry[CHUNK - 1 :, :], pairs)
        fed = (d_scan[rows] * spread(entry, pairs)).astype(BF16)
        state[...] = passed * state[...] + nn(input_c[rows].T.astype(BF16), fed)
        decay[...] = decay[...] * passed
    fin[...] = state[...]
    decay_end[...] = decay[...]


def turn(
    scan, gate, dgate, sums, u, rec, prm, fin_before, decay_before, wo, inner_total, half, n_parts,
    after,
):
    rows, inner = scan.shape
    steps = rows // STEP
    chunks = rows // CHUNK
    first = half * steps
    state_size = LANES
    c_block = u.shape[1] // LANES - 1
    width = wo.shape[0]

    def whole(a):
        return pl.BlockSpec(a.shape, lambda i: (0,) * a.ndim)

    def tall(cols):
        return pl.BlockSpec((STEP, cols), lambda i: (first + steps - 1 - i, 0))

    def own(cols):
        return pl.BlockSpec((STEP, cols), lambda i: (steps - 1 - i, 0))

    return pl.pallas_call(
        ordered(functools.partial(turn_kernel, float(inner_total)), 10, len(after)),
        grid=(steps,),
        in_specs=[
            own(inner),
            tall(inner),
            own(inner),
            pl.BlockSpec((8, STEP), lambda i: (0, steps - 1 - i)),
            pl.BlockSpec((STEP, LANES), lambda i: (first + steps - 1 - i, c_block)),
            tall(LANES),
            whole(prm),
            whole(fin_before),
            whole(decay_before),
            whole(wo),
        ]
        + [ANYWHERE] * len(after),
        out_specs=[
            own(inner),
            own(inner),
            own(inner),
            pl.BlockSpec((SUB, state_size, inner), lambda i: (steps - 1 - i, 0, 0)),
            pl.BlockSpec((8 * SUB, inner), lambda i: (steps - 1 - i, 0)),
            pl.BlockSpec((state_size, inner), lambda i: (0, 0)),
            pl.BlockSpec((8, inner), lambda i: (0, 0)),
            pl.BlockSpec((8, inner), lambda i: (0, 0)),
        ]
        + [
            pl.BlockSpec((STEP, width), lambda i: (jnp.maximum(steps // 2 - 1 - i, 0), 0)),
            pl.BlockSpec(
                (STEP, width),
                lambda i: (jnp.minimum(steps - 1 - i, steps // 2 - 1), 0),
            ),
        ][:n_parts],
        out_shape=[
            jax.ShapeDtypeStruct((rows, inner), F32),
            jax.ShapeDtypeStruct((rows, inner), BF16),
            jax.ShapeDtypeStruct((rows, inner), BF16),
            jax.ShapeDtypeStruct((chunks, state_size, inner), F32),
            jax.ShapeDtypeStruct((8 * chunks, inner), F32),
            jax.ShapeDtypeStruct((state_size, inner), F32),
            jax.ShapeDtypeStruct((8, inner), F32),
            jax.ShapeDtypeStruct((8, inner), F32),
        ]
        + [jax.ShapeDtypeStruct((rows // 2, width), BF16)] * n_parts,
        scratch_shapes=[pltpu.VMEM((state_size, inner), F32), pltpu.VMEM((8, inner), F32)],
        compiler_params=pltpu.CompilerParams(
            dimension_semantics=("arbitrary",), vmem_limit_bytes=VMEM_LIMIT
        ),
        cost_estimate=lasts(0.01),
        name="turn",
    )(scan, gate, dgate, sums, u, rec, prm, fin_before, decay_before, wo, *after)


def back_kernel(
    u, rec, dscan, st, pdx, sin, adj, psx, ain, prm, dtp,
    dpre, dstep, skip_acc, head_acc,
):
    inner = dscan.shape[1]
    pairs = inner // LANES
    heads = 2 * pairs

    @pl.when(pl.program_id(0) == 0)
    def _():
        skip_acc[...] = jnp.zeros_like(skip_acc)
        head_acc[...] = jnp.zeros_like(head_acc)

    raw = u[...]
    sig = jax.nn.sigmoid(raw)
    act = raw * sig
    slope = sig * (1.0 + raw * (1.0 - sig))
    above = iota((CHUNK, CHUNK), 0) <= iota((CHUNK, CHUNK), 1)
    upper = above.astype(F32)
    lane = iota((CHUNK, LANES), 1)
    gather_heads = (iota((inner, LANES), 0) // (LANES // 2) == iota((inner, LANES), 1)).astype(BF16)
    nega = dtp[1:2, :]
    for i in range(SUB):
        rows = slice(i * CHUNK, (i + 1) * CHUNK)
        record = rec[rows, :]
        turned = record.T
        state = st[i] + pdx[8 * i : 8 * i + 1, :] * sin[...]
        state_low = state.astype(BF16)
        later = adj[i] + psx[8 * i : 8 * i + 1, :] * ain[...]
        later_low = later.astype(BF16)
        x = act[rows, :inner]
        b_wide = act[rows, inner : inner + LANES]
        c_wide = act[rows, inner + LANES :]
        input_b = b_wide.astype(BF16)
        input_c = c_wide.astype(BF16)
        dy = dscan[rows, :]
        scores = nt(input_b, input_c)
        barred = jnp.where(
            above & (record[:, SEG : SEG + 1] == turned[SEG : SEG + 1, :]), 0.0, NEGATIVE
        )
        step = pltpu.roll(record, LANES - 8, axis=1)
        z = pltpu.roll(record, LANES - RAW, axis=1)
        d_scores = jnp.zeros((CHUNK, CHUNK), F32)
        direct = jnp.zeros((CHUNK, LANES), F32)
        arrivals = []
        dxs = []
        for j in range(pairs):
            cols = slice(j * LANES, (j + 1) * LANES)
            x_sides = halves(x[:, cols].astype(BF16))
            dy_pair = dy[:, cols].astype(BF16)
            dy_sides = halves(dy_pair)
            total = None
            for k in range(2):
                h = 2 * j + k
                step_col = record[:, 8 + h : 9 + h]
                link = jnp.exp(turned[h : h + 1, :] - record[:, h : h + 1] + barred)
                d_link = nt(x_sides[k], dy_pair) * link
                d_scaled = d_link * step_col
                d_scores = d_scores + d_scaled
                flow = d_scaled * scores
                arrivals.append(jnp.sum(flow, 0, keepdims=True))
                given = jnp.sum(d_link * scores, 1, keepdims=True)
                direct = jnp.where(lane == h, given, direct)
                weight = (scores * link * step_col).astype(BF16)
                term = nn(weight, dy_sides[k])
                total = term if total is None else total + term
            dxs.append(total)
        dx = jnp.concatenate(dxs, 1)
        arrived = jnp.concatenate(arrivals + [jnp.zeros((CHUNK - heads, CHUNK), F32)], 0).T
        decay_in = record[:, ENTRY : ENTRY + 1] * jnp.exp(record)
        last = record[CHUNK - 1 :, :]
        tail_exp = record[:, TAIL : TAIL + 1] * jnp.exp(last - record)
        tail = tail_exp * step
        tail_wide = spread(jnp.where(lane < 8, tail, 0.0), pairs)
        fed_back = (dy * spread(decay_in, pairs)).astype(BF16)
        fed = (x * tail_wide).astype(BF16)
        from_state = nn(input_c, state_low)
        d_fed = nn(input_b, later_low)
        d_score_low = d_scores.astype(BF16)
        d_c = nt(fed_back, state_low) + nn(d_scores.T.astype(BF16), input_b)
        d_b = nt(fed, later_low) + nn(d_score_low, input_c)
        d_entry = nn((dy * from_state).astype(BF16), gather_heads)
        d_tail = nn((x * d_fed).astype(BF16), gather_heads)
        through = jnp.broadcast_to(jnp.sum(later * state, 0, keepdims=True), (16, inner))
        d_through = nn(through.astype(BF16), gather_heads)[0:1, :]
        dx = dx + d_fed * tail_wide + prm[0:1, :] * dy
        tail_flow = d_tail * tail
        d_cum = arrived - direct * step + d_entry * decay_in - tail_flow
        d_cum = jnp.where(lane < 8, d_cum, 0.0)
        d_last = jnp.sum(tail_flow, 0, keepdims=True) + decay_in[CHUNK - 1 :, :] * d_through
        d_rate = exact(upper, d_cum) + jnp.where(lane < 8, d_last, 0.0)
        d_step = direct + d_tail * tail_exp + nega * d_rate
        d_z = jnp.where(lane < 8, d_step * jax.nn.sigmoid(z), 0.0)
        dstep[rows, :] = d_z.astype(BF16)
        dpre[rows, :] = jnp.concatenate([dx, d_b, d_c], 1) * slope[rows]
        skip_acc[...] += jnp.broadcast_to(jnp.sum(dy * x, 0, keepdims=True), skip_acc.shape)
        head_acc[0:1, :] += jnp.sum(d_z, 0, keepdims=True)
        head_acc[1:2, :] += jnp.sum(
            jnp.where(lane < 8, d_rate * (nega * step), 0.0), 0, keepdims=True
        )


def back(u, rec, dscan, st, pdx, sin, adj, psx, ain, prm, dtp, after, group):
    rows, wide = u.shape
    inner = dscan.shape[1]
    steps = rows // STEP // GROUPS
    first = group * steps
    in_half = group % (GROUPS // 2) * steps

    def whole(a):
        return pl.BlockSpec(a.shape, lambda i: (0,) * a.ndim)

    def tall(cols):
        return pl.BlockSpec((STEP, cols), lambda i: (first + i, 0))

    def out_tall(cols):
        return pl.BlockSpec((STEP, cols), lambda i: (i, 0))

    def states(at):
        return pl.BlockSpec((SUB,) + st.shape[1:], lambda i: (at + i, 0, 0))

    def decays(at):
        return pl.BlockSpec((8 * SUB, inner), lambda i: (at + i, 0))

    return pl.pallas_call(
        ordered(back_kernel, 11, len(after)),
        grid=(steps,),
        in_specs=[
            tall(wide),
            tall(LANES),
            pl.BlockSpec((STEP, inner), lambda i: (in_half + i, 0)),
            states(first),
            decays(first),
            whole(sin),
            states(in_half),
            decays(in_half),
            whole(ain),
            whole(prm),
            whole(dtp),
        ]
        + [ANYWHERE] * len(after),
        out_specs=[
            out_tall(wide),
            out_tall(LANES),
            pl.BlockSpec((8, inner), lambda i: (0, 0)),
            pl.BlockSpec((8, LANES), lambda i: (0, 0)),
        ],
        out_shape=[
            jax.ShapeDtypeStruct((steps * STEP, wide), F32),
            jax.ShapeDtypeStruct((steps * STEP, LANES), BF16),
            jax.ShapeDtypeStruct((8, inner), F32),
            jax.ShapeDtypeStruct((8, LANES), F32),
        ],
        compiler_params=pltpu.CompilerParams(
            dimension_semantics=("arbitrary",), vmem_limit_bytes=VMEM_LIMIT
        ),
        cost_estimate=lasts(0.01),
        name="back",
    )(u, rec, dscan, st, pdx, sin, adj, psx, ain, prm, dtp, *after)


def rear_kernel(
    dpre, rec, pre, dgr, dstep, follow, w, cw,
    dproj, dnorm, conv_acc,
    buf, mbuf,
):
    wide = dpre.shape[1]
    inner = dgr.shape[1]

    @pl.when(pl.program_id(0) == 0)
    def _():
        buf[STEP : STEP + 8, :] = follow[:, :wide]
        mbuf[STEP : STEP + 8, :] = follow[:, wide:]
        conv_acc[...] = jnp.zeros_like(conv_acc)

    @pl.when(pl.program_id(0) > 0)
    def _():
        buf[STEP : STEP + 8, :] = buf[0:8, :]
        mbuf[STEP : STEP + 8, :] = mbuf[0:8, :]

    grad = dpre[...]
    buf[0:STEP, :] = grad
    mbuf[0:STEP, :] = rec[...]
    value = pre[...]
    total = cw[3:4, :] * grad
    conv_acc[3:4, :] += jnp.sum(value * grad, 0, keepdims=True)
    conv_acc[4:5, :] += jnp.sum(grad, 0, keepdims=True)
    for shift in (1, 2, 3):
        mark = mbuf[shift : shift + STEP, :][:, M1 + shift - 1 : M1 + shift]
        moved = buf[shift : shift + STEP, :] * mark
        total = total + cw[3 - shift : 4 - shift, :] * moved
        conv_acc[3 - shift : 4 - shift, :] += jnp.sum(value * moved, 0, keepdims=True)
    dproj[:, :inner] = dgr[...]
    dproj[:, inner : inner + wide] = total.astype(BF16)
    dproj[:, inner + wide :] = dstep[...]
    dnorm[...] = nt(dproj[...], w[...]).astype(BF16)


def rear(dpre, rec, pre, dgr, dstep, follow, w, cw, after, group):
    rows, wide = dpre.shape
    in_half = group % (GROUPS // 2) * (rows // STEP)
    steps = rows // STEP
    inner = dgr.shape[1]
    width, packed = w.shape
    first = group * steps

    def whole(a):
        return pl.BlockSpec(a.shape, lambda i: (0,) * a.ndim)

    def tall(cols):
        return pl.BlockSpec((STEP, cols), lambda i: (first + steps - 1 - i, 0))

    def own(cols):
        return pl.BlockSpec((STEP, cols), lambda i: (steps - 1 - i, 0))

    return pl.pallas_call(
        ordered(rear_kernel, 8, len(after)),
        grid=(steps,),
        in_specs=[
            own(wide),
            tall(LANES),
            tall(wide),
            pl.BlockSpec((STEP, inner), lambda i: (in_half + steps - 1 - i, 0)),
            own(LANES),
            whole(follow),
            whole(w),
            whole(cw),
        ]
        + [ANYWHERE] * len(after),
        out_specs=[
            own(packed),
            own(width),
            pl.BlockSpec((8, wide), lambda i: (0, 0)),
        ],
        out_shape=[
            jax.ShapeDtypeStruct((rows, packed), BF16),
            jax.ShapeDtypeStruct((rows, width), BF16),
            jax.ShapeDtypeStruct((8, wide), F32),
        ],
        scratch_shapes=[
            pltpu.VMEM((STEP + 8, wide), F32),
            pltpu.VMEM((STEP + 8, LANES), F32),
        ],
        compiler_params=pltpu.CompilerParams(
            dimension_semantics=("arbitrary",), vmem_limit_bytes=VMEM_LIMIT
        ),
        cost_estimate=lasts(0.01),
        name="rear",
    )(dpre, rec, pre, dgr, dstep, follow, w, cw, *after)


def settle_kernel(inner_total, hid, sums, given, held, outer, filled, out):
    column = jnp.concatenate([sums[...], jnp.zeros((LANES - 8, STEP), F32)], 0).T
    inv = lax.rsqrt(column[:, 0:1] / inner_total + EPSILON)
    total = jnp.where(outer[0:1, 0:1] > 0.0, given[...].astype(F32), held[...].astype(F32))
    out[...] = (hid[...].astype(F32) + inv * total).astype(BF16)


def finish_kernel(hid, cot, gain, given, held, outer, filled, out):
    x = hid[...].astype(F32)
    inv = lax.rsqrt(jnp.mean(x * x, -1, keepdims=True) + EPSILON)
    total = jnp.where(outer[0:1, 0:1] > 0.0, given[...].astype(F32), held[...].astype(F32))
    scaled = total * gain[0:1, :]
    cross = jnp.mean(scaled * x, -1, keepdims=True)
    out[...] = cot[...].astype(F32) + inv * scaled - x * (inv * inv * inv * cross)


def by_group(kernel, out_like, dtype, group, fresh, operands, filled, after, name):
    rows, width = out_like.shape
    steps = rows // GROUPS // STEP
    first = group * steps
    in_half = group % (GROUPS // 2) * steps
    specs = {
        "all": lambda a: pl.BlockSpec((STEP, a.shape[1]), lambda i: (first + i, 0)),
        "group": lambda a: pl.BlockSpec((STEP, a.shape[1]), lambda i: (i, 0)),
        "half": lambda a: pl.BlockSpec((8, STEP), lambda i: (0, in_half + i)),
        "whole": lambda a: pl.BlockSpec(a.shape, lambda i: (0, 0)),
    }
    count = len(operands) + 1
    return pl.pallas_call(
        ordered(kernel, count, len(after)),
        grid=(steps,),
        in_specs=[specs[kind](a) for a, kind in operands] + [ANYWHERE] * (1 + len(after)),
        out_specs=pl.BlockSpec((STEP, width), lambda i: (first + i, 0)),
        out_shape=jax.ShapeDtypeStruct((rows, width), dtype),
        input_output_aliases={} if fresh else {count - 1: 0},
        compiler_params=pltpu.CompilerParams(
            dimension_semantics=("arbitrary",), vmem_limit_bytes=VMEM_LIMIT
        ),
        cost_estimate=lasts(0.01),
        name=name,
    )(*[a for a, _ in operands], filled, *after)


def passed_along(value, axis, steps):
    count = lax.axis_size(axis)
    leading, last = (max(0, -steps), min(count, count - steps))
    return lax.ppermute(value, axis, [(source, source + steps) for source in range(leading, last)])


def chained(own, decay, axis, steps):
    entering = jnp.zeros_like(own)
    for turn_at in range(lax.axis_size(axis) - 1):
        leaving = own if turn_at == 0 else own + decay * entering
        entering = passed_along(leaving, axis, steps)
    return entering


def butterfly_sum(value, axis):
    bit = 1
    while bit < lax.axis_size(axis):
        pairs = [(i, i ^ bit) for i in range(lax.axis_size(axis))]
        value = value + lax.ppermute(value, axis, pairs)
        bit *= 2
    return value


def join_kernel(*refs):
    pairs = len(refs) // 3
    for k in range(pairs):
        left, right, out = refs[2 * k], refs[2 * k + 1], refs[2 * pairs + k]
        out[...] = (left[...].astype(F32) + right[...].astype(F32)).astype(out.dtype)


def join(pairs, after):
    rows, width = pairs[0][0].shape
    spec = pl.BlockSpec((STEP, width), lambda i: (i, 0))
    return pl.pallas_call(
        ordered(join_kernel, 2 * len(pairs), len(after)),
        grid=(rows // STEP,),
        in_specs=[spec] * (2 * len(pairs)) + [ANYWHERE] * len(after),
        out_specs=[spec] * len(pairs),
        out_shape=[jax.ShapeDtypeStruct((rows, width), BF16)] * len(pairs),
        compiler_params=pltpu.CompilerParams(
            dimension_semantics=("arbitrary",), vmem_limit_bytes=VMEM_LIMIT
        ),
        cost_estimate=lasts(0.01),
        name="join",
    )(*[a for pair in pairs for a in pair], *after)


class LineSum:
    def __init__(self, value):
        self.own = value
        self.come = lax.ppermute(value, "tp", [(0, 1), (3, 2)])
        self.near = self.across = self.given = None

    def pair(self):
        return (self.own if self.near is None else self.near, self.come)

    def joined(self, value):
        if self.near is None:
            self.near = value
            self.come = lax.ppermute(value, "tp", [(1, 2), (2, 1)])
        else:
            self.across = value
            self.given = lax.ppermute(value, "tp", [(1, 0), (2, 3)])


def advance(sums, after):
    outs = join([one.pair() for one in sums], after)
    for one, value in zip(sums, outs):
        one.joined(value)
    return tuple(outs)


def total_kernel(own, one, two, three, held, out, released):
    out[...] = (own[...] + one[...]) + (two[...] + three[...])


def total_over_row(own, held):
    others = [lax.ppermute(own, "tp", [(i, i ^ bits) for i in range(4)]) for bits in (1, 2, 3)]
    spec = pl.BlockSpec(own.shape, lambda i: (0, 0))
    return pl.pallas_call(
        total_kernel,
        grid=(1,),
        in_specs=[spec] * 4 + [ANYWHERE],
        out_specs=[spec, ANYWHERE],
        out_shape=[
            jax.ShapeDtypeStruct(own.shape, own.dtype),
            jax.ShapeDtypeStruct(held.shape, held.dtype),
        ],
        input_output_aliases={4: 1},
        cost_estimate=lasts(0.01),
        name="total",
    )(own, *others, held)


def other_core_kernel(place, w, wo, out):
    packed = w.shape[1]
    out[:, :packed] = w[...].astype(BF16)
    out[:, packed:] = wo[...].astype(BF16)


def split_kernel(
    place, w_ka, w_sa, w_kb, w_sb, wo_kb, wo_sb, r_ka, r_sa, r_kb, r_sb,
    keep_a, send_a, keep_b, send_b,
):
    cut, packed = keep_a.shape[1], w_ka.shape[1]
    keep_a[...] = w_ka[:, :cut] + r_ka[:, :cut].astype(F32)
    send_a[...] = (w_sa[:, :cut] + r_sa[:, :cut].astype(F32)).astype(BF16)
    for w, wo, r, out in ((w_kb, wo_kb, r_kb, keep_b), (w_sb, wo_sb, r_sb, send_b)):
        out[:, : packed - cut] = (w[:, cut:] + r[:, cut:packed].astype(F32)).astype(out.dtype)
        out[:, packed - cut :] = (wo[...] + r[:, packed:].astype(F32)).astype(out.dtype)


def second_kernel(place, ka, ra, sa, rsa, kb, rb, sb, rsb, keep_a, send_a, keep_b, send_b):
    keep_a[...] = ka[...] + ra[...].astype(F32)
    send_a[...] = (sa[...] + rsa[...].astype(F32)).astype(BF16)
    keep_b[...] = kb[...] + rb[...].astype(F32)
    send_b[...] = (sb[...] + rsb[...].astype(F32)).astype(BF16)


def placed_call(kernel, steps, place, inputs, outputs, name, after=()):
    return pl.pallas_call(
        ordered(kernel, 1 + len(inputs), len(after)),
        grid_spec=pltpu.PrefetchScalarGridSpec(
            num_scalar_prefetch=1,
            grid=(steps,),
            in_specs=[
                pl.BlockSpec((LANES, a.shape[1]), functools.partial(lambda f, i, p: (f(i, p), 0), f))
                for a, f in inputs
            ]
            + [ANYWHERE] * len(after),
            out_specs=[pl.BlockSpec((LANES, cols), lambda i, p: (i, 0)) for cols, _ in outputs],
        ),
        out_shape=[jax.ShapeDtypeStruct((steps * LANES, cols), kind) for cols, kind in outputs],
        compiler_params=pltpu.CompilerParams(
            dimension_semantics=("arbitrary",), vmem_limit_bytes=VMEM_LIMIT
        ),
        cost_estimate=lasts(0.01),
        name=name,
    )(place, *[a for a, _ in inputs], *after)


def to_owners(w, wo, after):
    packed, extra = w.shape[1], wo.shape[1]
    if lax.axis_size("fsdp") != 4 or lax.axis_size("ctx") != 2 or w.shape[0] != 8 * LANES:
        both = jnp.concatenate([w, wo], 1)
        return lax.psum_scatter(both, ("fsdp", "ctx"), scatter_dimension=0, tiled=True)

    def swapped(value, axis, bit):
        count = lax.axis_size(axis)
        return lax.ppermute(value, axis, [(i, i ^ bit) for i in range(count)])

    fsdp = lax.axis_index("fsdp")
    place = jnp.stack([fsdp % 2, fsdp // 2, lax.axis_index("ctx")]).astype(jnp.int32)
    cut = 1024
    rest = packed + extra - cut

    (sent,) = placed_call(
        other_core_kernel, 4, place,
        [(w, lambda i, p: 2 * i + 1 - p[2]), (wo, lambda i, p: 2 * i + 1 - p[2])],
        [(packed + extra, BF16)], "other_core", after,
    )
    come = swapped(sent, "ctx", 1)
    of = {
        "ka": lambda i, p: 2 * i + p[0],
        "sa": lambda i, p: 2 * i + 1 - p[0],
        "kb": lambda i, p: 2 * p[1] + i,
        "sb": lambda i, p: 2 * (1 - p[1]) + i,
    }

    def own(key):
        return lambda i, p: 2 * of[key](i, p) + p[2]

    keep_a, send_a, keep_b, send_b = placed_call(
        split_kernel, 2, place,
        [(w, own(key)) for key in ("ka", "sa", "kb", "sb")]
        + [(wo, own(key)) for key in ("kb", "sb")]
        + [(come, of[key]) for key in ("ka", "sa", "kb", "sb")],
        [(cut, F32), (cut, BF16), (rest, F32), (rest, BF16)], "split",
    )
    come_a, come_b = swapped(send_a, "fsdp", 1), swapped(send_b, "fsdp", 2)
    y, not_y = (lambda i, p: p[1]), (lambda i, p: 1 - p[1])
    x, not_x = (lambda i, p: p[0]), (lambda i, p: 1 - p[0])
    keep_a, send_a, keep_b, send_b = placed_call(
        second_kernel, 1, place,
        [(keep_a, y), (come_a, y), (keep_a, not_y), (come_a, not_y)]
        + [(keep_b, x), (come_b, x), (keep_b, not_x), (come_b, not_x)],
        [(cut, F32), (cut, BF16), (rest, F32), (rest, BF16)], "second",
    )
    come_a, come_b = swapped(send_a, "fsdp", 2), swapped(send_b, "fsdp", 1)
    return jnp.concatenate(
        [keep_a + come_a.astype(F32), keep_b + come_b.astype(F32)], 1
    )


def flip_kernel(value, out):
    out[...] = value[...].astype(F32).T.astype(out.dtype)


def flipped(value, after):
    rows, cols = value.shape
    return pl.pallas_call(
        ordered(flip_kernel, 1, len(after)),
        grid=(1,),
        in_specs=[pl.BlockSpec((rows, cols), lambda i: (0, 0))] + [ANYWHERE] * len(after),
        out_specs=pl.BlockSpec((cols, rows), lambda i: (0, 0)),
        out_shape=jax.ShapeDtypeStruct((cols, rows), value.dtype),
        cost_estimate=lasts(0.01),
        name="flip",
    )(value, *after)


def gathered_shards(own):
    rows = own.shape[0]
    if lax.axis_size("fsdp") != 4 or lax.axis_size("ctx") != 2:
        return [lax.all_gather(own, ("fsdp", "ctx"), axis=0, tiled=True)], [0]

    def swapped(value, axis, bit):
        count = lax.axis_size(axis)
        return lax.ppermute(value, axis, [(i, i ^ bit) for i in range(count)])

    half = rows // 2
    by_one, by_two = swapped(own, "fsdp", 1), swapped(own, "fsdp", 2)
    upper = swapped(by_two[:half], "fsdp", 1)
    under = swapped(by_one[half:], "fsdp", 2)
    mine = [own, by_one, by_two, upper, under]
    place = lax.axis_index("fsdp")
    core = lax.axis_index("ctx")
    shards, starts = [], []
    for other in (0, 1):
        for value, bits, offset in zip(mine, (0, 1, 2, 3, 3), (0, 0, 0, 0, half)):
            shards.append(swapped(value, "ctx", 1) if other else value)
            starts.append(((place ^ bits) * 2 + (core ^ other)) * rows + offset)
    return shards, starts


def token_marks(segment, before):
    rows = segment.shape[0]
    joined = jnp.concatenate([before, segment])
    marks = [joined[3 - j : 3 - j + rows] == segment for j in (1, 2, 3)]
    blocks = segment.reshape(-1, CHUNK)
    previous = jnp.concatenate([before[2:], blocks[:-1, -1]])
    marks.append((blocks == previous[:, None]).reshape(-1))
    marks.append((blocks == blocks[:, -1:]).reshape(-1))
    marks.append(segment)
    table = jnp.stack([mark.astype(F32) for mark in marks], 1)
    return jnp.pad(table, ((0, 0), (M1, LANES - M1 - len(marks))))


def body(
    hidden, segments, out_grad, norm_gain, w_zx, w_dt, w_bc, conv_x_w, conv_x_b,
    conv_bc_w, conv_bc_b, dt_bias, a_log, skip_d, out_gain, w_out,
):
    _, rows, width = hidden.shape
    inner = w_zx.shape[2]
    heads = w_dt.shape[1]
    head_size = inner // heads
    state_size = w_bc.shape[2]
    wide = inner + 2 * state_size
    taps = conv_x_w.shape[0]
    owned = w_zx.shape[0]
    shards = ("fsdp", "ctx")
    hid = hidden[0]
    cot = out_grad[0]
    segment = segments[0]

    packed = jnp.concatenate(
        [
            w_zx.reshape(owned, 2 * inner),
            w_bc.reshape(owned, 2 * state_size),
            w_dt, w_dt, w_dt, w_dt,
            norm_gain[:, None],
            jnp.zeros((owned, LANES - 4 * heads - 1), BF16),
        ],
        1,
    )
    w_shards, w_starts = gathered_shards(packed)
    w_starts = jnp.stack([jnp.asarray(start, jnp.int32) for start in w_starts])
    wo = lax.all_gather(
        flipped(w_out, tuple(w_shards[1:3])), shards, axis=0, tiled=True
    )

    edge, edge_segment = passed_along((hid[rows - EDGE :], segment[rows - 3 :]), "ctx", 1)
    tok = token_marks(segment, edge_segment)
    conv_rows = jnp.concatenate(
        [
            jnp.concatenate([conv_x_w, conv_bc_w.reshape(taps, -1)], 1),
            jnp.concatenate([conv_x_b, conv_bc_b.reshape(-1)])[None],
            jnp.zeros((8 - taps - 1, wide), F32),
        ],
        0,
    )
    spare = jnp.zeros((LANES - 4 * heads,), F32)
    rate = -jnp.exp(a_log)
    dtp = jnp.concatenate(
        [
            jnp.concatenate([dt_bias] * 4 + [spare])[None],
            jnp.concatenate([rate] * 4 + [spare])[None],
            jnp.zeros((6, LANES), F32),
        ],
        0,
    )
    prm = jnp.concatenate(
        [jnp.repeat(skip_d, head_size)[None], out_gain[None], jnp.zeros((6, inner), F32)], 0
    )

    normed, gate, pre, u, rec, st, pdx, state_end, decay_end, w_in, gain = front(
        hid, edge, tok, w_shards, w_starts, 4 * heads, conv_rows, dtp, inner, wide
    )
    sin = chained(state_end, decay_end[:1], "ctx", 1)
    inner_total = inner * lax.axis_size("tp")
    me = lax.axis_index("tp")
    outer = jnp.full((8, LANES), (me == 0) | (me == lax.axis_size("tp") - 1), F32)

    out_sums = [None] * GROUPS
    scan_hi, dgate_hi, sums_hi, part = middle(u, rec, gate, st, pdx, sin, cot, wo, prm, 1, True)
    sums_hi, part = total_over_row(sums_hi, part)
    out_sums[2] = LineSum(part)
    scan_lo, dgate_lo, sums_lo = middle(u, rec, gate, st, pdx, sin, cot, wo, prm, 0, False)
    *turned_hi, adj_start, out_gain_acc, decay_start, part = turn(
        scan_hi, dgate=dgate_hi, gate=gate, sums=sums_hi, u=u, rec=rec, prm=prm,
        fin_before=jnp.zeros_like(state_end), decay_before=jnp.ones_like(decay_end), wo=wo,
        inner_total=inner_total, half=1, n_parts=1, after=(sums_lo,),
    )
    sums_lo, part = total_over_row(sums_lo, part)
    out_sums[3] = LineSum(part)
    done = advance([out_sums[2]], (sums_lo,))
    *turned_lo, adj_start, gain_part, _, part_b, part_a = turn(
        scan_lo, dgate=dgate_lo, gate=gate, sums=sums_lo, u=u, rec=rec, prm=prm,
        fin_before=adj_start, decay_before=decay_start, wo=wo,
        inner_total=inner_total, half=0, n_parts=2, after=done,
    )
    out_sums[1], out_sums[0] = LineSum(part_b), LineSum(part_a)
    out_gain_acc = out_gain_acc + gain_part
    turned = [turned_lo, turned_hi]
    sums_of = [sums_lo, sums_hi]
    ain = chained(adj_start, decay_end[:1], "ctx", -1)
    contract_rows = (((0,), (0,)), ((), ()))
    glow = jnp.concatenate([turned_lo[2], turned_hi[2]], 0)
    wo_grad = lax.dot_general(cot, glow, contract_rows, preferred_element_type=F32)

    group_rows = rows // GROUPS
    backs = [None] * GROUPS
    rears = [None] * GROUPS
    d_normed = [None] * GROUPS
    follows = [None] * GROUPS

    def run_back(group, after):
        dscan, _, _, adj, psx = turned[group // (GROUPS // 2)]
        backs[group] = back(u, rec, dscan, st, pdx, sin, adj, psx, ain, prm, dtp, after, group)
        start = jnp.concatenate(
            [backs[group][0][:8], rec[group * group_rows : group * group_rows + 8]], 1
        )
        if group == 0:
            follows[GROUPS - 1] = passed_along(start, "ctx", -1)
        else:
            follows[group - 1] = start

    def run_rear(group, after):
        dgr = turned[group // (GROUPS // 2)][1]
        rears[group] = rear(
            backs[group][0], rec, pre, dgr, backs[group][1], follows[group], w_in,
            conv_rows, after, group,
        )
        d_normed[group] = LineSum(rears[group][1])

    def settle(group, filled, after=()):
        total = out_sums[group]
        return by_group(
            functools.partial(settle_kernel, float(inner_total)), hid, BF16, group, filled is None,
            [
                (hid, "all"),
                (sums_of[group // (GROUPS // 2)], "half"),
                (total.given, "group"),
                (total.across, "group"),
                (outer, "whole"),
            ],
            outer if filled is None else filled, after, "settle",
        )

    def finish(group, filled, after):
        total = d_normed[group]
        return by_group(
            finish_kernel, hid, F32, group, filled is None,
            [
                (hid, "all"),
                (cot, "all"),
                (gain, "whole"),
                (total.given, "group"),
                (total.across, "group"),
                (outer, "whole"),
            ],
            outer if filled is None else filled, after, "finish",
        )

    sum_a, sum_b, sum_c, sum_d = (out_sums[group] for group in (2, 3, 1, 0))
    done = advance([sum_a], (wo_grad,))
    run_back(0, done)
    done = advance([sum_b], (backs[0][3],))
    run_back(1, done)
    run_rear(0, ())
    done = advance([sum_c, sum_b], (rears[0][2],))
    block_out = settle(2, None, done)
    run_back(2, (block_out,))
    run_rear(1, (backs[2][3],))
    done = advance([sum_d, sum_c], (rears[1][2],))
    block_out = settle(3, block_out, done)
    run_back(3, (block_out,))
    run_rear(2, (backs[3][3],))
    done = advance([d_normed[0], d_normed[1], sum_d], (rears[2][2],))
    block_out = settle(1, block_out, done)
    run_rear(3, (block_out,))

    conv_acc = sum(r[2] for r in rears)
    skip_acc = sum(b[2][0] for b in backs)
    head_acc = sum(b[3] for b in backs)

    dproj = jnp.concatenate([r[0] for r in rears], 0)
    w_grad = lax.dot_general(normed, dproj, contract_rows, preferred_element_type=F32)
    done = advance([d_normed[2], d_normed[0]], (w_grad[:8, :LANES],))
    both_owned = to_owners(w_grad, wo_grad, done)
    block_out = settle(0, block_out, done)
    done = advance([d_normed[1]], (block_out,))
    done = advance([d_normed[3], d_normed[2]], done)
    hidden_grad = finish(0, None, done)
    done = advance([d_normed[3]], (hidden_grad,))
    for group in range(1, GROUPS):
        hidden_grad = finish(group, hidden_grad, done)
    w_owned, wo_owned = both_owned[:, : w_grad.shape[1]], both_owned[:, w_grad.shape[1] :]

    small = jnp.concatenate(
        [
            conv_acc[: taps + 1].reshape(-1),
            out_gain_acc[0],
            skip_acc,
            head_acc[:2].reshape(-1),
        ]
    )
    small = butterfly_sum(butterfly_sum(small, "ctx"), "fsdp")
    conv_sum = small[: (taps + 1) * wide].reshape(taps + 1, wide)
    rest = small[(taps + 1) * wide :]
    shared = jnp.concatenate(
        [
            w_owned[:, 2 * inner : 2 * inner + 2 * state_size].reshape(-1),
            jnp.sum(packed.astype(F32) * w_owned, 1),
            conv_sum[:, inner:].reshape(-1),
        ]
    )
    shared = butterfly_sum(shared, "tp")
    bc_size = owned * 2 * state_size
    bc_owned = shared[:bc_size].reshape(owned, 2, state_size)
    gain_owned = shared[bc_size : bc_size + owned] / norm_gain.astype(F32)
    conv_bc = shared[bc_size + owned :].reshape(taps + 1, 2, state_size)

    return (
        block_out[None],
        hidden_grad[None],
        gain_owned,
        w_owned[:, : 2 * inner].reshape(owned, 2, inner),
        w_owned[:, 2 * inner + 2 * state_size : 2 * inner + 2 * state_size + heads],
        bc_owned,
        conv_sum[:taps, :inner],
        conv_sum[taps, :inner],
        conv_bc[:taps],
        conv_bc[taps],
        rest[2 * inner : 2 * inner + heads],
        rest[2 * inner + LANES : 2 * inner + LANES + heads],
        jnp.sum(rest[inner : 2 * inner].reshape(heads, head_size), 1),
        rest[:inner],
        wo_owned.T,
    )


def solution(mesh):
    placed = (
        P("fsdp", "ctx", None),
        P("fsdp", "ctx"),
        P("fsdp", "ctx", None),
        P(("fsdp", "ctx")),
        P(("fsdp", "ctx"), None, "tp"),
        P(("fsdp", "ctx"), "tp"),
        P(("fsdp", "ctx"), None, None),
        P(None, "tp"),
        P("tp"),
        P(),
        P(),
        P("tp"),
        P("tp"),
        P("tp"),
        P("tp"),
        P("tp", ("fsdp", "ctx")),
    )
    return jax.shard_map(
        body,
        mesh=mesh,
        in_specs=placed,
        out_specs=(
            P("fsdp", "ctx", None),
            P("fsdp", "ctx", None),
            P(("fsdp", "ctx")),
            P(("fsdp", "ctx"), None, "tp"),
            P(("fsdp", "ctx"), "tp"),
            P(("fsdp", "ctx"), None, None),
            P(None, "tp"),
            P("tp"),
            P(),
            P(),
            P("tp"),
            P("tp"),
            P("tp"),
            P("tp"),
            P("tp", ("fsdp", "ctx")),
        ),
        check_vma=False,
    )
```

```python
import functools

import jax
import jax.numpy as jnp
from jax import lax
from jax.experimental import pallas as pl
from jax.experimental.pallas import tpu as pltpu
from jax.sharding import PartitionSpec as P

CHUNK = 128
STEP = 256
SUB = STEP // CHUNK
LANES = 128
EDGE = 16
GROUPS = 4
EPSILON = 1e-05
EXACT = lax.Precision.HIGHEST
F32 = jnp.float32
BF16 = jnp.bfloat16
NEGATIVE = -1e30
M1, M2, M3, ENTRY, TAIL, SEG, RAW = 16, 17, 18, 19, 20, 21, 24
VMEM_LIMIT = 56 * 1024 * 1024


def nn(a, b):
    return lax.dot_general(a, b, (((1,), (0,)), ((), ())), preferred_element_type=F32)


def nt(a, b):
    return lax.dot_general(a, b, (((1,), (1,)), ((), ())), preferred_element_type=F32)


def tn(a, b):
    return nn(a.T, b)


def exact(a, b):
    return lax.dot_general(
        a, b, (((1,), (0,)), ((), ())), precision=EXACT, preferred_element_type=F32
    )


def lasts(microseconds):
    return pl.CostEstimate(
        flops=0, bytes_accessed=int(microseconds * 3.69e6), transcendentals=0
    )


ANYWHERE = pl.BlockSpec(memory_space=pl.ANY)


def ordered(kernel, inputs, after):
    def run(*refs):
        kernel(*refs[:inputs], *refs[inputs + after :])

    return run


def iota(shape, dim):
    return lax.broadcasted_iota(jnp.int32, shape, dim)


def spread(per_head, pairs):
    rows = per_head.shape[0]
    low = iota((rows, LANES), 1) < LANES // 2
    parts = []
    for j in range(pairs):
        left = jnp.broadcast_to(per_head[:, 2 * j : 2 * j + 1], (rows, LANES))
        right = jnp.broadcast_to(per_head[:, 2 * j + 1 : 2 * j + 2], (rows, LANES))
        parts.append(jnp.where(low, left, right))
    return jnp.concatenate(parts, 1)


def halves(block):
    low = iota(block.shape, 1) < LANES // 2
    zero = jnp.zeros_like(block)
    return jnp.where(low, block, zero), jnp.where(low, zero, block)


def silu(v):
    return v * jax.nn.sigmoid(v)


def rms_unit(x):
    return x * lax.rsqrt(jnp.mean(x * x, -1, keepdims=True) + EPSILON)


def front_kernel(
    gain_lane, starts, hid, edge, tok, cw, dtp, *refs
):
    (normed, gate, pre_out, u_out, rec, st, pdx, fin, pdfin, w, gain_out,
     buf, state, decay) = refs[-14:]
    shards = refs[:-14]
    inner = gate.shape[1]
    wide = pre_out.shape[1]
    pairs = inner // LANES
    at = pl.program_id(0)

    @pl.when(at == 0)
    def _():
        for k, shard in enumerate(shards):
            size = shard.shape[0]
            w[pl.ds(pl.multiple_of(starts[k], 16), size), :] = shard[...]
        for k in range(w.shape[0] // LANES):
            tile = w[k * LANES : (k + 1) * LANES, inner + wide :].astype(F32).T
            gain_out[:, k * LANES : (k + 1) * LANES] = jnp.broadcast_to(
                tile[gain_lane : gain_lane + 1, :], (8, LANES)
            )
        edge_low = (rms_unit(edge[...].astype(F32)) * gain_out[0:1, :]).astype(BF16)
        edge_pre = nn(edge_low, w[:, inner : inner + wide])
        buf[0:8, :] = edge_pre[EDGE - 8 :, :]
        state[...] = jnp.zeros_like(state)
        decay[...] = jnp.ones_like(decay)

    @pl.when(at > 0)
    def _():
        buf[0:8, :] = buf[STEP : STEP + 8, :]

    low = (rms_unit(hid[...].astype(F32)) * gain_out[0:1, :]).astype(BF16)
    normed[...] = low
    gate[...] = nn(low, w[:, :inner])
    pre = nn(low, w[:, inner : inner + wide])
    pre_out[...] = pre
    buf[8 : 8 + STEP, :] = pre
    raw_all = nn(low, w[:, inner + wide :]) + dtp[0:1, :]
    marks = tok[...]
    u = cw[3:4, :] * pre + cw[4:5, :]
    u = u + cw[2:3, :] * (buf[7 : 7 + STEP, :] * marks[:, M1 : M1 + 1])
    u = u + cw[1:2, :] * (buf[6 : 6 + STEP, :] * marks[:, M2 : M2 + 1])
    u = u + cw[0:1, :] * (buf[5 : 5 + STEP, :] * marks[:, M3 : M3 + 1])
    u_out[...] = u
    act = silu(u)
    step_all = jax.nn.softplus(raw_all)
    lane = iota((CHUNK, LANES), 1)
    lower = (iota((CHUNK, CHUNK), 0) >= iota((CHUNK, CHUNK), 1)).astype(F32)
    for i in range(SUB):
        rows = slice(i * CHUNK, (i + 1) * CHUNK)
        step = step_all[rows]
        cum = exact(lower, step * dtp[1:2, :])
        mark = marks[rows]
        rec[rows, :] = jnp.where(
            lane < 8, cum, jnp.where(lane < 16, step, jnp.where(lane < 24, mark, raw_all[rows]))
        )
        last = cum[CHUNK - 1 :, :]
        tail = mark[:, TAIL : TAIL + 1] * jnp.exp(last - cum) * step
        fed = (act[rows, :inner] * spread(tail, pairs)).astype(BF16)
        st[i] = state[...]
        pdx[8 * i : 8 * i + 8, :] = decay[...]
        passed = spread(mark[CHUNK - 1 :, ENTRY : ENTRY + 1] * jnp.exp(last), pairs)
        input_b = act[rows, inner : inner + LANES].T.astype(BF16)
        state[...] = passed * state[...] + nn(input_b, fed)
        decay[...] = decay[...] * passed
    fin[...] = state[...]
    pdfin[...] = decay[...]


def front(hidden, edge, tok, shards, starts, gain_lane, cw, dtp, inner, wide):
    rows, width = hidden.shape
    packed = shards[0].shape[1]
    steps = rows // STEP
    state_size = LANES

    def whole(a):
        return pl.BlockSpec(a.shape, lambda i: (0,) * a.ndim)

    def tall(cols):
        return pl.BlockSpec((STEP, cols), lambda i: (i, 0))

    chunks = rows // CHUNK
    return pl.pallas_call(
        functools.partial(front_kernel, gain_lane),
        grid=(steps,),
        in_specs=[
            pl.BlockSpec(memory_space=pltpu.SMEM),
            tall(width),
            whole(edge),
            tall(LANES),
            whole(cw),
            whole(dtp),
        ]
        + [whole(shard) for shard in shards],
        out_specs=[
            tall(width),
            tall(inner),
            tall(wide),
            tall(wide),
            tall(LANES),
            pl.BlockSpec((SUB, state_size, inner), lambda i: (i, 0, 0)),
            pl.BlockSpec((8 * SUB, inner), lambda i: (i, 0)),
            pl.BlockSpec((state_size, inner), lambda i: (0, 0)),
            pl.BlockSpec((8, inner), lambda i: (0, 0)),
            pl.BlockSpec((width, packed), lambda i: (0, 0)),
            pl.BlockSpec((8, width), lambda i: (0, 0)),
        ],
        out_shape=[
            jax.ShapeDtypeStruct((rows, width), BF16),
            jax.ShapeDtypeStruct((rows, inner), F32),
            jax.ShapeDtypeStruct((rows, wide), F32),
            jax.ShapeDtypeStruct((rows, wide), F32),
            jax.ShapeDtypeStruct((rows, LANES), F32),
            jax.ShapeDtypeStruct((chunks, state_size, inner), F32),
            jax.ShapeDtypeStruct((8 * chunks, inner), F32),
            jax.ShapeDtypeStruct((state_size, inner), F32),
            jax.ShapeDtypeStruct((8, inner), F32),
            jax.ShapeDtypeStruct((width, packed), BF16),
            jax.ShapeDtypeStruct((8, width), F32),
        ],
        scratch_shapes=[
            pltpu.VMEM((STEP + 8, wide), F32),
            pltpu.VMEM((state_size, inner), F32),
            pltpu.VMEM((8, inner), F32),
        ],
        compiler_params=pltpu.CompilerParams(
            dimension_semantics=("arbitrary",), vmem_limit_bytes=VMEM_LIMIT
        ),
        cost_estimate=lasts(0.01),
        name="front",
    )(starts, hidden, edge, tok, cw, dtp, *shards)


def middle_kernel(
    u, rec, gate, st, pdx, sin, og, wo, prm,
    scan, dgate, sums, *parts,
):
    inner = gate.shape[1]
    pairs = inner // LANES
    d_gate = nn(og[...], wo[...])
    dgate[...] = d_gate
    act = silu(u[...])
    below = iota((CHUNK, CHUNK), 0) >= iota((CHUNK, CHUNK), 1)
    for i in range(SUB):
        rows = slice(i * CHUNK, (i + 1) * CHUNK)
        record = rec[rows, :]
        turned = record.T
        state = (st[i] + pdx[8 * i : 8 * i + 1, :] * sin[...]).astype(BF16)
        x = act[rows, :inner]
        input_b = act[rows, inner : inner + LANES].astype(BF16)
        input_c = act[rows, inner + LANES :].astype(BF16)
        scores = nt(input_c, input_b)
        barred = jnp.where(
            below & (record[:, SEG : SEG + 1] == turned[SEG : SEG + 1, :]), 0.0, NEGATIVE
        )
        entry = record[:, ENTRY : ENTRY + 1] * jnp.exp(record)
        outs = []
        for j in range(pairs):
            block = x[:, j * LANES : (j + 1) * LANES].astype(BF16)
            total = None
            for k, side in enumerate(halves(block)):
                h = 2 * j + k
                link = jnp.exp(record[:, h : h + 1] - turned[h : h + 1, :] + barred)
                weight = (scores * link * turned[8 + h : 9 + h, :]).astype(BF16)
                term = nn(weight, side)
                total = term if total is None else total + term
            outs.append(total)
        y = jnp.concatenate(outs, 1)
        y = y + nn(input_c, state) * spread(entry, pairs) + prm[0:1, :] * x
        scan[rows, :] = y
    gated = scan[...] * silu(gate[...])
    scaled = gated * prm[1:2, :]
    squares = jnp.sum(gated * gated, -1, keepdims=True)
    crosses = jnp.sum(scaled * d_gate, -1, keepdims=True)
    lane = iota((STEP, LANES), 1)
    both = jnp.where(lane == 0, squares, jnp.where(lane == 1, crosses, 0.0))
    sums[...] = both.T[0:8, :]
    part_low = nt(scaled.astype(BF16), wo[...]).astype(BF16)
    steps_each = pl.num_programs(0) // len(parts)
    for k, part in enumerate(parts):

        @pl.when(pl.program_id(0) // steps_each == k)
        def _():
            part[...] = part_low


def middle(u, rec, gate, st, pdx, sin, og, wo, prm):
    rows, inner = gate.shape
    width = og.shape[1]
    steps = rows // STEP
    each = steps // GROUPS

    def whole(a):
        return pl.BlockSpec(a.shape, lambda i: (0,) * a.ndim)

    def tall(cols):
        return pl.BlockSpec((STEP, cols), lambda i: (i, 0))

    def part(k):
        return pl.BlockSpec((STEP, width), lambda i: (jnp.clip(i - k * each, 0, each - 1), 0))

    return pl.pallas_call(
        middle_kernel,
        grid=(steps,),
        in_specs=[
            tall(u.shape[1]),
            tall(LANES),
            tall(inner),
            pl.BlockSpec((SUB,) + st.shape[1:], lambda i: (i, 0, 0)),
            pl.BlockSpec((8 * SUB, inner), lambda i: (i, 0)),
            whole(sin),
            tall(width),
            whole(wo),
            whole(prm),
        ],
        out_specs=[
            tall(inner),
            tall(inner),
            pl.BlockSpec((8, STEP), lambda i: (0, i)),
        ]
        + [part(k) for k in range(GROUPS)],
        out_shape=[
            jax.ShapeDtypeStruct((rows, inner), F32),
            jax.ShapeDtypeStruct((rows, inner), F32),
            jax.ShapeDtypeStruct((8, rows), F32),
        ]
        + [jax.ShapeDtypeStruct((rows // GROUPS, width), BF16)] * GROUPS,
        compiler_params=pltpu.CompilerParams(
            dimension_semantics=("arbitrary",), vmem_limit_bytes=VMEM_LIMIT
        ),
        cost_estimate=lasts(0.01),
        name="middle",
    )(u, rec, gate, st, pdx, sin, og, wo, prm)


def turn_kernel(
    inner_total, scan, gate, dgate, sums, upre_c, rec, prm,
    dscan, dgr, glow, adj, psx, fin, gain_grad,
    state, decay,
):
    inner = gate.shape[1]
    pairs = inner // LANES
    at = pl.program_id(0)

    @pl.when(at == 0)
    def _():
        state[...] = jnp.zeros_like(state)
        decay[...] = jnp.ones_like(decay)
        gain_grad[...] = jnp.zeros_like(gain_grad)

    head = sums[...]
    column = jnp.concatenate([head, jnp.zeros((LANES - 8, STEP), F32)], 0).T
    inv = lax.rsqrt(column[:, 0:1] / inner_total + EPSILON)
    cube = inv * inv * inv * (column[:, 1:2] / inner_total)
    raw = gate[...]
    sig = jax.nn.sigmoid(raw)
    sil = raw * sig
    y = scan[...]
    gated = y * sil
    unit = gated * inv
    d_gate = dgate[...]
    gain = prm[1:2, :]
    glow[...] = (unit * gain).astype(BF16)
    gain_grad[...] += jnp.broadcast_to(jnp.sum(d_gate * unit, 0, keepdims=True), gain_grad.shape)
    d_gated = inv * gain * d_gate - gated * cube
    d_scan = d_gated * sil
    dscan[...] = d_scan
    dgr[...] = (d_gated * y * (sig * (1.0 + raw * (1.0 - sig)))).astype(BF16)
    input_c = silu(upre_c[...])
    for i in reversed(range(SUB)):
        rows = slice(i * CHUNK, (i + 1) * CHUNK)
        record = rec[rows, :]
        entry = record[:, ENTRY : ENTRY + 1] * jnp.exp(record)
        adj[i] = state[...]
        psx[8 * i : 8 * i + 8, :] = decay[...]
        passed = spread(entry[CHUNK - 1 :, :], pairs)
        fed = (d_scan[rows] * spread(entry, pairs)).astype(BF16)
        state[...] = passed * state[...] + nn(input_c[rows].T.astype(BF16), fed)
        decay[...] = decay[...] * passed
    fin[...] = state[...]


def turn(scan, gate, dgate, sums, u, rec, prm, inner_total):
    rows, inner = scan.shape
    steps = rows // STEP
    chunks = rows // CHUNK
    state_size = LANES
    c_block = u.shape[1] // LANES - 1

    def whole(a):
        return pl.BlockSpec(a.shape, lambda i: (0,) * a.ndim)

    def tall(cols):
        return pl.BlockSpec((STEP, cols), lambda i: (steps - 1 - i, 0))

    return pl.pallas_call(
        functools.partial(turn_kernel, float(inner_total)),
        grid=(steps,),
        in_specs=[
            tall(inner),
            tall(inner),
            tall(inner),
            pl.BlockSpec((8, STEP), lambda i: (0, steps - 1 - i)),
            pl.BlockSpec((STEP, LANES), lambda i: (steps - 1 - i, c_block)),
            tall(LANES),
            whole(prm),
        ],
        out_specs=[
            tall(inner),
            tall(inner),
            tall(inner),
            pl.BlockSpec((SUB, state_size, inner), lambda i: (steps - 1 - i, 0, 0)),
            pl.BlockSpec((8 * SUB, inner), lambda i: (steps - 1 - i, 0)),
            pl.BlockSpec((state_size, inner), lambda i: (0, 0)),
            pl.BlockSpec((8, inner), lambda i: (0, 0)),
        ],
        out_shape=[
            jax.ShapeDtypeStruct((rows, inner), F32),
            jax.ShapeDtypeStruct((rows, inner), BF16),
            jax.ShapeDtypeStruct((rows, inner), BF16),
            jax.ShapeDtypeStruct((chunks, state_size, inner), F32),
            jax.ShapeDtypeStruct((8 * chunks, inner), F32),
            jax.ShapeDtypeStruct((state_size, inner), F32),
            jax.ShapeDtypeStruct((8, inner), F32),
        ],
        scratch_shapes=[pltpu.VMEM((state_size, inner), F32), pltpu.VMEM((8, inner), F32)],
        compiler_params=pltpu.CompilerParams(
            dimension_semantics=("arbitrary",), vmem_limit_bytes=VMEM_LIMIT
        ),
        cost_estimate=lasts(0.01),
        name="turn",
    )(scan, gate, dgate, sums, u, rec, prm)


def back_kernel(
    u, rec, dscan, st, pdx, sin, adj, psx, ain, prm, dtp,
    dpre, dstep, skip_acc, head_acc,
):
    inner = dscan.shape[1]
    pairs = inner // LANES
    heads = 2 * pairs

    @pl.when(pl.program_id(0) == 0)
    def _():
        skip_acc[...] = jnp.zeros_like(skip_acc)
        head_acc[...] = jnp.zeros_like(head_acc)

    raw = u[...]
    sig = jax.nn.sigmoid(raw)
    act = raw * sig
    slope = sig * (1.0 + raw * (1.0 - sig))
    above = iota((CHUNK, CHUNK), 0) <= iota((CHUNK, CHUNK), 1)
    upper = above.astype(F32)
    lane = iota((CHUNK, LANES), 1)
    gather_heads = (iota((inner, LANES), 0) // (LANES // 2) == iota((inner, LANES), 1)).astype(BF16)
    nega = dtp[1:2, :]
    for i in range(SUB):
        rows = slice(i * CHUNK, (i + 1) * CHUNK)
        record = rec[rows, :]
        turned = record.T
        state = st[i] + pdx[8 * i : 8 * i + 1, :] * sin[...]
        state_low = state.astype(BF16)
        later = adj[i] + psx[8 * i : 8 * i + 1, :] * ain[...]
        later_low = later.astype(BF16)
        x = act[rows, :inner]
        b_wide = act[rows, inner : inner + LANES]
        c_wide = act[rows, inner + LANES :]
        input_b = b_wide.astype(BF16)
        input_c = c_wide.astype(BF16)
        dy = dscan[rows, :]
        scores = nt(input_b, input_c)
        barred = jnp.where(
            above & (record[:, SEG : SEG + 1] == turned[SEG : SEG + 1, :]), 0.0, NEGATIVE
        )
        step = pltpu.roll(record, LANES - 8, axis=1)
        z = pltpu.roll(record, LANES - RAW, axis=1)
        d_scores = jnp.zeros((CHUNK, CHUNK), F32)
        direct = jnp.zeros((CHUNK, LANES), F32)
        arrivals = []
        dxs = []
        for j in range(pairs):
            cols = slice(j * LANES, (j + 1) * LANES)
            x_sides = halves(x[:, cols].astype(BF16))
            dy_pair = dy[:, cols].astype(BF16)
            dy_sides = halves(dy_pair)
            total = None
            for k in range(2):
                h = 2 * j + k
                step_col = record[:, 8 + h : 9 + h]
                link = jnp.exp(turned[h : h + 1, :] - record[:, h : h + 1] + barred)
                d_link = nt(x_sides[k], dy_pair) * link
                d_scaled = d_link * step_col
                d_scores = d_scores + d_scaled
                flow = d_scaled * scores
                arrivals.append(jnp.sum(flow, 0, keepdims=True))
                given = jnp.sum(d_link * scores, 1, keepdims=True)
                direct = jnp.where(lane == h, given, direct)
                weight = (scores * link * step_col).astype(BF16)
                term = nn(weight, dy_sides[k])
                total = term if total is None else total + term
            dxs.append(total)
        dx = jnp.concatenate(dxs, 1)
        arrived = jnp.concatenate(arrivals + [jnp.zeros((CHUNK - heads, CHUNK), F32)], 0).T
        decay_in = record[:, ENTRY : ENTRY + 1] * jnp.exp(record)
        last = record[CHUNK - 1 :, :]
        tail_exp = record[:, TAIL : TAIL + 1] * jnp.exp(last - record)
        tail = tail_exp * step
        tail_wide = spread(jnp.where(lane < 8, tail, 0.0), pairs)
        fed_back = (dy * spread(decay_in, pairs)).astype(BF16)
        fed = (x * tail_wide).astype(BF16)
        from_state = nn(input_c, state_low)
        d_fed = nn(input_b, later_low)
        d_score_low = d_scores.astype(BF16)
        d_c = nt(fed_back, state_low) + nn(d_scores.T.astype(BF16), input_b)
        d_b = nt(fed, later_low) + nn(d_score_low, input_c)
        d_entry = nn((dy * from_state).astype(BF16), gather_heads)
        d_tail = nn((x * d_fed).astype(BF16), gather_heads)
        through = jnp.broadcast_to(jnp.sum(later * state, 0, keepdims=True), (16, inner))
        d_through = nn(through.astype(BF16), gather_heads)[0:1, :]
        dx = dx + d_fed * tail_wide + prm[0:1, :] * dy
        tail_flow = d_tail * tail
        d_cum = arrived - direct * step + d_entry * decay_in - tail_flow
        d_cum = jnp.where(lane < 8, d_cum, 0.0)
        d_last = jnp.sum(tail_flow, 0, keepdims=True) + decay_in[CHUNK - 1 :, :] * d_through
        d_rate = exact(upper, d_cum) + jnp.where(lane < 8, d_last, 0.0)
        d_step = direct + d_tail * tail_exp + nega * d_rate
        d_z = jnp.where(lane < 8, d_step * jax.nn.sigmoid(z), 0.0)
        dstep[rows, :] = d_z.astype(BF16)
        dpre[rows, :] = jnp.concatenate([dx, d_b, d_c], 1) * slope[rows]
        skip_acc[...] += jnp.broadcast_to(jnp.sum(dy * x, 0, keepdims=True), skip_acc.shape)
        head_acc[0:1, :] += jnp.sum(d_z, 0, keepdims=True)
        head_acc[1:2, :] += jnp.sum(
            jnp.where(lane < 8, d_rate * (nega * step), 0.0), 0, keepdims=True
        )


def back(u, rec, dscan, st, pdx, sin, adj, psx, ain, prm, dtp, after, group):
    rows, wide = u.shape
    inner = dscan.shape[1]
    steps = rows // STEP // GROUPS
    first = group * steps

    def whole(a):
        return pl.BlockSpec(a.shape, lambda i: (0,) * a.ndim)

    def tall(cols):
        return pl.BlockSpec((STEP, cols), lambda i: (first + i, 0))

    def out_tall(cols):
        return pl.BlockSpec((STEP, cols), lambda i: (i, 0))

    def states(at):
        return pl.BlockSpec((SUB,) + st.shape[1:], lambda i: (at + i, 0, 0))

    def decays(at):
        return pl.BlockSpec((8 * SUB, inner), lambda i: (at + i, 0))

    return pl.pallas_call(
        ordered(back_kernel, 11, len(after)),
        grid=(steps,),
        in_specs=[
            tall(wide),
            tall(LANES),
            tall(inner),
            states(first),
            decays(first),
            whole(sin),
            states(first),
            decays(first),
            whole(ain),
            whole(prm),
            whole(dtp),
        ]
        + [ANYWHERE] * len(after),
        out_specs=[
            out_tall(wide),
            out_tall(LANES),
            pl.BlockSpec((8, inner), lambda i: (0, 0)),
            pl.BlockSpec((8, LANES), lambda i: (0, 0)),
        ],
        out_shape=[
            jax.ShapeDtypeStruct((steps * STEP, wide), F32),
            jax.ShapeDtypeStruct((steps * STEP, LANES), BF16),
            jax.ShapeDtypeStruct((8, inner), F32),
            jax.ShapeDtypeStruct((8, LANES), F32),
        ],
        compiler_params=pltpu.CompilerParams(
            dimension_semantics=("arbitrary",), vmem_limit_bytes=VMEM_LIMIT
        ),
        cost_estimate=lasts(0.01),
        name="back",
    )(u, rec, dscan, st, pdx, sin, adj, psx, ain, prm, dtp, *after)


def rear_kernel(
    dpre, rec, pre, dgr, dstep, follow, w, cw,
    dproj, dnorm, conv_acc,
    buf, mbuf,
):
    wide = dpre.shape[1]
    inner = dgr.shape[1]

    @pl.when(pl.program_id(0) == 0)
    def _():
        buf[STEP : STEP + 8, :] = follow[:, :wide]
        mbuf[STEP : STEP + 8, :] = follow[:, wide:]
        conv_acc[...] = jnp.zeros_like(conv_acc)

    @pl.when(pl.program_id(0) > 0)
    def _():
        buf[STEP : STEP + 8, :] = buf[0:8, :]
        mbuf[STEP : STEP + 8, :] = mbuf[0:8, :]

    grad = dpre[...]
    buf[0:STEP, :] = grad
    mbuf[0:STEP, :] = rec[...]
    value = pre[...]
    total = cw[3:4, :] * grad
    conv_acc[3:4, :] += jnp.sum(value * grad, 0, keepdims=True)
    conv_acc[4:5, :] += jnp.sum(grad, 0, keepdims=True)
    for shift in (1, 2, 3):
        mark = mbuf[shift : shift + STEP, :][:, M1 + shift - 1 : M1 + shift]
        moved = buf[shift : shift + STEP, :] * mark
        total = total + cw[3 - shift : 4 - shift, :] * moved
        conv_acc[3 - shift : 4 - shift, :] += jnp.sum(value * moved, 0, keepdims=True)
    dproj[:, :inner] = dgr[...]
    dproj[:, inner : inner + wide] = total.astype(BF16)
    dproj[:, inner + wide :] = dstep[...]
    dnorm[...] = nt(dproj[...], w[...]).astype(BF16)


def rear(dpre, rec, pre, dgr, dstep, follow, w, cw, after, group):
    rows, wide = dpre.shape
    steps = rows // STEP
    inner = dgr.shape[1]
    width, packed = w.shape
    first = group * steps

    def whole(a):
        return pl.BlockSpec(a.shape, lambda i: (0,) * a.ndim)

    def tall(cols):
        return pl.BlockSpec((STEP, cols), lambda i: (first + steps - 1 - i, 0))

    def own(cols):
        return pl.BlockSpec((STEP, cols), lambda i: (steps - 1 - i, 0))

    return pl.pallas_call(
        ordered(rear_kernel, 8, len(after)),
        grid=(steps,),
        in_specs=[
            own(wide),
            tall(LANES),
            tall(wide),
            tall(inner),
            own(LANES),
            whole(follow),
            whole(w),
            whole(cw),
        ]
        + [ANYWHERE] * len(after),
        out_specs=[
            own(packed),
            own(width),
            pl.BlockSpec((8, wide), lambda i: (0, 0)),
        ],
        out_shape=[
            jax.ShapeDtypeStruct((rows, packed), BF16),
            jax.ShapeDtypeStruct((rows, width), BF16),
            jax.ShapeDtypeStruct((8, wide), F32),
        ],
        scratch_shapes=[
            pltpu.VMEM((STEP + 8, wide), F32),
            pltpu.VMEM((STEP + 8, LANES), F32),
        ],
        compiler_params=pltpu.CompilerParams(
            dimension_semantics=("arbitrary",), vmem_limit_bytes=VMEM_LIMIT
        ),
        cost_estimate=lasts(0.01),
        name="rear",
    )(dpre, rec, pre, dgr, dstep, follow, w, cw, *after)


def settle_kernel(inner_total, hid, sums, given, held, outer, filled, out):
    column = jnp.concatenate([sums[...], jnp.zeros((LANES - 8, STEP), F32)], 0).T
    inv = lax.rsqrt(column[:, 0:1] / inner_total + EPSILON)
    total = jnp.where(outer[0:1, 0:1] > 0.0, given[...].astype(F32), held[...].astype(F32))
    out[...] = (hid[...].astype(F32) + inv * total).astype(BF16)


def finish_kernel(hid, cot, gain, given, held, outer, filled, out):
    x = hid[...].astype(F32)
    inv = lax.rsqrt(jnp.mean(x * x, -1, keepdims=True) + EPSILON)
    total = jnp.where(outer[0:1, 0:1] > 0.0, given[...].astype(F32), held[...].astype(F32))
    scaled = total * gain[0:1, :]
    cross = jnp.mean(scaled * x, -1, keepdims=True)
    out[...] = cot[...].astype(F32) + inv * scaled - x * (inv * inv * inv * cross)


def by_group(kernel, out_like, dtype, group, fresh, operands, filled, after, name):
    rows, width = out_like.shape
    steps = rows // GROUPS // STEP
    first = group * steps
    specs = {
        "all": lambda a: pl.BlockSpec((STEP, a.shape[1]), lambda i: (first + i, 0)),
        "group": lambda a: pl.BlockSpec((STEP, a.shape[1]), lambda i: (i, 0)),
        "columns": lambda a: pl.BlockSpec((8, STEP), lambda i: (0, first + i)),
        "whole": lambda a: pl.BlockSpec(a.shape, lambda i: (0, 0)),
    }
    count = len(operands) + 1
    return pl.pallas_call(
        ordered(kernel, count, len(after)),
        grid=(steps,),
        in_specs=[specs[kind](a) for a, kind in operands] + [ANYWHERE] * (1 + len(after)),
        out_specs=pl.BlockSpec((STEP, width), lambda i: (first + i, 0)),
        out_shape=jax.ShapeDtypeStruct((rows, width), dtype),
        input_output_aliases={} if fresh else {count - 1: 0},
        compiler_params=pltpu.CompilerParams(
            dimension_semantics=("arbitrary",), vmem_limit_bytes=VMEM_LIMIT
        ),
        cost_estimate=lasts(0.01),
        name=name,
    )(*[a for a, _ in operands], filled, *after)


def passed_along(value, axis, steps):
    count = lax.axis_size(axis)
    leading, last = (max(0, -steps), min(count, count - steps))
    return lax.ppermute(value, axis, [(source, source + steps) for source in range(leading, last)])


def chained(own, decay, axis, steps):
    entering = jnp.zeros_like(own)
    for turn_at in range(lax.axis_size(axis) - 1):
        leaving = own if turn_at == 0 else own + decay * entering
        entering = passed_along(leaving, axis, steps)
    return entering


def butterfly_sum(value, axis):
    bit = 1
    while bit < lax.axis_size(axis):
        pairs = [(i, i ^ bit) for i in range(lax.axis_size(axis))]
        value = value + lax.ppermute(value, axis, pairs)
        bit *= 2
    return value


def join_kernel(pairs, *refs):
    outs = refs[2 * pairs :]
    for k in range(pairs):
        left, right, out = refs[2 * k], refs[2 * k + 1], outs[k]
        out[...] = (left[...].astype(F32) + right[...].astype(F32)).astype(out.dtype)


def join(pairs, after, held=()):
    rows, width = pairs[0][0].shape
    spec = pl.BlockSpec((STEP, width), lambda i: (i, 0))
    return pl.pallas_call(
        ordered(
            functools.partial(join_kernel, len(pairs)), 2 * len(pairs), len(after) + len(held)
        ),
        grid=(rows // STEP,),
        in_specs=[spec] * (2 * len(pairs)) + [ANYWHERE] * (len(after) + len(held)),
        out_specs=[spec] * len(pairs) + [ANYWHERE] * len(held),
        out_shape=[jax.ShapeDtypeStruct((rows, width), BF16)] * len(pairs)
        + [jax.ShapeDtypeStruct(a.shape, a.dtype) for a in held],
        input_output_aliases={
            2 * len(pairs) + len(after) + k: len(pairs) + k for k in range(len(held))
        },
        compiler_params=pltpu.CompilerParams(
            dimension_semantics=("arbitrary",), vmem_limit_bytes=VMEM_LIMIT
        ),
        cost_estimate=lasts(0.01),
        name="join",
    )(*[a for pair in pairs for a in pair], *after, *held)


class LineSum:
    def __init__(self, value):
        self.own = value
        self.come = lax.ppermute(value, "tp", [(0, 1), (3, 2)])
        self.near = self.across = self.given = None

    def pair(self):
        return (self.own if self.near is None else self.near, self.come)

    def joined(self, value):
        if self.near is None:
            self.near = value
            self.come = lax.ppermute(value, "tp", [(1, 2), (2, 1)])
        else:
            self.across = value
            self.given = lax.ppermute(value, "tp", [(1, 0), (2, 3)])


def advance(sums, after, held=()):
    outs = join([one.pair() for one in sums], after, held)
    for one, value in zip(sums, outs):
        one.joined(value)
    return tuple(outs)


def total_kernel(own, one, two, three, *refs):
    out = refs[len(refs) // 2]
    out[...] = (own[...] + one[...]) + (two[...] + three[...])


def total_over_row(own, held):
    others = [lax.ppermute(own, "tp", [(i, i ^ bits) for i in range(4)]) for bits in (1, 2, 3)]
    spec = pl.BlockSpec(own.shape, lambda i: (0, 0))
    return pl.pallas_call(
        total_kernel,
        grid=(1,),
        in_specs=[spec] * 4 + [ANYWHERE] * len(held),
        out_specs=[spec] + [ANYWHERE] * len(held),
        out_shape=[jax.ShapeDtypeStruct(own.shape, own.dtype)]
        + [jax.ShapeDtypeStruct(a.shape, a.dtype) for a in held],
        input_output_aliases={4 + k: 1 + k for k in range(len(held))},
        cost_estimate=lasts(0.01),
        name="total",
    )(own, *others, *held)


def other_core_kernel(place, w, wo, out):
    packed = w.shape[1]
    out[:, :packed] = w[...].astype(BF16)
    out[:, packed:] = wo[...].astype(BF16)


def split_kernel(
    place, w_ka, w_sa, w_kb, w_sb, wo_kb, wo_sb, r_ka, r_sa, r_kb, r_sb,
    keep_a, send_a, keep_b, send_b,
):
    cut, packed = keep_a.shape[1], w_ka.shape[1]
    keep_a[...] = w_ka[:, :cut] + r_ka[:, :cut].astype(F32)
    send_a[...] = (w_sa[:, :cut] + r_sa[:, :cut].astype(F32)).astype(BF16)
    for w, wo, r, out in ((w_kb, wo_kb, r_kb, keep_b), (w_sb, wo_sb, r_sb, send_b)):
        out[:, : packed - cut] = (w[:, cut:] + r[:, cut:packed].astype(F32)).astype(out.dtype)
        out[:, packed - cut :] = (wo[...] + r[:, packed:].astype(F32)).astype(out.dtype)


def second_kernel(place, ka, ra, sa, rsa, kb, rb, sb, rsb, keep_a, send_a, keep_b, send_b):
    keep_a[...] = ka[...] + ra[...].astype(F32)
    send_a[...] = (sa[...] + rsa[...].astype(F32)).astype(BF16)
    keep_b[...] = kb[...] + rb[...].astype(F32)
    send_b[...] = (sb[...] + rsb[...].astype(F32)).astype(BF16)


def placed_call(kernel, steps, place, inputs, outputs, name, after=()):
    return pl.pallas_call(
        ordered(kernel, 1 + len(inputs), len(after)),
        grid_spec=pltpu.PrefetchScalarGridSpec(
            num_scalar_prefetch=1,
            grid=(steps,),
            in_specs=[
                pl.BlockSpec((LANES, a.shape[1]), functools.partial(lambda f, i, p: (f(i, p), 0), f))
                for a, f in inputs
            ]
            + [ANYWHERE] * len(after),
            out_specs=[pl.BlockSpec((LANES, cols), lambda i, p: (i, 0)) for cols, _ in outputs],
        ),
        out_shape=[jax.ShapeDtypeStruct((steps * LANES, cols), kind) for cols, kind in outputs],
        compiler_params=pltpu.CompilerParams(
            dimension_semantics=("arbitrary",), vmem_limit_bytes=VMEM_LIMIT
        ),
        cost_estimate=lasts(0.01),
        name=name,
    )(place, *[a for a, _ in inputs], *after)


def to_owners(w, wo):
    after = yield
    packed, extra = w.shape[1], wo.shape[1]
    if lax.axis_size("fsdp") != 4 or lax.axis_size("ctx") != 2 or w.shape[0] != 8 * LANES:
        both = jnp.concatenate([w, wo], 1)
        summed = lax.psum_scatter(both, ("fsdp", "ctx"), scatter_dimension=0, tiled=True)
        yield w
        yield w
        yield w
        yield summed
        return

    def swapped(value, axis, bit):
        count = lax.axis_size(axis)
        return lax.ppermute(value, axis, [(i, i ^ bit) for i in range(count)])

    fsdp = lax.axis_index("fsdp")
    place = jnp.stack([fsdp % 2, fsdp // 2, lax.axis_index("ctx")]).astype(jnp.int32)
    cut = 1024
    rest = packed + extra - cut

    (sent,) = placed_call(
        other_core_kernel, 4, place,
        [(w, lambda i, p: 2 * i + 1 - p[2]), (wo, lambda i, p: 2 * i + 1 - p[2])],
        [(packed + extra, BF16)], "other_core", after,
    )
    come = swapped(sent, "ctx", 1)
    after = yield sent
    of = {
        "ka": lambda i, p: 2 * i + p[0],
        "sa": lambda i, p: 2 * i + 1 - p[0],
        "kb": lambda i, p: 2 * p[1] + i,
        "sb": lambda i, p: 2 * (1 - p[1]) + i,
    }

    def own(key):
        return lambda i, p: 2 * of[key](i, p) + p[2]

    keep_a, send_a, keep_b, send_b = placed_call(
        split_kernel, 2, place,
        [(w, own(key)) for key in ("ka", "sa", "kb", "sb")]
        + [(wo, own(key)) for key in ("kb", "sb")]
        + [(come, of[key]) for key in ("ka", "sa", "kb", "sb")],
        [(cut, F32), (cut, BF16), (rest, F32), (rest, BF16)], "split", after,
    )
    come_a, come_b = swapped(send_a, "fsdp", 1), swapped(send_b, "fsdp", 2)
    after = yield send_a
    y, not_y = (lambda i, p: p[1]), (lambda i, p: 1 - p[1])
    x, not_x = (lambda i, p: p[0]), (lambda i, p: 1 - p[0])
    keep_a, send_a, keep_b, send_b = placed_call(
        second_kernel, 1, place,
        [(keep_a, y), (come_a, y), (keep_a, not_y), (come_a, not_y)]
        + [(keep_b, x), (come_b, x), (keep_b, not_x), (come_b, not_x)],
        [(cut, F32), (cut, BF16), (rest, F32), (rest, BF16)], "second", after,
    )
    come_a, come_b = swapped(send_a, "fsdp", 2), swapped(send_b, "fsdp", 1)
    yield send_a
    yield jnp.concatenate([keep_a + come_a.astype(F32), keep_b + come_b.astype(F32)], 1)


def flip_kernel(value, out):
    out[...] = value[...].astype(F32).T.astype(out.dtype)


def flipped(value, after):
    rows, cols = value.shape
    return pl.pallas_call(
        ordered(flip_kernel, 1, len(after)),
        grid=(1,),
        in_specs=[pl.BlockSpec((rows, cols), lambda i: (0, 0))] + [ANYWHERE] * len(after),
        out_specs=pl.BlockSpec((cols, rows), lambda i: (0, 0)),
        out_shape=jax.ShapeDtypeStruct((cols, rows), value.dtype),
        cost_estimate=lasts(0.01),
        name="flip",
    )(value, *after)


def gathered_shards(own):
    rows = own.shape[0]
    if lax.axis_size("fsdp") != 4 or lax.axis_size("ctx") != 2:
        return [lax.all_gather(own, ("fsdp", "ctx"), axis=0, tiled=True)], [0]

    def swapped(value, axis, bit):
        count = lax.axis_size(axis)
        return lax.ppermute(value, axis, [(i, i ^ bit) for i in range(count)])

    half = rows // 2
    by_one, by_two = swapped(own, "fsdp", 1), swapped(own, "fsdp", 2)
    upper = swapped(by_two[:half], "fsdp", 1)
    under = swapped(by_one[half:], "fsdp", 2)
    mine = [own, by_one, by_two, upper, under]
    place = lax.axis_index("fsdp")
    core = lax.axis_index("ctx")
    shards, starts = [], []
    for other in (0, 1):
        for value, bits, offset in zip(mine, (0, 1, 2, 3, 3), (0, 0, 0, 0, half)):
            shards.append(swapped(value, "ctx", 1) if other else value)
            starts.append(((place ^ bits) * 2 + (core ^ other)) * rows + offset)
    return shards, starts


def token_marks(segment, before):
    rows = segment.shape[0]
    joined = jnp.concatenate([before, segment])
    marks = [joined[3 - j : 3 - j + rows] == segment for j in (1, 2, 3)]
    blocks = segment.reshape(-1, CHUNK)
    previous = jnp.concatenate([before[2:], blocks[:-1, -1]])
    marks.append((blocks == previous[:, None]).reshape(-1))
    marks.append((blocks == blocks[:, -1:]).reshape(-1))
    marks.append(segment)
    table = jnp.stack([mark.astype(F32) for mark in marks], 1)
    return jnp.pad(table, ((0, 0), (M1, LANES - M1 - len(marks))))


def body(
    hidden, segments, out_grad, norm_gain, w_zx, w_dt, w_bc, conv_x_w, conv_x_b,
    conv_bc_w, conv_bc_b, dt_bias, a_log, skip_d, out_gain, w_out,
):
    _, rows, width = hidden.shape
    inner = w_zx.shape[2]
    heads = w_dt.shape[1]
    head_size = inner // heads
    state_size = w_bc.shape[2]
    wide = inner + 2 * state_size
    taps = conv_x_w.shape[0]
    owned = w_zx.shape[0]
    shards = ("fsdp", "ctx")
    hid = hidden[0]
    cot = out_grad[0]
    segment = segments[0]

    packed = jnp.concatenate(
        [
            w_zx.reshape(owned, 2 * inner),
            w_bc.reshape(owned, 2 * state_size),
            w_dt, w_dt, w_dt, w_dt,
            norm_gain[:, None],
            jnp.zeros((owned, LANES - 4 * heads - 1), BF16),
        ],
        1,
    )
    w_shards, w_starts = gathered_shards(packed)
    w_starts = jnp.stack([jnp.asarray(start, jnp.int32) for start in w_starts])
    wo = lax.all_gather(
        flipped(w_out, tuple(w_shards[3:5])), shards, axis=0, tiled=True
    )

    edge, edge_segment = passed_along((hid[rows - EDGE :], segment[rows - 3 :]), "ctx", 1)
    tok = token_marks(segment, edge_segment)
    conv_rows = jnp.concatenate(
        [
            jnp.concatenate([conv_x_w, conv_bc_w.reshape(taps, -1)], 1),
            jnp.concatenate([conv_x_b, conv_bc_b.reshape(-1)])[None],
            jnp.zeros((8 - taps - 1, wide), F32),
        ],
        0,
    )
    spare = jnp.zeros((LANES - 4 * heads,), F32)
    rate = -jnp.exp(a_log)
    dtp = jnp.concatenate(
        [
            jnp.concatenate([dt_bias] * 4 + [spare])[None],
            jnp.concatenate([rate] * 4 + [spare])[None],
            jnp.zeros((6, LANES), F32),
        ],
        0,
    )
    prm = jnp.concatenate(
        [jnp.repeat(skip_d, head_size)[None], out_gain[None], jnp.zeros((6, inner), F32)], 0
    )

    normed, gate, pre, u, rec, st, pdx, state_end, decay_end, w_in, gain = front(
        hid, edge, tok, w_shards, w_starts, 4 * heads, conv_rows, dtp, inner, wide
    )
    sin = chained(state_end, decay_end[:1], "ctx", 1)
    inner_total = inner * lax.axis_size("tp")
    me = lax.axis_index("tp")
    outer = jnp.full((8, LANES), (me == 0) | (me == lax.axis_size("tp") - 1), F32)

    scan, dgate, sums, *parts = middle(u, rec, gate, st, pdx, sin, cot, wo, prm)
    sums, *parts = total_over_row(sums, parts)
    out_sums = [LineSum(part) for part in parts]
    dscan, dgr, glow, adj, psx, adj_start, out_gain_acc = turn(
        scan, gate, dgate, sums, u, rec, prm, inner_total
    )
    ain = chained(adj_start, decay_end[:1], "ctx", -1)
    contract_rows = (((0,), (0,)), ((), ()))
    wo_grad = lax.dot_general(cot, glow, contract_rows, preferred_element_type=F32)

    group_rows = rows // GROUPS
    backs = [None] * GROUPS
    rears = [None] * GROUPS
    d_normed = [None] * GROUPS
    follows = [None] * GROUPS

    def run_back(group, after):
        backs[group] = back(u, rec, dscan, st, pdx, sin, adj, psx, ain, prm, dtp, after, group)
        start = jnp.concatenate(
            [backs[group][0][:8], rec[group * group_rows : group * group_rows + 8]], 1
        )
        if group == 0:
            follows[GROUPS - 1] = passed_along(start, "ctx", -1)
        else:
            follows[group - 1] = start

    def run_rear(group, after):
        rears[group] = rear(
            backs[group][0], rec, pre, dgr, backs[group][1], follows[group], w_in,
            conv_rows, after, group,
        )
        d_normed[group] = LineSum(rears[group][1])

    def settle(group, filled, after=()):
        total = out_sums[group]
        return by_group(
            functools.partial(settle_kernel, float(inner_total)), hid, BF16, group, filled is None,
            [
                (hid, "all"),
                (sums, "columns"),
                (total.given, "group"),
                (total.across, "group"),
                (outer, "whole"),
            ],
            outer if filled is None else filled, after, "settle",
        )

    def finish(group, filled, after):
        total = d_normed[group]
        return by_group(
            finish_kernel, hid, F32, group, filled is None,
            [
                (hid, "all"),
                (cot, "all"),
                (gain, "whole"),
                (total.given, "group"),
                (total.across, "group"),
                (outer, "whole"),
            ],
            outer if filled is None else filled, after, "finish",
        )

    sum_a, sum_b, sum_c, sum_d = out_sums
    done = advance([sum_a], (wo_grad,))
    run_back(0, done)
    done = advance([sum_b, sum_a], (backs[0][3],))
    run_back(1, done)
    run_rear(0, (backs[1][3],))
    done = advance([sum_c, sum_b], (rears[0][2],))
    block_out = settle(0, None, done)
    run_back(2, (block_out,))
    run_rear(1, (backs[2][3],))
    done = advance([sum_d, sum_c], (rears[1][2],))
    block_out = settle(1, block_out, done)
    run_back(3, (block_out,))
    run_rear(2, (backs[3][3],))
    done = advance([d_normed[0], sum_d], (rears[2][2],))
    block_out = settle(2, block_out, done)
    run_rear(3, (block_out,))
    *done, last_dproj = advance(
        [d_normed[1], d_normed[0]], (rears[3][2],), (rears[3][0],)
    )

    conv_acc = sum(r[2] for r in rears)
    skip_acc = sum(b[2][0] for b in backs)
    head_acc = sum(b[3] for b in backs)

    dproj = jnp.concatenate([r[0] for r in rears[:-1]] + [last_dproj], 0)
    w_grad = lax.dot_general(normed, dproj, contract_rows, preferred_element_type=F32)
    owners = to_owners(w_grad, wo_grad)
    next(owners)
    done = advance([d_normed[2]], (w_grad[:8, :LANES],))
    block_out = settle(3, block_out, done)
    done = advance([d_normed[1]], (block_out,))
    hidden_grad = finish(0, None, done)
    owners.send((hidden_grad,))
    done = advance([d_normed[3], d_normed[2]], (hidden_grad,))
    owners.send(done)
    hidden_grad = finish(1, hidden_grad, done)
    done = advance([d_normed[3]], (hidden_grad,))
    owners.send(done)
    both_owned = next(owners)
    for group in range(2, GROUPS):
        hidden_grad = finish(group, hidden_grad, done)
    w_owned, wo_owned = both_owned[:, : w_grad.shape[1]], both_owned[:, w_grad.shape[1] :]

    small = jnp.concatenate(
        [
            conv_acc[: taps + 1].reshape(-1),
            out_gain_acc[0],
            skip_acc,
            head_acc[:2].reshape(-1),
        ]
    )
    small = butterfly_sum(butterfly_sum(small, "ctx"), "fsdp")
    conv_sum = small[: (taps + 1) * wide].reshape(taps + 1, wide)
    rest = small[(taps + 1) * wide :]
    shared = jnp.concatenate(
        [
            w_owned[:, 2 * inner : 2 * inner + 2 * state_size].reshape(-1),
            jnp.sum(packed.astype(F32) * w_owned, 1),
            conv_sum[:, inner:].reshape(-1),
        ]
    )
    shared = butterfly_sum(shared, "tp")
    bc_size = owned * 2 * state_size
    bc_owned = shared[:bc_size].reshape(owned, 2, state_size)
    gain_owned = shared[bc_size : bc_size + owned] / norm_gain.astype(F32)
    conv_bc = shared[bc_size + owned :].reshape(taps + 1, 2, state_size)

    return (
        block_out[None],
        hidden_grad[None],
        gain_owned,
        w_owned[:, : 2 * inner].reshape(owned, 2, inner),
        w_owned[:, 2 * inner + 2 * state_size : 2 * inner + 2 * state_size + heads],
        bc_owned,
        conv_sum[:taps, :inner],
        conv_sum[taps, :inner],
        conv_bc[:taps],
        conv_bc[taps],
        rest[2 * inner : 2 * inner + heads],
        rest[2 * inner + LANES : 2 * inner + LANES + heads],
        jnp.sum(rest[inner : 2 * inner].reshape(heads, head_size), 1),
        rest[:inner],
        wo_owned.T,
    )


def solution(mesh):
    placed = (
        P("fsdp", "ctx", None),
        P("fsdp", "ctx"),
        P("fsdp", "ctx", None),
        P(("fsdp", "ctx")),
        P(("fsdp", "ctx"), None, "tp"),
        P(("fsdp", "ctx"), "tp"),
        P(("fsdp", "ctx"), None, None),
        P(None, "tp"),
        P("tp"),
        P(),
        P(),
        P("tp"),
        P("tp"),
        P("tp"),
        P("tp"),
        P("tp", ("fsdp", "ctx")),
    )
    return jax.shard_map(
        body,
        mesh=mesh,
        in_specs=placed,
        out_specs=(
            P("fsdp", "ctx", None),
            P("fsdp", "ctx", None),
            P(("fsdp", "ctx")),
            P(("fsdp", "ctx"), None, "tp"),
            P(("fsdp", "ctx"), "tp"),
            P(("fsdp", "ctx"), None, None),
            P(None, "tp"),
            P("tp"),
            P(),
            P(),
            P("tp"),
            P("tp"),
            P("tp"),
            P("tp"),
            P("tp", ("fsdp", "ctx")),
        ),
        check_vma=False,
    )
```

```python
import functools

import jax
import jax.numpy as jnp
from jax import lax
from jax.experimental import pallas as pl
from jax.experimental.pallas import tpu as pltpu
from jax.sharding import PartitionSpec as P

CHUNK = 128
STEP = 256
SUB = STEP // CHUNK
LANES = 128
EDGE = 16
GROUPS = 2
EPSILON = 1e-05
EXACT = lax.Precision.HIGHEST
F32 = jnp.float32
BF16 = jnp.bfloat16
NEGATIVE = -1e30
M1, M2, M3, ENTRY, TAIL, SEG, RAW = 16, 17, 18, 19, 20, 21, 24
VMEM_LIMIT = 56 * 1024 * 1024


def nn(a, b):
    return lax.dot_general(a, b, (((1,), (0,)), ((), ())), preferred_element_type=F32)


def nt(a, b):
    return lax.dot_general(a, b, (((1,), (1,)), ((), ())), preferred_element_type=F32)


def tn(a, b):
    return nn(a.T, b)


def exact(a, b):
    return lax.dot_general(
        a, b, (((1,), (0,)), ((), ())), precision=EXACT, preferred_element_type=F32
    )


def lasts(microseconds):
    return pl.CostEstimate(
        flops=0, bytes_accessed=int(microseconds * 3.69e6), transcendentals=0
    )


ANYWHERE = pl.BlockSpec(memory_space=pl.ANY)


def ordered(kernel, inputs, after):
    def run(*refs):
        kernel(*refs[:inputs], *refs[inputs + after :])

    return run


def iota(shape, dim):
    return lax.broadcasted_iota(jnp.int32, shape, dim)


def spread(per_head, pairs):
    rows = per_head.shape[0]
    low = iota((rows, LANES), 1) < LANES // 2
    parts = []
    for j in range(pairs):
        left = jnp.broadcast_to(per_head[:, 2 * j : 2 * j + 1], (rows, LANES))
        right = jnp.broadcast_to(per_head[:, 2 * j + 1 : 2 * j + 2], (rows, LANES))
        parts.append(jnp.where(low, left, right))
    return jnp.concatenate(parts, 1)


def halves(block):
    low = iota(block.shape, 1) < LANES // 2
    zero = jnp.zeros_like(block)
    return jnp.where(low, block, zero), jnp.where(low, zero, block)


def silu(v):
    return v * jax.nn.sigmoid(v)


def rms_unit(x):
    return x * lax.rsqrt(jnp.mean(x * x, -1, keepdims=True) + EPSILON)


def front_kernel(
    gain_lane, starts, hid, edge, tok, cw, dtp, *refs
):
    (normed, gate, pre_out, u_out, rec, st, pdx, fin, pdfin, w, gain_out,
     buf, state, decay) = refs[-14:]
    shards = refs[:-14]
    inner = gate.shape[1]
    wide = pre_out.shape[1]
    pairs = inner // LANES
    at = pl.program_id(0)

    @pl.when(at == 0)
    def _():
        for k, shard in enumerate(shards):
            size = shard.shape[0]
            w[pl.ds(pl.multiple_of(starts[k], 16), size), :] = shard[...]
        for k in range(w.shape[0] // LANES):
            tile = w[k * LANES : (k + 1) * LANES, inner + wide :].astype(F32).T
            gain_out[:, k * LANES : (k + 1) * LANES] = jnp.broadcast_to(
                tile[gain_lane : gain_lane + 1, :], (8, LANES)
            )
        edge_low = (rms_unit(edge[...].astype(F32)) * gain_out[0:1, :]).astype(BF16)
        edge_pre = nn(edge_low, w[:, inner : inner + wide])
        buf[0:8, :] = edge_pre[EDGE - 8 :, :]
        state[...] = jnp.zeros_like(state)
        decay[...] = jnp.ones_like(decay)

    @pl.when(at > 0)
    def _():
        buf[0:8, :] = buf[STEP : STEP + 8, :]

    low = (rms_unit(hid[...].astype(F32)) * gain_out[0:1, :]).astype(BF16)
    normed[...] = low
    gate[...] = nn(low, w[:, :inner])
    pre = nn(low, w[:, inner : inner + wide])
    pre_out[...] = pre
    buf[8 : 8 + STEP, :] = pre
    raw_all = nn(low, w[:, inner + wide :]) + dtp[0:1, :]
    marks = tok[...]
    u = cw[3:4, :] * pre + cw[4:5, :]
    u = u + cw[2:3, :] * (buf[7 : 7 + STEP, :] * marks[:, M1 : M1 + 1])
    u = u + cw[1:2, :] * (buf[6 : 6 + STEP, :] * marks[:, M2 : M2 + 1])
    u = u + cw[0:1, :] * (buf[5 : 5 + STEP, :] * marks[:, M3 : M3 + 1])
    u_out[...] = u
    act = silu(u)
    step_all = jax.nn.softplus(raw_all)
    lane = iota((CHUNK, LANES), 1)
    lower = (iota((CHUNK, CHUNK), 0) >= iota((CHUNK, CHUNK), 1)).astype(F32)
    for i in range(SUB):
        rows = slice(i * CHUNK, (i + 1) * CHUNK)
        step = step_all[rows]
        cum = exact(lower, step * dtp[1:2, :])
        mark = marks[rows]
        rec[rows, :] = jnp.where(
            lane < 8, cum, jnp.where(lane < 16, step, jnp.where(lane < 24, mark, raw_all[rows]))
        )
        last = cum[CHUNK - 1 :, :]
        tail = mark[:, TAIL : TAIL + 1] * jnp.exp(last - cum) * step
        fed = (act[rows, :inner] * spread(tail, pairs)).astype(BF16)
        st[i] = state[...]
        pdx[8 * i : 8 * i + 8, :] = decay[...]
        passed = spread(mark[CHUNK - 1 :, ENTRY : ENTRY + 1] * jnp.exp(last), pairs)
        input_b = act[rows, inner : inner + LANES].T.astype(BF16)
        state[...] = passed * state[...] + nn(input_b, fed)
        decay[...] = decay[...] * passed
    fin[...] = state[...]
    pdfin[...] = decay[...]


def front(hidden, edge, tok, shards, starts, gain_lane, cw, dtp, inner, wide):
    rows, width = hidden.shape
    packed = shards[0].shape[1]
    steps = rows // STEP
    state_size = LANES

    def whole(a):
        return pl.BlockSpec(a.shape, lambda i: (0,) * a.ndim)

    def tall(cols):
        return pl.BlockSpec((STEP, cols), lambda i: (i, 0))

    chunks = rows // CHUNK
    return pl.pallas_call(
        functools.partial(front_kernel, gain_lane),
        grid=(steps,),
        in_specs=[
            pl.BlockSpec(memory_space=pltpu.SMEM),
            tall(width),
            whole(edge),
            tall(LANES),
            whole(cw),
            whole(dtp),
        ]
        + [whole(shard) for shard in shards],
        out_specs=[
            tall(width),
            tall(inner),
            tall(wide),
            tall(wide),
            tall(LANES),
            pl.BlockSpec((SUB, state_size, inner), lambda i: (i, 0, 0)),
            pl.BlockSpec((8 * SUB, inner), lambda i: (i, 0)),
            pl.BlockSpec((state_size, inner), lambda i: (0, 0)),
            pl.BlockSpec((8, inner), lambda i: (0, 0)),
            pl.BlockSpec((width, packed), lambda i: (0, 0)),
            pl.BlockSpec((8, width), lambda i: (0, 0)),
        ],
        out_shape=[
            jax.ShapeDtypeStruct((rows, width), BF16),
            jax.ShapeDtypeStruct((rows, inner), F32),
            jax.ShapeDtypeStruct((rows, wide), F32),
            jax.ShapeDtypeStruct((rows, wide), F32),
            jax.ShapeDtypeStruct((rows, LANES), F32),
            jax.ShapeDtypeStruct((chunks, state_size, inner), F32),
            jax.ShapeDtypeStruct((8 * chunks, inner), F32),
            jax.ShapeDtypeStruct((state_size, inner), F32),
            jax.ShapeDtypeStruct((8, inner), F32),
            jax.ShapeDtypeStruct((width, packed), BF16),
            jax.ShapeDtypeStruct((8, width), F32),
        ],
        scratch_shapes=[
            pltpu.VMEM((STEP + 8, wide), F32),
            pltpu.VMEM((state_size, inner), F32),
            pltpu.VMEM((8, inner), F32),
        ],
        compiler_params=pltpu.CompilerParams(
            dimension_semantics=("arbitrary",), vmem_limit_bytes=VMEM_LIMIT
        ),
        cost_estimate=lasts(0.01),
        name="front",
    )(starts, hidden, edge, tok, cw, dtp, *shards)


def middle_kernel(
    u, rec, gate, st, pdx, sin, og, wo, prm,
    scan, dgate, sums, *parts,
):
    inner = gate.shape[1]
    pairs = inner // LANES
    d_gate = nn(og[...], wo[...])
    dgate[...] = d_gate
    act = silu(u[...])
    below = iota((CHUNK, CHUNK), 0) >= iota((CHUNK, CHUNK), 1)
    for i in range(SUB):
        rows = slice(i * CHUNK, (i + 1) * CHUNK)
        record = rec[rows, :]
        turned = record.T
        state = (st[i] + pdx[8 * i : 8 * i + 1, :] * sin[...]).astype(BF16)
        x = act[rows, :inner]
        input_b = act[rows, inner : inner + LANES].astype(BF16)
        input_c = act[rows, inner + LANES :].astype(BF16)
        scores = nt(input_c, input_b)
        barred = jnp.where(
            below & (record[:, SEG : SEG + 1] == turned[SEG : SEG + 1, :]), 0.0, NEGATIVE
        )
        entry = record[:, ENTRY : ENTRY + 1] * jnp.exp(record)
        outs = []
        for j in range(pairs):
            block = x[:, j * LANES : (j + 1) * LANES].astype(BF16)
            total = None
            for k, side in enumerate(halves(block)):
                h = 2 * j + k
                link = jnp.exp(record[:, h : h + 1] - turned[h : h + 1, :] + barred)
                weight = (scores * link * turned[8 + h : 9 + h, :]).astype(BF16)
                term = nn(weight, side)
                total = term if total is None else total + term
            outs.append(total)
        y = jnp.concatenate(outs, 1)
        y = y + nn(input_c, state) * spread(entry, pairs) + prm[0:1, :] * x
        scan[rows, :] = y
    gated = scan[...] * silu(gate[...])
    scaled = gated * prm[1:2, :]
    squares = jnp.sum(gated * gated, -1, keepdims=True)
    crosses = jnp.sum(scaled * d_gate, -1, keepdims=True)
    lane = iota((STEP, LANES), 1)
    both = jnp.where(lane == 0, squares, jnp.where(lane == 1, crosses, 0.0))
    sums[...] = both.T[0:8, :]
    part_low = nt(scaled.astype(BF16), wo[...]).astype(BF16)
    steps_each = pl.num_programs(0) // len(parts)
    for k, part in enumerate(parts):

        @pl.when(pl.program_id(0) // steps_each == k)
        def _():
            part[...] = part_low


def middle(u, rec, gate, st, pdx, sin, og, wo, prm):
    rows, inner = gate.shape
    width = og.shape[1]
    steps = rows // STEP
    each = steps // GROUPS

    def whole(a):
        return pl.BlockSpec(a.shape, lambda i: (0,) * a.ndim)

    def tall(cols):
        return pl.BlockSpec((STEP, cols), lambda i: (i, 0))

    def part(k):
        return pl.BlockSpec((STEP, width), lambda i: (jnp.clip(i - k * each, 0, each - 1), 0))

    return pl.pallas_call(
        middle_kernel,
        grid=(steps,),
        in_specs=[
            tall(u.shape[1]),
            tall(LANES),
            tall(inner),
            pl.BlockSpec((SUB,) + st.shape[1:], lambda i: (i, 0, 0)),
            pl.BlockSpec((8 * SUB, inner), lambda i: (i, 0)),
            whole(sin),
            tall(width),
            whole(wo),
            whole(prm),
        ],
        out_specs=[
            tall(inner),
            tall(inner),
            pl.BlockSpec((8, STEP), lambda i: (0, i)),
        ]
        + [part(k) for k in range(GROUPS)],
        out_shape=[
            jax.ShapeDtypeStruct((rows, inner), F32),
            jax.ShapeDtypeStruct((rows, inner), F32),
            jax.ShapeDtypeStruct((8, rows), F32),
        ]
        + [jax.ShapeDtypeStruct((rows // GROUPS, width), BF16)] * GROUPS,
        compiler_params=pltpu.CompilerParams(
            dimension_semantics=("arbitrary",), vmem_limit_bytes=VMEM_LIMIT
        ),
        cost_estimate=lasts(0.01),
        name="middle",
    )(u, rec, gate, st, pdx, sin, og, wo, prm)


def turn_kernel(
    inner_total, scan, gate, dgate, sums, upre_c, rec, prm,
    dscan, dgr, glow, adj, psx, fin, gain_grad,
    state, decay,
):
    inner = gate.shape[1]
    pairs = inner // LANES
    at = pl.program_id(0)

    @pl.when(at == 0)
    def _():
        state[...] = jnp.zeros_like(state)
        decay[...] = jnp.ones_like(decay)
        gain_grad[...] = jnp.zeros_like(gain_grad)

    head = sums[...]
    column = jnp.concatenate([head, jnp.zeros((LANES - 8, STEP), F32)], 0).T
    inv = lax.rsqrt(column[:, 0:1] / inner_total + EPSILON)
    cube = inv * inv * inv * (column[:, 1:2] / inner_total)
    raw = gate[...]
    sig = jax.nn.sigmoid(raw)
    sil = raw * sig
    y = scan[...]
    gated = y * sil
    unit = gated * inv
    d_gate = dgate[...]
    gain = prm[1:2, :]
    glow[...] = (unit * gain).astype(BF16)
    gain_grad[...] += jnp.broadcast_to(jnp.sum(d_gate * unit, 0, keepdims=True), gain_grad.shape)
    d_gated = inv * gain * d_gate - gated * cube
    d_scan = d_gated * sil
    dscan[...] = d_scan
    dgr[...] = (d_gated * y * (sig * (1.0 + raw * (1.0 - sig)))).astype(BF16)
    input_c = silu(upre_c[...])
    for i in reversed(range(SUB)):
        rows = slice(i * CHUNK, (i + 1) * CHUNK)
        record = rec[rows, :]
        entry = record[:, ENTRY : ENTRY + 1] * jnp.exp(record)
        adj[i] = state[...]
        psx[8 * i : 8 * i + 8, :] = decay[...]
        passed = spread(entry[CHUNK - 1 :, :], pairs)
        fed = (d_scan[rows] * spread(entry, pairs)).astype(BF16)
        state[...] = passed * state[...] + nn(input_c[rows].T.astype(BF16), fed)
        decay[...] = decay[...] * passed
    fin[...] = state[...]


def turn(scan, gate, dgate, sums, u, rec, prm, inner_total):
    rows, inner = scan.shape
    steps = rows // STEP
    chunks = rows // CHUNK
    state_size = LANES
    c_block = u.shape[1] // LANES - 1

    def whole(a):
        return pl.BlockSpec(a.shape, lambda i: (0,) * a.ndim)

    def tall(cols):
        return pl.BlockSpec((STEP, cols), lambda i: (steps - 1 - i, 0))

    return pl.pallas_call(
        functools.partial(turn_kernel, float(inner_total)),
        grid=(steps,),
        in_specs=[
            tall(inner),
            tall(inner),
            tall(inner),
            pl.BlockSpec((8, STEP), lambda i: (0, steps - 1 - i)),
            pl.BlockSpec((STEP, LANES), lambda i: (steps - 1 - i, c_block)),
            tall(LANES),
            whole(prm),
        ],
        out_specs=[
            tall(inner),
            tall(inner),
            tall(inner),
            pl.BlockSpec((SUB, state_size, inner), lambda i: (steps - 1 - i, 0, 0)),
            pl.BlockSpec((8 * SUB, inner), lambda i: (steps - 1 - i, 0)),
            pl.BlockSpec((state_size, inner), lambda i: (0, 0)),
            pl.BlockSpec((8, inner), lambda i: (0, 0)),
        ],
        out_shape=[
            jax.ShapeDtypeStruct((rows, inner), F32),
            jax.ShapeDtypeStruct((rows, inner), BF16),
            jax.ShapeDtypeStruct((rows, inner), BF16),
            jax.ShapeDtypeStruct((chunks, state_size, inner), F32),
            jax.ShapeDtypeStruct((8 * chunks, inner), F32),
            jax.ShapeDtypeStruct((state_size, inner), F32),
            jax.ShapeDtypeStruct((8, inner), F32),
        ],
        scratch_shapes=[pltpu.VMEM((state_size, inner), F32), pltpu.VMEM((8, inner), F32)],
        compiler_params=pltpu.CompilerParams(
            dimension_semantics=("arbitrary",), vmem_limit_bytes=VMEM_LIMIT
        ),
        cost_estimate=lasts(0.01),
        name="turn",
    )(scan, gate, dgate, sums, u, rec, prm)


def back_kernel(
    u, rec, dscan, st, pdx, sin, adj, psx, ain, prm, dtp,
    dpre, dstep, skip_acc, head_acc,
):
    inner = dscan.shape[1]
    pairs = inner // LANES
    heads = 2 * pairs

    @pl.when(pl.program_id(0) == 0)
    def _():
        skip_acc[...] = jnp.zeros_like(skip_acc)
        head_acc[...] = jnp.zeros_like(head_acc)

    raw = u[...]
    sig = jax.nn.sigmoid(raw)
    act = raw * sig
    slope = sig * (1.0 + raw * (1.0 - sig))
    above = iota((CHUNK, CHUNK), 0) <= iota((CHUNK, CHUNK), 1)
    upper = above.astype(F32)
    lane = iota((CHUNK, LANES), 1)
    gather_heads = (iota((inner, LANES), 0) // (LANES // 2) == iota((inner, LANES), 1)).astype(BF16)
    nega = dtp[1:2, :]
    for i in range(SUB):
        rows = slice(i * CHUNK, (i + 1) * CHUNK)
        record = rec[rows, :]
        turned = record.T
        state = st[i] + pdx[8 * i : 8 * i + 1, :] * sin[...]
        state_low = state.astype(BF16)
        later = adj[i] + psx[8 * i : 8 * i + 1, :] * ain[...]
        later_low = later.astype(BF16)
        x = act[rows, :inner]
        b_wide = act[rows, inner : inner + LANES]
        c_wide = act[rows, inner + LANES :]
        input_b = b_wide.astype(BF16)
        input_c = c_wide.astype(BF16)
        dy = dscan[rows, :]
        scores = nt(input_b, input_c)
        barred = jnp.where(
            above & (record[:, SEG : SEG + 1] == turned[SEG : SEG + 1, :]), 0.0, NEGATIVE
        )
        step = pltpu.roll(record, LANES - 8, axis=1)
        z = pltpu.roll(record, LANES - RAW, axis=1)
        d_scores = jnp.zeros((CHUNK, CHUNK), F32)
        direct = jnp.zeros((CHUNK, LANES), F32)
        arrivals = []
        dxs = []
        for j in range(pairs):
            cols = slice(j * LANES, (j + 1) * LANES)
            x_sides = halves(x[:, cols].astype(BF16))
            dy_pair = dy[:, cols].astype(BF16)
            dy_sides = halves(dy_pair)
            total = None
            for k in range(2):
                h = 2 * j + k
                step_col = record[:, 8 + h : 9 + h]
                link = jnp.exp(turned[h : h + 1, :] - record[:, h : h + 1] + barred)
                d_link = nt(x_sides[k], dy_pair) * link
                d_scaled = d_link * step_col
                d_scores = d_scores + d_scaled
                flow = d_scaled * scores
                arrivals.append(jnp.sum(flow, 0, keepdims=True))
                given = jnp.sum(d_link * scores, 1, keepdims=True)
                direct = jnp.where(lane == h, given, direct)
                weight = (scores * link * step_col).astype(BF16)
                term = nn(weight, dy_sides[k])
                total = term if total is None else total + term
            dxs.append(total)
        dx = jnp.concatenate(dxs, 1)
        arrived = jnp.concatenate(arrivals + [jnp.zeros((CHUNK - heads, CHUNK), F32)], 0).T
        decay_in = record[:, ENTRY : ENTRY + 1] * jnp.exp(record)
        last = record[CHUNK - 1 :, :]
        tail_exp = record[:, TAIL : TAIL + 1] * jnp.exp(last - record)
        tail = tail_exp * step
        tail_wide = spread(jnp.where(lane < 8, tail, 0.0), pairs)
        fed_back = (dy * spread(decay_in, pairs)).astype(BF16)
        fed = (x * tail_wide).astype(BF16)
        from_state = nn(input_c, state_low)
        d_fed = nn(input_b, later_low)
        d_score_low = d_scores.astype(BF16)
        d_c = nt(fed_back, state_low) + nn(d_scores.T.astype(BF16), input_b)
        d_b = nt(fed, later_low) + nn(d_score_low, input_c)
        d_entry = nn((dy * from_state).astype(BF16), gather_heads)
        d_tail = nn((x * d_fed).astype(BF16), gather_heads)
        through = jnp.broadcast_to(jnp.sum(later * state, 0, keepdims=True), (16, inner))
        d_through = nn(through.astype(BF16), gather_heads)[0:1, :]
        dx = dx + d_fed * tail_wide + prm[0:1, :] * dy
        tail_flow = d_tail * tail
        d_cum = arrived - direct * step + d_entry * decay_in - tail_flow
        d_cum = jnp.where(lane < 8, d_cum, 0.0)
        d_last = jnp.sum(tail_flow, 0, keepdims=True) + decay_in[CHUNK - 1 :, :] * d_through
        d_rate = exact(upper, d_cum) + jnp.where(lane < 8, d_last, 0.0)
        d_step = direct + d_tail * tail_exp + nega * d_rate
        d_z = jnp.where(lane < 8, d_step * jax.nn.sigmoid(z), 0.0)
        dstep[rows, :] = d_z.astype(BF16)
        dpre[rows, :] = jnp.concatenate([dx, d_b, d_c], 1) * slope[rows]
        skip_acc[...] += jnp.broadcast_to(jnp.sum(dy * x, 0, keepdims=True), skip_acc.shape)
        head_acc[0:1, :] += jnp.sum(d_z, 0, keepdims=True)
        head_acc[1:2, :] += jnp.sum(
            jnp.where(lane < 8, d_rate * (nega * step), 0.0), 0, keepdims=True
        )


def back(u, rec, dscan, st, pdx, sin, adj, psx, ain, prm, dtp, after, group):
    rows, wide = u.shape
    inner = dscan.shape[1]
    steps = rows // STEP // GROUPS
    first = group * steps

    def whole(a):
        return pl.BlockSpec(a.shape, lambda i: (0,) * a.ndim)

    def tall(cols):
        return pl.BlockSpec((STEP, cols), lambda i: (first + i, 0))

    def out_tall(cols):
        return pl.BlockSpec((STEP, cols), lambda i: (i, 0))

    def states(at):
        return pl.BlockSpec((SUB,) + st.shape[1:], lambda i: (at + i, 0, 0))

    def decays(at):
        return pl.BlockSpec((8 * SUB, inner), lambda i: (at + i, 0))

    return pl.pallas_call(
        ordered(back_kernel, 11, len(after)),
        grid=(steps,),
        in_specs=[
            tall(wide),
            tall(LANES),
            tall(inner),
            states(first),
            decays(first),
            whole(sin),
            states(first),
            decays(first),
            whole(ain),
            whole(prm),
            whole(dtp),
        ]
        + [ANYWHERE] * len(after),
        out_specs=[
            out_tall(wide),
            out_tall(LANES),
            pl.BlockSpec((8, inner), lambda i: (0, 0)),
            pl.BlockSpec((8, LANES), lambda i: (0, 0)),
        ],
        out_shape=[
            jax.ShapeDtypeStruct((steps * STEP, wide), F32),
            jax.ShapeDtypeStruct((steps * STEP, LANES), BF16),
            jax.ShapeDtypeStruct((8, inner), F32),
            jax.ShapeDtypeStruct((8, LANES), F32),
        ],
        compiler_params=pltpu.CompilerParams(
            dimension_semantics=("arbitrary",), vmem_limit_bytes=VMEM_LIMIT
        ),
        cost_estimate=lasts(0.01),
        name="back",
    )(u, rec, dscan, st, pdx, sin, adj, psx, ain, prm, dtp, *after)


def rear_kernel(
    dpre, rec, pre, dgr, dstep, follow, w, cw,
    dproj, dnorm, conv_acc,
    buf, mbuf,
):
    wide = dpre.shape[1]
    inner = dgr.shape[1]

    @pl.when(pl.program_id(0) == 0)
    def _():
        buf[STEP : STEP + 8, :] = follow[:, :wide]
        mbuf[STEP : STEP + 8, :] = follow[:, wide:]
        conv_acc[...] = jnp.zeros_like(conv_acc)

    @pl.when(pl.program_id(0) > 0)
    def _():
        buf[STEP : STEP + 8, :] = buf[0:8, :]
        mbuf[STEP : STEP + 8, :] = mbuf[0:8, :]

    grad = dpre[...]
    buf[0:STEP, :] = grad
    mbuf[0:STEP, :] = rec[...]
    value = pre[...]
    total = cw[3:4, :] * grad
    conv_acc[3:4, :] += jnp.sum(value * grad, 0, keepdims=True)
    conv_acc[4:5, :] += jnp.sum(grad, 0, keepdims=True)
    for shift in (1, 2, 3):
        mark = mbuf[shift : shift + STEP, :][:, M1 + shift - 1 : M1 + shift]
        moved = buf[shift : shift + STEP, :] * mark
        total = total + cw[3 - shift : 4 - shift, :] * moved
        conv_acc[3 - shift : 4 - shift, :] += jnp.sum(value * moved, 0, keepdims=True)
    dproj[:, :inner] = dgr[...]
    dproj[:, inner : inner + wide] = total.astype(BF16)
    dproj[:, inner + wide :] = dstep[...]
    dnorm[...] = nt(dproj[...], w[...]).astype(BF16)


def rear(dpre, rec, pre, dgr, dstep, follow, w, cw, after, group):
    rows, wide = dpre.shape
    steps = rows // STEP
    inner = dgr.shape[1]
    width, packed = w.shape
    first = group * steps

    def whole(a):
        return pl.BlockSpec(a.shape, lambda i: (0,) * a.ndim)

    def tall(cols):
        return pl.BlockSpec((STEP, cols), lambda i: (first + steps - 1 - i, 0))

    def own(cols):
        return pl.BlockSpec((STEP, cols), lambda i: (steps - 1 - i, 0))

    return pl.pallas_call(
        ordered(rear_kernel, 8, len(after)),
        grid=(steps,),
        in_specs=[
            own(wide),
            tall(LANES),
            tall(wide),
            tall(inner),
            own(LANES),
            whole(follow),
            whole(w),
            whole(cw),
        ]
        + [ANYWHERE] * len(after),
        out_specs=[
            own(packed),
            own(width),
            pl.BlockSpec((8, wide), lambda i: (0, 0)),
        ],
        out_shape=[
            jax.ShapeDtypeStruct((rows, packed), BF16),
            jax.ShapeDtypeStruct((rows, width), BF16),
            jax.ShapeDtypeStruct((8, wide), F32),
        ],
        scratch_shapes=[
            pltpu.VMEM((STEP + 8, wide), F32),
            pltpu.VMEM((STEP + 8, LANES), F32),
        ],
        compiler_params=pltpu.CompilerParams(
            dimension_semantics=("arbitrary",), vmem_limit_bytes=VMEM_LIMIT
        ),
        cost_estimate=lasts(0.01),
        name="rear",
    )(dpre, rec, pre, dgr, dstep, follow, w, cw, *after)


def settle_kernel(inner_total, hid, sums, given, held, outer, filled, out):
    column = jnp.concatenate([sums[...], jnp.zeros((LANES - 8, STEP), F32)], 0).T
    inv = lax.rsqrt(column[:, 0:1] / inner_total + EPSILON)
    total = jnp.where(outer[0:1, 0:1] > 0.0, given[...].astype(F32), held[...].astype(F32))
    out[...] = (hid[...].astype(F32) + inv * total).astype(BF16)


def finish_kernel(hid, cot, gain, given, held, outer, filled, out):
    x = hid[...].astype(F32)
    inv = lax.rsqrt(jnp.mean(x * x, -1, keepdims=True) + EPSILON)
    total = jnp.where(outer[0:1, 0:1] > 0.0, given[...].astype(F32), held[...].astype(F32))
    scaled = total * gain[0:1, :]
    cross = jnp.mean(scaled * x, -1, keepdims=True)
    out[...] = cot[...].astype(F32) + inv * scaled - x * (inv * inv * inv * cross)


def by_group(kernel, out_like, dtype, group, fresh, operands, filled, after, name):
    rows, width = out_like.shape
    steps = rows // GROUPS // STEP
    first = group * steps
    specs = {
        "all": lambda a: pl.BlockSpec((STEP, a.shape[1]), lambda i: (first + i, 0)),
        "group": lambda a: pl.BlockSpec((STEP, a.shape[1]), lambda i: (i, 0)),
        "columns": lambda a: pl.BlockSpec((8, STEP), lambda i: (0, first + i)),
        "whole": lambda a: pl.BlockSpec(a.shape, lambda i: (0, 0)),
    }
    count = len(operands) + 1
    return pl.pallas_call(
        ordered(kernel, count, len(after)),
        grid=(steps,),
        in_specs=[specs[kind](a) for a, kind in operands] + [ANYWHERE] * (1 + len(after)),
        out_specs=pl.BlockSpec((STEP, width), lambda i: (first + i, 0)),
        out_shape=jax.ShapeDtypeStruct((rows, width), dtype),
        input_output_aliases={} if fresh else {count - 1: 0},
        compiler_params=pltpu.CompilerParams(
            dimension_semantics=("arbitrary",), vmem_limit_bytes=VMEM_LIMIT
        ),
        cost_estimate=lasts(0.01),
        name=name,
    )(*[a for a, _ in operands], filled, *after)


def passed_along(value, axis, steps):
    count = lax.axis_size(axis)
    leading, last = (max(0, -steps), min(count, count - steps))
    return lax.ppermute(value, axis, [(source, source + steps) for source in range(leading, last)])


def chained(own, decay, axis, steps):
    entering = jnp.zeros_like(own)
    for turn_at in range(lax.axis_size(axis) - 1):
        leaving = own if turn_at == 0 else own + decay * entering
        entering = passed_along(leaving, axis, steps)
    return entering


def butterfly_sum(value, axis):
    bit = 1
    while bit < lax.axis_size(axis):
        pairs = [(i, i ^ bit) for i in range(lax.axis_size(axis))]
        value = value + lax.ppermute(value, axis, pairs)
        bit *= 2
    return value


def join_kernel(pairs, *refs):
    outs = refs[2 * pairs :]
    for k in range(pairs):
        left, right, out = refs[2 * k], refs[2 * k + 1], outs[k]
        out[...] = (left[...].astype(F32) + right[...].astype(F32)).astype(out.dtype)


def join(pairs, after, held=()):
    rows, width = pairs[0][0].shape
    spec = pl.BlockSpec((STEP, width), lambda i: (i, 0))
    return pl.pallas_call(
        ordered(
            functools.partial(join_kernel, len(pairs)), 2 * len(pairs), len(after) + len(held)
        ),
        grid=(rows // STEP,),
        in_specs=[spec] * (2 * len(pairs)) + [ANYWHERE] * (len(after) + len(held)),
        out_specs=[spec] * len(pairs) + [ANYWHERE] * len(held),
        out_shape=[jax.ShapeDtypeStruct((rows, width), BF16)] * len(pairs)
        + [jax.ShapeDtypeStruct(a.shape, a.dtype) for a in held],
        input_output_aliases={
            2 * len(pairs) + len(after) + k: len(pairs) + k for k in range(len(held))
        },
        compiler_params=pltpu.CompilerParams(
            dimension_semantics=("arbitrary",), vmem_limit_bytes=VMEM_LIMIT
        ),
        cost_estimate=lasts(0.01),
        name="join",
    )(*[a for pair in pairs for a in pair], *after, *held)


class LineSum:
    def __init__(self, value):
        self.own = value
        self.come = lax.ppermute(value, "tp", [(0, 1), (3, 2)])
        self.near = self.across = self.given = None

    def pair(self):
        return (self.own if self.near is None else self.near, self.come)

    def joined(self, value):
        if self.near is None:
            self.near = value
            self.come = lax.ppermute(value, "tp", [(1, 2), (2, 1)])
        else:
            self.across = value
            self.given = lax.ppermute(value, "tp", [(1, 0), (2, 3)])


def advance(sums, after, held=()):
    outs = join([one.pair() for one in sums], after, held)
    for one, value in zip(sums, outs):
        one.joined(value)
    return tuple(outs)


def total_kernel(own, one, two, three, *refs):
    out = refs[len(refs) // 2]
    out[...] = (own[...] + one[...]) + (two[...] + three[...])


def total_over_row(own, held):
    others = [lax.ppermute(own, "tp", [(i, i ^ bits) for i in range(4)]) for bits in (1, 2, 3)]
    spec = pl.BlockSpec(own.shape, lambda i: (0, 0))
    return pl.pallas_call(
        total_kernel,
        grid=(1,),
        in_specs=[spec] * 4 + [ANYWHERE] * len(held),
        out_specs=[spec] + [ANYWHERE] * len(held),
        out_shape=[jax.ShapeDtypeStruct(own.shape, own.dtype)]
        + [jax.ShapeDtypeStruct(a.shape, a.dtype) for a in held],
        input_output_aliases={4 + k: 1 + k for k in range(len(held))},
        cost_estimate=lasts(0.01),
        name="total",
    )(own, *others, *held)


def other_core_kernel(place, w, wo, out):
    packed = w.shape[1]
    out[:, :packed] = w[...].astype(BF16)
    out[:, packed:] = wo[...].astype(BF16)


def split_kernel(
    place, w_ka, w_sa, w_kb, w_sb, wo_kb, wo_sb, r_ka, r_sa, r_kb, r_sb,
    keep_a, send_a, keep_b, send_b,
):
    cut, packed = keep_a.shape[1], w_ka.shape[1]
    keep_a[...] = w_ka[:, :cut] + r_ka[:, :cut].astype(F32)
    send_a[...] = (w_sa[:, :cut] + r_sa[:, :cut].astype(F32)).astype(BF16)
    for w, wo, r, out in ((w_kb, wo_kb, r_kb, keep_b), (w_sb, wo_sb, r_sb, send_b)):
        out[:, : packed - cut] = (w[:, cut:] + r[:, cut:packed].astype(F32)).astype(out.dtype)
        out[:, packed - cut :] = (wo[...] + r[:, packed:].astype(F32)).astype(out.dtype)


def second_kernel(place, ka, ra, sa, rsa, kb, rb, sb, rsb, keep_a, send_a, keep_b, send_b):
    keep_a[...] = ka[...] + ra[...].astype(F32)
    send_a[...] = (sa[...] + rsa[...].astype(F32)).astype(BF16)
    keep_b[...] = kb[...] + rb[...].astype(F32)
    send_b[...] = (sb[...] + rsb[...].astype(F32)).astype(BF16)


def placed_call(kernel, steps, place, inputs, outputs, name, after=()):
    return pl.pallas_call(
        ordered(kernel, 1 + len(inputs), len(after)),
        grid_spec=pltpu.PrefetchScalarGridSpec(
            num_scalar_prefetch=1,
            grid=(steps,),
            in_specs=[
                pl.BlockSpec((LANES, a.shape[1]), functools.partial(lambda f, i, p: (f(i, p), 0), f))
                for a, f in inputs
            ]
            + [ANYWHERE] * len(after),
            out_specs=[pl.BlockSpec((LANES, cols), lambda i, p: (i, 0)) for cols, _ in outputs],
        ),
        out_shape=[jax.ShapeDtypeStruct((steps * LANES, cols), kind) for cols, kind in outputs],
        compiler_params=pltpu.CompilerParams(
            dimension_semantics=("arbitrary",), vmem_limit_bytes=VMEM_LIMIT
        ),
        cost_estimate=lasts(0.01),
        name=name,
    )(place, *[a for a, _ in inputs], *after)


def to_owners(w, wo):
    after = yield
    packed, extra = w.shape[1], wo.shape[1]
    if lax.axis_size("fsdp") != 4 or lax.axis_size("ctx") != 2 or w.shape[0] != 8 * LANES:
        both = jnp.concatenate([w, wo], 1)
        summed = lax.psum_scatter(both, ("fsdp", "ctx"), scatter_dimension=0, tiled=True)
        yield w
        yield w
        yield w
        yield summed
        return

    def swapped(value, axis, bit):
        count = lax.axis_size(axis)
        return lax.ppermute(value, axis, [(i, i ^ bit) for i in range(count)])

    fsdp = lax.axis_index("fsdp")
    place = jnp.stack([fsdp % 2, fsdp // 2, lax.axis_index("ctx")]).astype(jnp.int32)
    cut = 1024
    rest = packed + extra - cut

    (sent,) = placed_call(
        other_core_kernel, 4, place,
        [(w, lambda i, p: 2 * i + 1 - p[2]), (wo, lambda i, p: 2 * i + 1 - p[2])],
        [(packed + extra, BF16)], "other_core", after,
    )
    come = swapped(sent, "ctx", 1)
    after = yield sent
    of = {
        "ka": lambda i, p: 2 * i + p[0],
        "sa": lambda i, p: 2 * i + 1 - p[0],
        "kb": lambda i, p: 2 * p[1] + i,
        "sb": lambda i, p: 2 * (1 - p[1]) + i,
    }

    def own(key):
        return lambda i, p: 2 * of[key](i, p) + p[2]

    keep_a, send_a, keep_b, send_b = placed_call(
        split_kernel, 2, place,
        [(w, own(key)) for key in ("ka", "sa", "kb", "sb")]
        + [(wo, own(key)) for key in ("kb", "sb")]
        + [(come, of[key]) for key in ("ka", "sa", "kb", "sb")],
        [(cut, F32), (cut, BF16), (rest, F32), (rest, BF16)], "split", after,
    )
    come_a, come_b = swapped(send_a, "fsdp", 1), swapped(send_b, "fsdp", 2)
    after = yield send_a
    y, not_y = (lambda i, p: p[1]), (lambda i, p: 1 - p[1])
    x, not_x = (lambda i, p: p[0]), (lambda i, p: 1 - p[0])
    keep_a, send_a, keep_b, send_b = placed_call(
        second_kernel, 1, place,
        [(keep_a, y), (come_a, y), (keep_a, not_y), (come_a, not_y)]
        + [(keep_b, x), (come_b, x), (keep_b, not_x), (come_b, not_x)],
        [(cut, F32), (cut, BF16), (rest, F32), (rest, BF16)], "second", after,
    )
    come_a, come_b = swapped(send_a, "fsdp", 2), swapped(send_b, "fsdp", 1)
    yield send_a
    yield jnp.concatenate([keep_a + come_a.astype(F32), keep_b + come_b.astype(F32)], 1)


def flip_kernel(value, out):
    out[...] = value[...].astype(F32).T.astype(out.dtype)


def flipped(value, after):
    rows, cols = value.shape
    return pl.pallas_call(
        ordered(flip_kernel, 1, len(after)),
        grid=(1,),
        in_specs=[pl.BlockSpec((rows, cols), lambda i: (0, 0))] + [ANYWHERE] * len(after),
        out_specs=pl.BlockSpec((cols, rows), lambda i: (0, 0)),
        out_shape=jax.ShapeDtypeStruct((cols, rows), value.dtype),
        cost_estimate=lasts(0.01),
        name="flip",
    )(value, *after)


def gathered_shards(own):
    rows = own.shape[0]
    if lax.axis_size("fsdp") != 4 or lax.axis_size("ctx") != 2:
        return [lax.all_gather(own, ("fsdp", "ctx"), axis=0, tiled=True)], [0]

    def swapped(value, axis, bit):
        count = lax.axis_size(axis)
        return lax.ppermute(value, axis, [(i, i ^ bit) for i in range(count)])

    half = rows // 2
    by_one, by_two = swapped(own, "fsdp", 1), swapped(own, "fsdp", 2)
    upper = swapped(by_two[:half], "fsdp", 1)
    under = swapped(by_one[half:], "fsdp", 2)
    mine = [own, by_one, by_two, upper, under]
    place = lax.axis_index("fsdp")
    core = lax.axis_index("ctx")
    shards, starts = [], []
    for other in (0, 1):
        for value, bits, offset in zip(mine, (0, 1, 2, 3, 3), (0, 0, 0, 0, half)):
            shards.append(swapped(value, "ctx", 1) if other else value)
            starts.append(((place ^ bits) * 2 + (core ^ other)) * rows + offset)
    return shards, starts


def token_marks(segment, before):
    rows = segment.shape[0]
    joined = jnp.concatenate([before, segment])
    marks = [joined[3 - j : 3 - j + rows] == segment for j in (1, 2, 3)]
    blocks = segment.reshape(-1, CHUNK)
    previous = jnp.concatenate([before[2:], blocks[:-1, -1]])
    marks.append((blocks == previous[:, None]).reshape(-1))
    marks.append((blocks == blocks[:, -1:]).reshape(-1))
    marks.append(segment)
    table = jnp.stack([mark.astype(F32) for mark in marks], 1)
    return jnp.pad(table, ((0, 0), (M1, LANES - M1 - len(marks))))


def body(
    hidden, segments, out_grad, norm_gain, w_zx, w_dt, w_bc, conv_x_w, conv_x_b,
    conv_bc_w, conv_bc_b, dt_bias, a_log, skip_d, out_gain, w_out,
):
    _, rows, width = hidden.shape
    inner = w_zx.shape[2]
    heads = w_dt.shape[1]
    head_size = inner // heads
    state_size = w_bc.shape[2]
    wide = inner + 2 * state_size
    taps = conv_x_w.shape[0]
    owned = w_zx.shape[0]
    shards = ("fsdp", "ctx")
    hid = hidden[0]
    cot = out_grad[0]
    segment = segments[0]

    packed = jnp.concatenate(
        [
            w_zx.reshape(owned, 2 * inner),
            w_bc.reshape(owned, 2 * state_size),
            w_dt, w_dt, w_dt, w_dt,
            norm_gain[:, None],
            jnp.zeros((owned, LANES - 4 * heads - 1), BF16),
        ],
        1,
    )
    w_shards, w_starts = gathered_shards(packed)
    w_starts = jnp.stack([jnp.asarray(start, jnp.int32) for start in w_starts])
    wo = lax.all_gather(
        flipped(w_out, tuple(w_shards[3:5])), shards, axis=0, tiled=True
    )

    edge, edge_segment = passed_along((hid[rows - EDGE :], segment[rows - 3 :]), "ctx", 1)
    tok = token_marks(segment, edge_segment)
    conv_rows = jnp.concatenate(
        [
            jnp.concatenate([conv_x_w, conv_bc_w.reshape(taps, -1)], 1),
            jnp.concatenate([conv_x_b, conv_bc_b.reshape(-1)])[None],
            jnp.zeros((8 - taps - 1, wide), F32),
        ],
        0,
    )
    spare = jnp.zeros((LANES - 4 * heads,), F32)
    rate = -jnp.exp(a_log)
    dtp = jnp.concatenate(
        [
            jnp.concatenate([dt_bias] * 4 + [spare])[None],
            jnp.concatenate([rate] * 4 + [spare])[None],
            jnp.zeros((6, LANES), F32),
        ],
        0,
    )
    prm = jnp.concatenate(
        [jnp.repeat(skip_d, head_size)[None], out_gain[None], jnp.zeros((6, inner), F32)], 0
    )

    normed, gate, pre, u, rec, st, pdx, state_end, decay_end, w_in, gain = front(
        hid, edge, tok, w_shards, w_starts, 4 * heads, conv_rows, dtp, inner, wide
    )
    sin = chained(state_end, decay_end[:1], "ctx", 1)
    inner_total = inner * lax.axis_size("tp")
    me = lax.axis_index("tp")
    outer = jnp.full((8, LANES), (me == 0) | (me == lax.axis_size("tp") - 1), F32)

    scan, dgate, sums, *parts = middle(u, rec, gate, st, pdx, sin, cot, wo, prm)
    sums, *parts = total_over_row(sums, parts)
    out_sums = [LineSum(part) for part in parts]
    dscan, dgr, glow, adj, psx, adj_start, out_gain_acc = turn(
        scan, gate, dgate, sums, u, rec, prm, inner_total
    )
    ain = chained(adj_start, decay_end[:1], "ctx", -1)
    contract_rows = (((0,), (0,)), ((), ()))
    wo_grad = lax.dot_general(cot, glow, contract_rows, preferred_element_type=F32)

    group_rows = rows // GROUPS
    backs = [None] * GROUPS
    rears = [None] * GROUPS
    d_normed = [None] * GROUPS
    follows = [None] * GROUPS

    def run_back(group, after):
        backs[group] = back(u, rec, dscan, st, pdx, sin, adj, psx, ain, prm, dtp, after, group)
        start = jnp.concatenate(
            [backs[group][0][:8], rec[group * group_rows : group * group_rows + 8]], 1
        )
        if group == 0:
            follows[GROUPS - 1] = passed_along(start, "ctx", -1)
        else:
            follows[group - 1] = start

    def run_rear(group, after):
        rears[group] = rear(
            backs[group][0], rec, pre, dgr, backs[group][1], follows[group], w_in,
            conv_rows, after, group,
        )
        d_normed[group] = LineSum(rears[group][1])

    def settle(group, filled, after=()):
        total = out_sums[group]
        return by_group(
            functools.partial(settle_kernel, float(inner_total)), hid, BF16, group, filled is None,
            [
                (hid, "all"),
                (sums, "columns"),
                (total.given, "group"),
                (total.across, "group"),
                (outer, "whole"),
            ],
            outer if filled is None else filled, after, "settle",
        )

    def finish(group, filled, after):
        total = d_normed[group]
        return by_group(
            finish_kernel, hid, F32, group, filled is None,
            [
                (hid, "all"),
                (cot, "all"),
                (gain, "whole"),
                (total.given, "group"),
                (total.across, "group"),
                (outer, "whole"),
            ],
            outer if filled is None else filled, after, "finish",
        )

    sum_a, sum_b = out_sums
    run_back(0, (wo_grad,))
    done = advance([sum_a], (backs[0][3],))
    run_back(1, done)
    run_rear(0, (backs[1][3],))
    done = advance([sum_b, sum_a], (rears[0][2],))
    run_rear(1, done)

    conv_acc = sum(r[2] for r in rears)
    skip_acc = sum(b[2][0] for b in backs)
    head_acc = sum(b[3] for b in backs)

    dproj = jnp.concatenate([r[0] for r in rears], 0)
    w_grad = lax.dot_general(normed, dproj, contract_rows, preferred_element_type=F32)
    owners = to_owners(w_grad, wo_grad)
    next(owners)
    sum_c, sum_d = d_normed
    done = advance([sum_b], (w_grad[:8, :LANES],))
    block_out = settle(0, None, done)
    done = advance([sum_c], (block_out,))
    owners.send(done)
    done = advance([sum_c], done)
    owners.send(done)
    block_out = settle(1, block_out, done)
    done = advance([sum_d], (block_out,))
    done = advance([sum_d], done)
    hidden_grad = finish(0, None, done)
    owners.send((hidden_grad,))
    both_owned = next(owners)
    hidden_grad = finish(1, hidden_grad, ())
    w_owned, wo_owned = both_owned[:, : w_grad.shape[1]], both_owned[:, w_grad.shape[1] :]

    small = jnp.concatenate(
        [
            conv_acc[: taps + 1].reshape(-1),
            out_gain_acc[0],
            skip_acc,
            head_acc[:2].reshape(-1),
        ]
    )
    small = butterfly_sum(butterfly_sum(small, "ctx"), "fsdp")
    conv_sum = small[: (taps + 1) * wide].reshape(taps + 1, wide)
    rest = small[(taps + 1) * wide :]
    shared = jnp.concatenate(
        [
            w_owned[:, 2 * inner : 2 * inner + 2 * state_size].reshape(-1),
            jnp.sum(packed.astype(F32) * w_owned, 1),
            conv_sum[:, inner:].reshape(-1),
        ]
    )
    shared = butterfly_sum(shared, "tp")
    bc_size = owned * 2 * state_size
    bc_owned = shared[:bc_size].reshape(owned, 2, state_size)
    gain_owned = shared[bc_size : bc_size + owned] / norm_gain.astype(F32)
    conv_bc = shared[bc_size + owned :].reshape(taps + 1, 2, state_size)

    return (
        block_out[None],
        hidden_grad[None],
        gain_owned,
        w_owned[:, : 2 * inner].reshape(owned, 2, inner),
        w_owned[:, 2 * inner + 2 * state_size : 2 * inner + 2 * state_size + heads],
        bc_owned,
        conv_sum[:taps, :inner],
        conv_sum[taps, :inner],
        conv_bc[:taps],
        conv_bc[taps],
        rest[2 * inner : 2 * inner + heads],
        rest[2 * inner + LANES : 2 * inner + LANES + heads],
        jnp.sum(rest[inner : 2 * inner].reshape(heads, head_size), 1),
        rest[:inner],
        wo_owned.T,
    )


def solution(mesh):
    placed = (
        P("fsdp", "ctx", None),
        P("fsdp", "ctx"),
        P("fsdp", "ctx", None),
        P(("fsdp", "ctx")),
        P(("fsdp", "ctx"), None, "tp"),
        P(("fsdp", "ctx"), "tp"),
        P(("fsdp", "ctx"), None, None),
        P(None, "tp"),
        P("tp"),
        P(),
        P(),
        P("tp"),
        P("tp"),
        P("tp"),
        P("tp"),
        P("tp", ("fsdp", "ctx")),
    )
    return jax.shard_map(
        body,
        mesh=mesh,
        in_specs=placed,
        out_specs=(
            P("fsdp", "ctx", None),
            P("fsdp", "ctx", None),
            P(("fsdp", "ctx")),
            P(("fsdp", "ctx"), None, "tp"),
            P(("fsdp", "ctx"), "tp"),
            P(("fsdp", "ctx"), None, None),
            P(None, "tp"),
            P("tp"),
            P(),
            P(),
            P("tp"),
            P("tp"),
            P("tp"),
            P("tp"),
            P("tp", ("fsdp", "ctx")),
        ),
        check_vma=False,
    )
```

```python
import functools

import jax
import jax.numpy as jnp
from jax import lax
from jax.experimental import pallas as pl
from jax.experimental.pallas import tpu as pltpu
from jax.sharding import PartitionSpec as P

CHUNK = 128
STEP = 256
SUB = STEP // CHUNK
LANES = 128
EDGE = 16
GROUPS = 2
EPSILON = 1e-05
EXACT = lax.Precision.HIGHEST
F32 = jnp.float32
BF16 = jnp.bfloat16
NEGATIVE = -1e30
M1, M2, M3, ENTRY, TAIL, SEG, RAW = 16, 17, 18, 19, 20, 21, 24
VMEM_LIMIT = 56 * 1024 * 1024


def nn(a, b):
    return lax.dot_general(a, b, (((1,), (0,)), ((), ())), preferred_element_type=F32)


def nt(a, b):
    return lax.dot_general(a, b, (((1,), (1,)), ((), ())), preferred_element_type=F32)


def tn(a, b):
    return nn(a.T, b)


def exact(a, b):
    return lax.dot_general(
        a, b, (((1,), (0,)), ((), ())), precision=EXACT, preferred_element_type=F32
    )


def lasts(microseconds):
    return pl.CostEstimate(
        flops=0, bytes_accessed=int(microseconds * 3.69e6), transcendentals=0
    )


ANYWHERE = pl.BlockSpec(memory_space=pl.ANY)


def ordered(kernel, inputs, after):
    def run(*refs):
        kernel(*refs[:inputs], *refs[inputs + after :])

    return run


def iota(shape, dim):
    return lax.broadcasted_iota(jnp.int32, shape, dim)


def spread(per_head, pairs):
    rows = per_head.shape[0]
    low = iota((rows, LANES), 1) < LANES // 2
    parts = []
    for j in range(pairs):
        left = jnp.broadcast_to(per_head[:, 2 * j : 2 * j + 1], (rows, LANES))
        right = jnp.broadcast_to(per_head[:, 2 * j + 1 : 2 * j + 2], (rows, LANES))
        parts.append(jnp.where(low, left, right))
    return jnp.concatenate(parts, 1)


def halves(block):
    low = iota(block.shape, 1) < LANES // 2
    zero = jnp.zeros_like(block)
    return jnp.where(low, block, zero), jnp.where(low, zero, block)


def silu(v):
    return v * jax.nn.sigmoid(v)


def rms_unit(x):
    return x * lax.rsqrt(jnp.mean(x * x, -1, keepdims=True) + EPSILON)


def front_kernel(
    gain_lane, starts, hid, edge, tok, cw, dtp, *refs
):
    (normed, gate, pre_out, u_out, rec, st, pdx, fin, pdfin, w, gain_out,
     buf, state, decay) = refs[-14:]
    shards = refs[:-14]
    inner = gate.shape[1]
    wide = pre_out.shape[1]
    pairs = inner // LANES
    at = pl.program_id(0)

    @pl.when(at == 0)
    def _():
        for k, shard in enumerate(shards):
            size = shard.shape[0]
            w[pl.ds(pl.multiple_of(starts[k], 16), size), :] = shard[...]
        for k in range(w.shape[0] // LANES):
            tile = w[k * LANES : (k + 1) * LANES, inner + wide :].astype(F32).T
            gain_out[:, k * LANES : (k + 1) * LANES] = jnp.broadcast_to(
                tile[gain_lane : gain_lane + 1, :], (8, LANES)
            )
        edge_low = (rms_unit(edge[...].astype(F32)) * gain_out[0:1, :]).astype(BF16)
        edge_pre = nn(edge_low, w[:, inner : inner + wide])
        buf[0:8, :] = edge_pre[EDGE - 8 :, :]
        state[...] = jnp.zeros_like(state)
        decay[...] = jnp.ones_like(decay)

    @pl.when(at > 0)
    def _():
        buf[0:8, :] = buf[STEP : STEP + 8, :]

    low = (rms_unit(hid[...].astype(F32)) * gain_out[0:1, :]).astype(BF16)
    normed[...] = low
    gate[...] = nn(low, w[:, :inner])
    pre = nn(low, w[:, inner : inner + wide])
    pre_out[...] = pre
    buf[8 : 8 + STEP, :] = pre
    raw_all = nn(low, w[:, inner + wide :]) + dtp[0:1, :]
    marks = tok[...]
    u = cw[3:4, :] * pre + cw[4:5, :]
    u = u + cw[2:3, :] * (buf[7 : 7 + STEP, :] * marks[:, M1 : M1 + 1])
    u = u + cw[1:2, :] * (buf[6 : 6 + STEP, :] * marks[:, M2 : M2 + 1])
    u = u + cw[0:1, :] * (buf[5 : 5 + STEP, :] * marks[:, M3 : M3 + 1])
    u_out[...] = u
    act = silu(u)
    step_all = jax.nn.softplus(raw_all)
    lane = iota((CHUNK, LANES), 1)
    lower = (iota((CHUNK, CHUNK), 0) >= iota((CHUNK, CHUNK), 1)).astype(F32)
    for i in range(SUB):
        rows = slice(i * CHUNK, (i + 1) * CHUNK)
        step = step_all[rows]
        cum = exact(lower, step * dtp[1:2, :])
        mark = marks[rows]
        rec[rows, :] = jnp.where(
            lane < 8, cum, jnp.where(lane < 16, step, jnp.where(lane < 24, mark, raw_all[rows]))
        )
        last = cum[CHUNK - 1 :, :]
        tail = mark[:, TAIL : TAIL + 1] * jnp.exp(last - cum) * step
        fed = (act[rows, :inner] * spread(tail, pairs)).astype(BF16)
        st[i] = state[...]
        pdx[8 * i : 8 * i + 8, :] = decay[...]
        passed = spread(mark[CHUNK - 1 :, ENTRY : ENTRY + 1] * jnp.exp(last), pairs)
        input_b = act[rows, inner : inner + LANES].T.astype(BF16)
        state[...] = passed * state[...] + nn(input_b, fed)
        decay[...] = decay[...] * passed
    fin[...] = state[...]
    pdfin[...] = decay[...]


def front(hidden, edge, tok, shards, starts, gain_lane, cw, dtp, inner, wide):
    rows, width = hidden.shape
    packed = shards[0].shape[1]
    steps = rows // STEP
    state_size = LANES

    def whole(a):
        return pl.BlockSpec(a.shape, lambda i: (0,) * a.ndim)

    def tall(cols):
        return pl.BlockSpec((STEP, cols), lambda i: (i, 0))

    chunks = rows // CHUNK
    return pl.pallas_call(
        functools.partial(front_kernel, gain_lane),
        grid=(steps,),
        in_specs=[
            pl.BlockSpec(memory_space=pltpu.SMEM),
            tall(width),
            whole(edge),
            tall(LANES),
            whole(cw),
            whole(dtp),
        ]
        + [whole(shard) for shard in shards],
        out_specs=[
            tall(width),
            tall(inner),
            tall(wide),
            tall(wide),
            tall(LANES),
            pl.BlockSpec((SUB, state_size, inner), lambda i: (i, 0, 0)),
            pl.BlockSpec((8 * SUB, inner), lambda i: (i, 0)),
            pl.BlockSpec((state_size, inner), lambda i: (0, 0)),
            pl.BlockSpec((8, inner), lambda i: (0, 0)),
            pl.BlockSpec((width, packed), lambda i: (0, 0)),
            pl.BlockSpec((8, width), lambda i: (0, 0)),
        ],
        out_shape=[
            jax.ShapeDtypeStruct((rows, width), BF16),
            jax.ShapeDtypeStruct((rows, inner), F32),
            jax.ShapeDtypeStruct((rows, wide), F32),
            jax.ShapeDtypeStruct((rows, wide), F32),
            jax.ShapeDtypeStruct((rows, LANES), F32),
            jax.ShapeDtypeStruct((chunks, state_size, inner), F32),
            jax.ShapeDtypeStruct((8 * chunks, inner), F32),
            jax.ShapeDtypeStruct((state_size, inner), F32),
            jax.ShapeDtypeStruct((8, inner), F32),
            jax.ShapeDtypeStruct((width, packed), BF16),
            jax.ShapeDtypeStruct((8, width), F32),
        ],
        scratch_shapes=[
            pltpu.VMEM((STEP + 8, wide), F32),
            pltpu.VMEM((state_size, inner), F32),
            pltpu.VMEM((8, inner), F32),
        ],
        compiler_params=pltpu.CompilerParams(
            dimension_semantics=("arbitrary",), vmem_limit_bytes=VMEM_LIMIT
        ),
        cost_estimate=lasts(0.01),
        name="front",
    )(starts, hidden, edge, tok, cw, dtp, *shards)


def middle_kernel(
    u, rec, gate, st, pdx, sin, og, wo, prm,
    scan, dgate, sums, *parts,
):
    inner = gate.shape[1]
    pairs = inner // LANES
    d_gate = nn(og[...], wo[...])
    dgate[...] = d_gate
    act = silu(u[...])
    below = iota((CHUNK, CHUNK), 0) >= iota((CHUNK, CHUNK), 1)
    for i in range(SUB):
        rows = slice(i * CHUNK, (i + 1) * CHUNK)
        record = rec[rows, :]
        turned = record.T
        state = (st[i] + pdx[8 * i : 8 * i + 1, :] * sin[...]).astype(BF16)
        x = act[rows, :inner]
        input_b = act[rows, inner : inner + LANES].astype(BF16)
        input_c = act[rows, inner + LANES :].astype(BF16)
        scores = nt(input_c, input_b)
        barred = jnp.where(
            below & (record[:, SEG : SEG + 1] == turned[SEG : SEG + 1, :]), 0.0, NEGATIVE
        )
        entry = record[:, ENTRY : ENTRY + 1] * jnp.exp(record)
        outs = []
        for j in range(pairs):
            block = x[:, j * LANES : (j + 1) * LANES].astype(BF16)
            total = None
            for k, side in enumerate(halves(block)):
                h = 2 * j + k
                link = jnp.exp(record[:, h : h + 1] - turned[h : h + 1, :] + barred)
                weight = (scores * link * turned[8 + h : 9 + h, :]).astype(BF16)
                term = nn(weight, side)
                total = term if total is None else total + term
            outs.append(total)
        y = jnp.concatenate(outs, 1)
        y = y + nn(input_c, state) * spread(entry, pairs) + prm[0:1, :] * x
        scan[rows, :] = y
    gated = scan[...] * silu(gate[...])
    scaled = gated * prm[1:2, :]
    squares = jnp.sum(gated * gated, -1, keepdims=True)
    crosses = jnp.sum(scaled * d_gate, -1, keepdims=True)
    lane = iota((STEP, LANES), 1)
    both = jnp.where(lane == 0, squares, jnp.where(lane == 1, crosses, 0.0))
    sums[...] = both.T[0:8, :]
    part_low = nt(scaled.astype(BF16), wo[...]).astype(BF16)
    steps_each = pl.num_programs(0) // len(parts)
    for k, part in enumerate(parts):

        @pl.when(pl.program_id(0) // steps_each == k)
        def _():
            part[...] = part_low


def middle(u, rec, gate, st, pdx, sin, og, wo, prm):
    rows, inner = gate.shape
    width = og.shape[1]
    steps = rows // STEP
    each = steps // GROUPS

    def whole(a):
        return pl.BlockSpec(a.shape, lambda i: (0,) * a.ndim)

    def tall(cols):
        return pl.BlockSpec((STEP, cols), lambda i: (i, 0))

    def part(k):
        return pl.BlockSpec((STEP, width), lambda i: (jnp.clip(i - k * each, 0, each - 1), 0))

    return pl.pallas_call(
        middle_kernel,
        grid=(steps,),
        in_specs=[
            tall(u.shape[1]),
            tall(LANES),
            tall(inner),
            pl.BlockSpec((SUB,) + st.shape[1:], lambda i: (i, 0, 0)),
            pl.BlockSpec((8 * SUB, inner), lambda i: (i, 0)),
            whole(sin),
            tall(width),
            whole(wo),
            whole(prm),
        ],
        out_specs=[
            tall(inner),
            tall(inner),
            pl.BlockSpec((8, STEP), lambda i: (0, i)),
        ]
        + [part(k) for k in range(GROUPS)],
        out_shape=[
            jax.ShapeDtypeStruct((rows, inner), F32),
            jax.ShapeDtypeStruct((rows, inner), F32),
            jax.ShapeDtypeStruct((8, rows), F32),
        ]
        + [jax.ShapeDtypeStruct((rows // GROUPS, width), BF16)] * GROUPS,
        compiler_params=pltpu.CompilerParams(
            dimension_semantics=("arbitrary",), vmem_limit_bytes=VMEM_LIMIT
        ),
        cost_estimate=lasts(0.01),
        name="middle",
    )(u, rec, gate, st, pdx, sin, og, wo, prm)


def turn_kernel(
    inner_total, scan, gate, dgate, sums, upre_c, rec, prm,
    dscan, dgr, glow, adj, psx, fin, gain_grad,
    state, decay,
):
    inner = gate.shape[1]
    pairs = inner // LANES
    at = pl.program_id(0)

    @pl.when(at == 0)
    def _():
        state[...] = jnp.zeros_like(state)
        decay[...] = jnp.ones_like(decay)
        gain_grad[...] = jnp.zeros_like(gain_grad)

    head = sums[...]
    column = jnp.concatenate([head, jnp.zeros((LANES - 8, STEP), F32)], 0).T
    inv = lax.rsqrt(column[:, 0:1] / inner_total + EPSILON)
    cube = inv * inv * inv * (column[:, 1:2] / inner_total)
    raw = gate[...]
    sig = jax.nn.sigmoid(raw)
    sil = raw * sig
    y = scan[...]
    gated = y * sil
    unit = gated * inv
    d_gate = dgate[...]
    gain = prm[1:2, :]
    glow[...] = (unit * gain).astype(BF16)
    gain_grad[...] += jnp.broadcast_to(jnp.sum(d_gate * unit, 0, keepdims=True), gain_grad.shape)
    d_gated = inv * gain * d_gate - gated * cube
    d_scan = d_gated * sil
    dscan[...] = d_scan
    dgr[...] = (d_gated * y * (sig * (1.0 + raw * (1.0 - sig)))).astype(BF16)
    input_c = silu(upre_c[...])
    for i in reversed(range(SUB)):
        rows = slice(i * CHUNK, (i + 1) * CHUNK)
        record = rec[rows, :]
        entry = record[:, ENTRY : ENTRY + 1] * jnp.exp(record)
        adj[i] = state[...]
        psx[8 * i : 8 * i + 8, :] = decay[...]
        passed = spread(entry[CHUNK - 1 :, :], pairs)
        fed = (d_scan[rows] * spread(entry, pairs)).astype(BF16)
        state[...] = passed * state[...] + nn(input_c[rows].T.astype(BF16), fed)
        decay[...] = decay[...] * passed
    fin[...] = state[...]


def turn(scan, gate, dgate, sums, u, rec, prm, inner_total):
    rows, inner = scan.shape
    steps = rows // STEP
    chunks = rows // CHUNK
    state_size = LANES
    c_block = u.shape[1] // LANES - 1

    def whole(a):
        return pl.BlockSpec(a.shape, lambda i: (0,) * a.ndim)

    def tall(cols):
        return pl.BlockSpec((STEP, cols), lambda i: (steps - 1 - i, 0))

    return pl.pallas_call(
        functools.partial(turn_kernel, float(inner_total)),
        grid=(steps,),
        in_specs=[
            tall(inner),
            tall(inner),
            tall(inner),
            pl.BlockSpec((8, STEP), lambda i: (0, steps - 1 - i)),
            pl.BlockSpec((STEP, LANES), lambda i: (steps - 1 - i, c_block)),
            tall(LANES),
            whole(prm),
        ],
        out_specs=[
            tall(inner),
            tall(inner),
            tall(inner),
            pl.BlockSpec((SUB, state_size, inner), lambda i: (steps - 1 - i, 0, 0)),
            pl.BlockSpec((8 * SUB, inner), lambda i: (steps - 1 - i, 0)),
            pl.BlockSpec((state_size, inner), lambda i: (0, 0)),
            pl.BlockSpec((8, inner), lambda i: (0, 0)),
        ],
        out_shape=[
            jax.ShapeDtypeStruct((rows, inner), F32),
            jax.ShapeDtypeStruct((rows, inner), BF16),
            jax.ShapeDtypeStruct((rows, inner), BF16),
            jax.ShapeDtypeStruct((chunks, state_size, inner), F32),
            jax.ShapeDtypeStruct((8 * chunks, inner), F32),
            jax.ShapeDtypeStruct((state_size, inner), F32),
            jax.ShapeDtypeStruct((8, inner), F32),
        ],
        scratch_shapes=[pltpu.VMEM((state_size, inner), F32), pltpu.VMEM((8, inner), F32)],
        compiler_params=pltpu.CompilerParams(
            dimension_semantics=("arbitrary",), vmem_limit_bytes=VMEM_LIMIT
        ),
        cost_estimate=lasts(0.01),
        name="turn",
    )(scan, gate, dgate, sums, u, rec, prm)


def back_kernel(
    u, rec, dscan, st, pdx, sin, adj, psx, ain, prm, dtp,
    dpre, dstep, skip_acc, head_acc,
):
    inner = dscan.shape[1]
    pairs = inner // LANES
    heads = 2 * pairs

    @pl.when(pl.program_id(0) == 0)
    def _():
        skip_acc[...] = jnp.zeros_like(skip_acc)
        head_acc[...] = jnp.zeros_like(head_acc)

    raw = u[...]
    sig = jax.nn.sigmoid(raw)
    act = raw * sig
    slope = sig * (1.0 + raw * (1.0 - sig))
    above = iota((CHUNK, CHUNK), 0) <= iota((CHUNK, CHUNK), 1)
    upper = above.astype(F32)
    lane = iota((CHUNK, LANES), 1)
    gather_heads = (iota((inner, LANES), 0) // (LANES // 2) == iota((inner, LANES), 1)).astype(BF16)
    nega = dtp[1:2, :]
    for i in range(SUB):
        rows = slice(i * CHUNK, (i + 1) * CHUNK)
        record = rec[rows, :]
        turned = record.T
        state = st[i] + pdx[8 * i : 8 * i + 1, :] * sin[...]
        state_low = state.astype(BF16)
        later = adj[i] + psx[8 * i : 8 * i + 1, :] * ain[...]
        later_low = later.astype(BF16)
        x = act[rows, :inner]
        b_wide = act[rows, inner : inner + LANES]
        c_wide = act[rows, inner + LANES :]
        input_b = b_wide.astype(BF16)
        input_c = c_wide.astype(BF16)
        dy = dscan[rows, :]
        scores = nt(input_b, input_c)
        barred = jnp.where(
            above & (record[:, SEG : SEG + 1] == turned[SEG : SEG + 1, :]), 0.0, NEGATIVE
        )
        step = pltpu.roll(record, LANES - 8, axis=1)
        z = pltpu.roll(record, LANES - RAW, axis=1)
        d_scores = jnp.zeros((CHUNK, CHUNK), F32)
        direct = jnp.zeros((CHUNK, LANES), F32)
        arrivals = []
        dxs = []
        for j in range(pairs):
            cols = slice(j * LANES, (j + 1) * LANES)
            x_sides = halves(x[:, cols].astype(BF16))
            dy_pair = dy[:, cols].astype(BF16)
            dy_sides = halves(dy_pair)
            total = None
            for k in range(2):
                h = 2 * j + k
                step_col = record[:, 8 + h : 9 + h]
                link = jnp.exp(turned[h : h + 1, :] - record[:, h : h + 1] + barred)
                d_link = nt(x_sides[k], dy_pair) * link
                d_scaled = d_link * step_col
                d_scores = d_scores + d_scaled
                flow = d_scaled * scores
                arrivals.append(jnp.sum(flow, 0, keepdims=True))
                given = jnp.sum(d_link * scores, 1, keepdims=True)
                direct = jnp.where(lane == h, given, direct)
                weight = (scores * link * step_col).astype(BF16)
                term = nn(weight, dy_sides[k])
                total = term if total is None else total + term
            dxs.append(total)
        dx = jnp.concatenate(dxs, 1)
        arrived = jnp.concatenate(arrivals + [jnp.zeros((CHUNK - heads, CHUNK), F32)], 0).T
        decay_in = record[:, ENTRY : ENTRY + 1] * jnp.exp(record)
        last = record[CHUNK - 1 :, :]
        tail_exp = record[:, TAIL : TAIL + 1] * jnp.exp(last - record)
        tail = tail_exp * step
        tail_wide = spread(jnp.where(lane < 8, tail, 0.0), pairs)
        fed_back = (dy * spread(decay_in, pairs)).astype(BF16)
        fed = (x * tail_wide).astype(BF16)
        from_state = nn(input_c, state_low)
        d_fed = nn(input_b, later_low)
        d_score_low = d_scores.astype(BF16)
        d_c = nt(fed_back, state_low) + nn(d_scores.T.astype(BF16), input_b)
        d_b = nt(fed, later_low) + nn(d_score_low, input_c)
        d_entry = nn((dy * from_state).astype(BF16), gather_heads)
        d_tail = nn((x * d_fed).astype(BF16), gather_heads)
        through = jnp.broadcast_to(jnp.sum(later * state, 0, keepdims=True), (16, inner))
        d_through = nn(through.astype(BF16), gather_heads)[0:1, :]
        dx = dx + d_fed * tail_wide + prm[0:1, :] * dy
        tail_flow = d_tail * tail
        d_cum = arrived - direct * step + d_entry * decay_in - tail_flow
        d_cum = jnp.where(lane < 8, d_cum, 0.0)
        d_last = jnp.sum(tail_flow, 0, keepdims=True) + decay_in[CHUNK - 1 :, :] * d_through
        d_rate = exact(upper, d_cum) + jnp.where(lane < 8, d_last, 0.0)
        d_step = direct + d_tail * tail_exp + nega * d_rate
        d_z = jnp.where(lane < 8, d_step * jax.nn.sigmoid(z), 0.0)
        dstep[rows, :] = d_z.astype(BF16)
        dpre[rows, :] = jnp.concatenate([dx, d_b, d_c], 1) * slope[rows]
        skip_acc[...] += jnp.broadcast_to(jnp.sum(dy * x, 0, keepdims=True), skip_acc.shape)
        head_acc[0:1, :] += jnp.sum(d_z, 0, keepdims=True)
        head_acc[1:2, :] += jnp.sum(
            jnp.where(lane < 8, d_rate * (nega * step), 0.0), 0, keepdims=True
        )


def back(u, rec, dscan, st, pdx, sin, adj, psx, ain, prm, dtp, after, group):
    rows, wide = u.shape
    inner = dscan.shape[1]
    steps = rows // STEP // GROUPS
    first = group * steps

    def whole(a):
        return pl.BlockSpec(a.shape, lambda i: (0,) * a.ndim)

    def tall(cols):
        return pl.BlockSpec((STEP, cols), lambda i: (first + i, 0))

    def out_tall(cols):
        return pl.BlockSpec((STEP, cols), lambda i: (i, 0))

    def states(at):
        return pl.BlockSpec((SUB,) + st.shape[1:], lambda i: (at + i, 0, 0))

    def decays(at):
        return pl.BlockSpec((8 * SUB, inner), lambda i: (at + i, 0))

    return pl.pallas_call(
        ordered(back_kernel, 11, len(after)),
        grid=(steps,),
        in_specs=[
            tall(wide),
            tall(LANES),
            tall(inner),
            states(first),
            decays(first),
            whole(sin),
            states(first),
            decays(first),
            whole(ain),
            whole(prm),
            whole(dtp),
        ]
        + [ANYWHERE] * len(after),
        out_specs=[
            out_tall(wide),
            out_tall(LANES),
            pl.BlockSpec((8, inner), lambda i: (0, 0)),
            pl.BlockSpec((8, LANES), lambda i: (0, 0)),
        ],
        out_shape=[
            jax.ShapeDtypeStruct((steps * STEP, wide), F32),
            jax.ShapeDtypeStruct((steps * STEP, LANES), BF16),
            jax.ShapeDtypeStruct((8, inner), F32),
            jax.ShapeDtypeStruct((8, LANES), F32),
        ],
        compiler_params=pltpu.CompilerParams(
            dimension_semantics=("arbitrary",), vmem_limit_bytes=VMEM_LIMIT
        ),
        cost_estimate=lasts(0.01),
        name="back",
    )(u, rec, dscan, st, pdx, sin, adj, psx, ain, prm, dtp, *after)


def rear_kernel(
    dpre, rec, pre, dgr, dstep, follow, w, cw,
    dproj, dnorm, conv_acc,
    buf, mbuf,
):
    wide = dpre.shape[1]
    inner = dgr.shape[1]

    @pl.when(pl.program_id(0) == 0)
    def _():
        buf[STEP : STEP + 8, :] = follow[:, :wide]
        mbuf[STEP : STEP + 8, :] = follow[:, wide:]
        conv_acc[...] = jnp.zeros_like(conv_acc)

    @pl.when(pl.program_id(0) > 0)
    def _():
        buf[STEP : STEP + 8, :] = buf[0:8, :]
        mbuf[STEP : STEP + 8, :] = mbuf[0:8, :]

    grad = dpre[...]
    buf[0:STEP, :] = grad
    mbuf[0:STEP, :] = rec[...]
    value = pre[...]
    total = cw[3:4, :] * grad
    conv_acc[3:4, :] += jnp.sum(value * grad, 0, keepdims=True)
    conv_acc[4:5, :] += jnp.sum(grad, 0, keepdims=True)
    for shift in (1, 2, 3):
        mark = mbuf[shift : shift + STEP, :][:, M1 + shift - 1 : M1 + shift]
        moved = buf[shift : shift + STEP, :] * mark
        total = total + cw[3 - shift : 4 - shift, :] * moved
        conv_acc[3 - shift : 4 - shift, :] += jnp.sum(value * moved, 0, keepdims=True)
    dproj[:, :inner] = dgr[...]
    dproj[:, inner : inner + wide] = total.astype(BF16)
    dproj[:, inner + wide :] = dstep[...]
    dnorm[...] = nt(dproj[...], w[...]).astype(BF16)


def rear(dpre, rec, pre, dgr, dstep, follow, w, cw, after, group):
    rows, wide = dpre.shape
    steps = rows // STEP
    inner = dgr.shape[1]
    width, packed = w.shape
    first = group * steps

    def whole(a):
        return pl.BlockSpec(a.shape, lambda i: (0,) * a.ndim)

    def tall(cols):
        return pl.BlockSpec((STEP, cols), lambda i: (first + steps - 1 - i, 0))

    def own(cols):
        return pl.BlockSpec((STEP, cols), lambda i: (steps - 1 - i, 0))

    return pl.pallas_call(
        ordered(rear_kernel, 8, len(after)),
        grid=(steps,),
        in_specs=[
            own(wide),
            tall(LANES),
            tall(wide),
            tall(inner),
            own(LANES),
            whole(follow),
            whole(w),
            whole(cw),
        ]
        + [ANYWHERE] * len(after),
        out_specs=[
            own(packed),
            own(width),
            pl.BlockSpec((8, wide), lambda i: (0, 0)),
        ],
        out_shape=[
            jax.ShapeDtypeStruct((rows, packed), BF16),
            jax.ShapeDtypeStruct((rows, width), BF16),
            jax.ShapeDtypeStruct((8, wide), F32),
        ],
        scratch_shapes=[
            pltpu.VMEM((STEP + 8, wide), F32),
            pltpu.VMEM((STEP + 8, LANES), F32),
        ],
        compiler_params=pltpu.CompilerParams(
            dimension_semantics=("arbitrary",), vmem_limit_bytes=VMEM_LIMIT
        ),
        cost_estimate=lasts(0.01),
        name="rear",
    )(dpre, rec, pre, dgr, dstep, follow, w, cw, *after)


def settle_kernel(inner_total, hid, sums, given, held, outer, filled, out, *handed):
    column = jnp.concatenate([sums[...], jnp.zeros((LANES - 8, STEP), F32)], 0).T
    inv = lax.rsqrt(column[:, 0:1] / inner_total + EPSILON)
    total = jnp.where(outer[0:1, 0:1] > 0.0, given[...].astype(F32), held[...].astype(F32))
    out[...] = (hid[...].astype(F32) + inv * total).astype(BF16)


def finish_kernel(hid, cot, gain, given, held, outer, filled, out, *handed):
    x = hid[...].astype(F32)
    inv = lax.rsqrt(jnp.mean(x * x, -1, keepdims=True) + EPSILON)
    total = jnp.where(outer[0:1, 0:1] > 0.0, given[...].astype(F32), held[...].astype(F32))
    scaled = total * gain[0:1, :]
    cross = jnp.mean(scaled * x, -1, keepdims=True)
    out[...] = cot[...].astype(F32) + inv * scaled - x * (inv * inv * inv * cross)


def by_group(kernel, out_like, dtype, group, fresh, operands, filled, after, name, held=()):
    rows, width = out_like.shape
    steps = rows // GROUPS // STEP
    first = group * steps
    specs = {
        "all": lambda a: pl.BlockSpec((STEP, a.shape[1]), lambda i: (first + i, 0)),
        "group": lambda a: pl.BlockSpec((STEP, a.shape[1]), lambda i: (i, 0)),
        "columns": lambda a: pl.BlockSpec((8, STEP), lambda i: (0, first + i)),
        "whole": lambda a: pl.BlockSpec(a.shape, lambda i: (0, 0)),
    }
    count = len(operands) + 1
    aliases = {} if fresh else {count - 1: 0}
    aliases.update({count + len(after) + k: 1 + k for k in range(len(held))})
    out, *handed = pl.pallas_call(
        ordered(kernel, count, len(after) + len(held)),
        grid=(steps,),
        in_specs=[specs[kind](a) for a, kind in operands]
        + [ANYWHERE] * (1 + len(after) + len(held)),
        out_specs=[pl.BlockSpec((STEP, width), lambda i: (first + i, 0))]
        + [ANYWHERE] * len(held),
        out_shape=[jax.ShapeDtypeStruct((rows, width), dtype)]
        + [jax.ShapeDtypeStruct(a.shape, a.dtype) for a in held],
        input_output_aliases=aliases,
        compiler_params=pltpu.CompilerParams(
            dimension_semantics=("arbitrary",), vmem_limit_bytes=VMEM_LIMIT
        ),
        cost_estimate=lasts(0.01),
        name=name,
    )(*[a for a, _ in operands], filled, *after, *held)
    return (out, handed) if held else out


def passed_along(value, axis, steps):
    count = lax.axis_size(axis)
    leading, last = (max(0, -steps), min(count, count - steps))
    return lax.ppermute(value, axis, [(source, source + steps) for source in range(leading, last)])


def chained(own, decay, axis, steps):
    entering = jnp.zeros_like(own)
    for turn_at in range(lax.axis_size(axis) - 1):
        leaving = own if turn_at == 0 else own + decay * entering
        entering = passed_along(leaving, axis, steps)
    return entering


def butterfly_sum(value, axis):
    bit = 1
    while bit < lax.axis_size(axis):
        pairs = [(i, i ^ bit) for i in range(lax.axis_size(axis))]
        value = value + lax.ppermute(value, axis, pairs)
        bit *= 2
    return value


def join_kernel(pairs, *refs):
    outs = refs[2 * pairs :]
    for k in range(pairs):
        left, right, out = refs[2 * k], refs[2 * k + 1], outs[k]
        out[...] = (left[...].astype(F32) + right[...].astype(F32)).astype(out.dtype)


def join(pairs, after, held=()):
    rows, width = pairs[0][0].shape
    spec = pl.BlockSpec((STEP, width), lambda i: (i, 0))
    return pl.pallas_call(
        ordered(
            functools.partial(join_kernel, len(pairs)), 2 * len(pairs), len(after) + len(held)
        ),
        grid=(rows // STEP,),
        in_specs=[spec] * (2 * len(pairs)) + [ANYWHERE] * (len(after) + len(held)),
        out_specs=[spec] * len(pairs) + [ANYWHERE] * len(held),
        out_shape=[jax.ShapeDtypeStruct((rows, width), BF16)] * len(pairs)
        + [jax.ShapeDtypeStruct(a.shape, a.dtype) for a in held],
        input_output_aliases={
            2 * len(pairs) + len(after) + k: len(pairs) + k for k in range(len(held))
        },
        compiler_params=pltpu.CompilerParams(
            dimension_semantics=("arbitrary",), vmem_limit_bytes=VMEM_LIMIT
        ),
        cost_estimate=lasts(0.01),
        name="join",
    )(*[a for pair in pairs for a in pair], *after, *held)


def trade_kernel(pairs, *refs):
    own, outer = refs[2 * pairs], refs[2 * pairs + 1]
    outs = refs[2 * pairs + 2 :]
    for k in range(pairs):
        left, right = refs[2 * k], refs[2 * k + 1]
        total = left[...].astype(F32) + right[...].astype(F32)
        outs[k][...] = total.astype(BF16)
    outs[pairs][...] = jnp.where(outer[0:1, 0:1] > 0.0, own[...].astype(F32), total).astype(BF16)


def trade(pairs, own, outer, after):
    rows, width = own.shape
    spec = pl.BlockSpec((STEP, width), lambda i: (i, 0))
    flag = pl.BlockSpec(outer.shape, lambda i: (0, 0))
    count = len(pairs)
    return pl.pallas_call(
        ordered(functools.partial(trade_kernel, count), 2 * count + 2, len(after)),
        grid=(rows // STEP,),
        in_specs=[spec] * (2 * count + 1) + [flag] + [ANYWHERE] * len(after),
        out_specs=[spec] * (count + 1),
        out_shape=[jax.ShapeDtypeStruct((rows, width), BF16)] * (count + 1),
        compiler_params=pltpu.CompilerParams(
            dimension_semantics=("arbitrary",), vmem_limit_bytes=VMEM_LIMIT
        ),
        cost_estimate=lasts(0.01),
        name="trade",
    )(*[a for pair in pairs for a in pair], own, outer, *after)


class LineSum:
    def __init__(self, value, come=None):
        self.own = value
        self.come = lax.ppermute(value, "tp", [(0, 1), (3, 2)]) if come is None else come
        self.near = self.across = self.given = None

    def pair(self):
        return (self.own if self.near is None else self.near, self.come)

    def joined(self, value):
        if self.near is None:
            self.near = value
            self.come = lax.ppermute(value, "tp", [(1, 2), (2, 1)])
        else:
            self.across = value
            self.given = lax.ppermute(value, "tp", [(1, 0), (2, 3)])


def advance_and_begin(sums, value, outer, after):
    *outs, both = trade([one.pair() for one in sums], value, outer, after)
    for one, out in zip(sums[:-1], outs):
        one.joined(out)
    sums[-1].across = outs[-1]
    come = lax.ppermute(both, "tp", [(0, 1), (1, 0), (2, 3), (3, 2)])
    sums[-1].given = come
    return LineSum(value, come), tuple(outs)


def advance(sums, after, held=()):
    outs = join([one.pair() for one in sums], after, held)
    for one, value in zip(sums, outs):
        one.joined(value)
    return tuple(outs)


def total_kernel(own, one, two, three, *refs):
    out = refs[len(refs) // 2]
    out[...] = (own[...] + one[...]) + (two[...] + three[...])


def total_over_row(own, held):
    others = [lax.ppermute(own, "tp", [(i, i ^ bits) for i in range(4)]) for bits in (1, 2, 3)]
    spec = pl.BlockSpec(own.shape, lambda i: (0, 0))
    return pl.pallas_call(
        total_kernel,
        grid=(1,),
        in_specs=[spec] * 4 + [ANYWHERE] * len(held),
        out_specs=[spec] + [ANYWHERE] * len(held),
        out_shape=[jax.ShapeDtypeStruct(own.shape, own.dtype)]
        + [jax.ShapeDtypeStruct(a.shape, a.dtype) for a in held],
        input_output_aliases={4 + k: 1 + k for k in range(len(held))},
        cost_estimate=lasts(0.01),
        name="total",
    )(own, *others, *held)


def other_core_kernel(place, w, wo, out):
    packed = w.shape[1]
    out[:, :packed] = w[...].astype(BF16)
    out[:, packed:] = wo[...].astype(BF16)


def split_kernel(
    place, w_ka, w_sa, w_kb, w_sb, wo_kb, wo_sb, r_ka, r_sa, r_kb, r_sb,
    keep_a, send_a, keep_b, send_b,
):
    cut, packed = keep_a.shape[1], w_ka.shape[1]
    keep_a[...] = w_ka[:, :cut] + r_ka[:, :cut].astype(F32)
    send_a[...] = (w_sa[:, :cut] + r_sa[:, :cut].astype(F32)).astype(BF16)
    for w, wo, r, out in ((w_kb, wo_kb, r_kb, keep_b), (w_sb, wo_sb, r_sb, send_b)):
        out[:, : packed - cut] = (w[:, cut:] + r[:, cut:packed].astype(F32)).astype(out.dtype)
        out[:, packed - cut :] = (wo[...] + r[:, packed:].astype(F32)).astype(out.dtype)


def second_kernel(place, ka, ra, sa, rsa, kb, rb, sb, rsb, keep_a, send_a, keep_b, send_b):
    keep_a[...] = ka[...] + ra[...].astype(F32)
    send_a[...] = (sa[...] + rsa[...].astype(F32)).astype(BF16)
    keep_b[...] = kb[...] + rb[...].astype(F32)
    send_b[...] = (sb[...] + rsb[...].astype(F32)).astype(BF16)


def placed_call(kernel, steps, place, inputs, outputs, name, after=()):
    return pl.pallas_call(
        ordered(kernel, 1 + len(inputs), len(after)),
        grid_spec=pltpu.PrefetchScalarGridSpec(
            num_scalar_prefetch=1,
            grid=(steps,),
            in_specs=[
                pl.BlockSpec((LANES, a.shape[1]), functools.partial(lambda f, i, p: (f(i, p), 0), f))
                for a, f in inputs
            ]
            + [ANYWHERE] * len(after),
            out_specs=[pl.BlockSpec((LANES, cols), lambda i, p: (i, 0)) for cols, _ in outputs],
        ),
        out_shape=[jax.ShapeDtypeStruct((steps * LANES, cols), kind) for cols, kind in outputs],
        compiler_params=pltpu.CompilerParams(
            dimension_semantics=("arbitrary",), vmem_limit_bytes=VMEM_LIMIT
        ),
        cost_estimate=lasts(0.01),
        name=name,
    )(place, *[a for a, _ in inputs], *after)


def to_owners(w, wo):
    after = yield
    packed, extra = w.shape[1], wo.shape[1]
    if lax.axis_size("fsdp") != 4 or lax.axis_size("ctx") != 2 or w.shape[0] != 8 * LANES:
        both = jnp.concatenate([w, wo], 1)
        summed = lax.psum_scatter(both, ("fsdp", "ctx"), scatter_dimension=0, tiled=True)
        yield w
        yield w
        (summed,) = yield w, [summed]
        yield summed
        return

    def swapped(value, axis, bit):
        count = lax.axis_size(axis)
        return lax.ppermute(value, axis, [(i, i ^ bit) for i in range(count)])

    fsdp = lax.axis_index("fsdp")
    place = jnp.stack([fsdp % 2, fsdp // 2, lax.axis_index("ctx")]).astype(jnp.int32)
    cut = 1024
    rest = packed + extra - cut

    (sent,) = placed_call(
        other_core_kernel, 4, place,
        [(w, lambda i, p: 2 * i + 1 - p[2]), (wo, lambda i, p: 2 * i + 1 - p[2])],
        [(packed + extra, BF16)], "other_core", after,
    )
    come = swapped(sent, "ctx", 1)
    after = yield sent
    of = {
        "ka": lambda i, p: 2 * i + p[0],
        "sa": lambda i, p: 2 * i + 1 - p[0],
        "kb": lambda i, p: 2 * p[1] + i,
        "sb": lambda i, p: 2 * (1 - p[1]) + i,
    }

    def own(key):
        return lambda i, p: 2 * of[key](i, p) + p[2]

    keep_a, send_a, keep_b, send_b = placed_call(
        split_kernel, 2, place,
        [(w, own(key)) for key in ("ka", "sa", "kb", "sb")]
        + [(wo, own(key)) for key in ("kb", "sb")]
        + [(come, of[key]) for key in ("ka", "sa", "kb", "sb")],
        [(cut, F32), (cut, BF16), (rest, F32), (rest, BF16)], "split", after,
    )
    come_a, come_b = swapped(send_a, "fsdp", 1), swapped(send_b, "fsdp", 2)
    after = yield send_a
    y, not_y = (lambda i, p: p[1]), (lambda i, p: 1 - p[1])
    x, not_x = (lambda i, p: p[0]), (lambda i, p: 1 - p[0])
    keep_a, send_a, keep_b, send_b = placed_call(
        second_kernel, 1, place,
        [(keep_a, y), (come_a, y), (keep_a, not_y), (come_a, not_y)]
        + [(keep_b, x), (come_b, x), (keep_b, not_x), (come_b, not_x)],
        [(cut, F32), (cut, BF16), (rest, F32), (rest, BF16)], "second", after,
    )
    come_a, come_b = swapped(send_a, "fsdp", 2), swapped(send_b, "fsdp", 1)
    keep_a, keep_b = yield send_a, [keep_a, keep_b]
    yield jnp.concatenate([keep_a + come_a.astype(F32), keep_b + come_b.astype(F32)], 1)


def flip_kernel(value, out):
    out[...] = value[...].astype(F32).T.astype(out.dtype)


def flipped(value, after):
    rows, cols = value.shape
    return pl.pallas_call(
        ordered(flip_kernel, 1, len(after)),
        grid=(1,),
        in_specs=[pl.BlockSpec((rows, cols), lambda i: (0, 0))] + [ANYWHERE] * len(after),
        out_specs=pl.BlockSpec((cols, rows), lambda i: (0, 0)),
        out_shape=jax.ShapeDtypeStruct((cols, rows), value.dtype),
        cost_estimate=lasts(0.01),
        name="flip",
    )(value, *after)


def gathered_shards(own):
    rows = own.shape[0]
    if lax.axis_size("fsdp") != 4 or lax.axis_size("ctx") != 2:
        return [lax.all_gather(own, ("fsdp", "ctx"), axis=0, tiled=True)], [0]

    def swapped(value, axis, bit):
        count = lax.axis_size(axis)
        return lax.ppermute(value, axis, [(i, i ^ bit) for i in range(count)])

    half = rows // 2
    by_one, by_two = swapped(own, "fsdp", 1), swapped(own, "fsdp", 2)
    upper = swapped(by_two[:half], "fsdp", 1)
    under = swapped(by_one[half:], "fsdp", 2)
    mine = [own, by_one, by_two, upper, under]
    place = lax.axis_index("fsdp")
    core = lax.axis_index("ctx")
    shards, starts = [], []
    for other in (0, 1):
        for value, bits, offset in zip(mine, (0, 1, 2, 3, 3), (0, 0, 0, 0, half)):
            shards.append(swapped(value, "ctx", 1) if other else value)
            starts.append(((place ^ bits) * 2 + (core ^ other)) * rows + offset)
    return shards, starts


def token_marks(segment, before):
    rows = segment.shape[0]
    joined = jnp.concatenate([before, segment])
    marks = [joined[3 - j : 3 - j + rows] == segment for j in (1, 2, 3)]
    blocks = segment.reshape(-1, CHUNK)
    previous = jnp.concatenate([before[2:], blocks[:-1, -1]])
    marks.append((blocks == previous[:, None]).reshape(-1))
    marks.append((blocks == blocks[:, -1:]).reshape(-1))
    marks.append(segment)
    table = jnp.stack([mark.astype(F32) for mark in marks], 1)
    return jnp.pad(table, ((0, 0), (M1, LANES - M1 - len(marks))))


def body(
    hidden, segments, out_grad, norm_gain, w_zx, w_dt, w_bc, conv_x_w, conv_x_b,
    conv_bc_w, conv_bc_b, dt_bias, a_log, skip_d, out_gain, w_out,
):
    _, rows, width = hidden.shape
    inner = w_zx.shape[2]
    heads = w_dt.shape[1]
    head_size = inner // heads
    state_size = w_bc.shape[2]
    wide = inner + 2 * state_size
    taps = conv_x_w.shape[0]
    owned = w_zx.shape[0]
    shards = ("fsdp", "ctx")
    hid = hidden[0]
    cot = out_grad[0]
    segment = segments[0]

    packed = jnp.concatenate(
        [
            w_zx.reshape(owned, 2 * inner),
            w_bc.reshape(owned, 2 * state_size),
            w_dt, w_dt, w_dt, w_dt,
            norm_gain[:, None],
            jnp.zeros((owned, LANES - 4 * heads - 1), BF16),
        ],
        1,
    )
    w_shards, w_starts = gathered_shards(packed)
    w_starts = jnp.stack([jnp.asarray(start, jnp.int32) for start in w_starts])
    wo = lax.all_gather(
        flipped(w_out, tuple(w_shards[3:5])), shards, axis=0, tiled=True
    )

    edge, edge_segment = passed_along((hid[rows - EDGE :], segment[rows - 3 :]), "ctx", 1)
    tok = token_marks(segment, edge_segment)
    conv_rows = jnp.concatenate(
        [
            jnp.concatenate([conv_x_w, conv_bc_w.reshape(taps, -1)], 1),
            jnp.concatenate([conv_x_b, conv_bc_b.reshape(-1)])[None],
            jnp.zeros((8 - taps - 1, wide), F32),
        ],
        0,
    )
    spare = jnp.zeros((LANES - 4 * heads,), F32)
    rate = -jnp.exp(a_log)
    dtp = jnp.concatenate(
        [
            jnp.concatenate([dt_bias] * 4 + [spare])[None],
            jnp.concatenate([rate] * 4 + [spare])[None],
            jnp.zeros((6, LANES), F32),
        ],
        0,
    )
    prm = jnp.concatenate(
        [jnp.repeat(skip_d, head_size)[None], out_gain[None], jnp.zeros((6, inner), F32)], 0
    )

    normed, gate, pre, u, rec, st, pdx, state_end, decay_end, w_in, gain = front(
        hid, edge, tok, w_shards, w_starts, 4 * heads, conv_rows, dtp, inner, wide
    )
    sin = chained(state_end, decay_end[:1], "ctx", 1)
    inner_total = inner * lax.axis_size("tp")
    me = lax.axis_index("tp")
    outer = jnp.full((8, LANES), (me == 0) | (me == lax.axis_size("tp") - 1), F32)

    scan, dgate, sums, *parts = middle(u, rec, gate, st, pdx, sin, cot, wo, prm)
    sums, *parts = total_over_row(sums, parts)
    out_sums = [LineSum(part) for part in parts]
    dscan, dgr, glow, adj, psx, adj_start, out_gain_acc = turn(
        scan, gate, dgate, sums, u, rec, prm, inner_total
    )
    ain = chained(adj_start, decay_end[:1], "ctx", -1)
    contract_rows = (((0,), (0,)), ((), ()))
    wo_grad = lax.dot_general(cot, glow, contract_rows, preferred_element_type=F32)

    group_rows = rows // GROUPS
    backs = [None] * GROUPS
    rears = [None] * GROUPS
    d_normed = [None] * GROUPS
    follows = [None] * GROUPS

    def run_back(group, after):
        backs[group] = back(u, rec, dscan, st, pdx, sin, adj, psx, ain, prm, dtp, after, group)
        start = jnp.concatenate(
            [backs[group][0][:8], rec[group * group_rows : group * group_rows + 8]], 1
        )
        if group == 0:
            follows[GROUPS - 1] = passed_along(start, "ctx", -1)
        else:
            follows[group - 1] = start

    def run_rear(group, after):
        rears[group] = rear(
            backs[group][0], rec, pre, dgr, backs[group][1], follows[group], w_in,
            conv_rows, after, group,
        )

    def settle(group, filled, after=()):
        total = out_sums[group]
        return by_group(
            functools.partial(settle_kernel, float(inner_total)), hid, BF16, group, filled is None,
            [
                (hid, "all"),
                (sums, "columns"),
                (total.given, "group"),
                (total.across, "group"),
                (outer, "whole"),
            ],
            outer if filled is None else filled, after, "settle",
        )

    def finish(group, filled, after, held=()):
        total = d_normed[group]
        return by_group(
            finish_kernel, hid, F32, group, filled is None,
            [
                (hid, "all"),
                (cot, "all"),
                (gain, "whole"),
                (total.given, "group"),
                (total.across, "group"),
                (outer, "whole"),
            ],
            outer if filled is None else filled, after, "finish", held,
        )

    sum_a, sum_b = out_sums
    run_back(0, (wo_grad,))
    done = advance([sum_a], (backs[0][3],))
    run_back(1, done)
    run_rear(0, (backs[1][3],))
    d_normed[0], done = advance_and_begin([sum_b, sum_a], rears[0][1], outer, (rears[0][2],))
    run_rear(1, done)

    conv_acc = sum(r[2] for r in rears)
    skip_acc = sum(b[2][0] for b in backs)
    head_acc = sum(b[3] for b in backs)

    dproj = jnp.concatenate([r[0] for r in rears], 0)
    w_grad = lax.dot_general(normed, dproj, contract_rows, preferred_element_type=F32)
    owners = to_owners(w_grad, wo_grad)
    next(owners)
    d_normed[1], done = advance_and_begin(
        [sum_b], rears[1][1], outer, (w_grad[:8, :LANES],)
    )
    sum_c, sum_d = d_normed
    block_out = settle(0, None, done)
    done = advance([sum_c], (block_out,))
    owners.send(done)
    done = advance([sum_c], done)
    sent = owners.send(done)
    block_out = settle(1, block_out, done + (sent,))
    done = advance([sum_d], (block_out,))
    sent, kept = owners.send(done)
    done = advance([sum_d], (sent,))
    hidden_grad, kept = finish(0, None, done, kept)
    both_owned = owners.send(kept)
    hidden_grad = finish(1, hidden_grad, ())
    w_owned, wo_owned = both_owned[:, : w_grad.shape[1]], both_owned[:, w_grad.shape[1] :]

    small = jnp.concatenate(
        [
            conv_acc[: taps + 1].reshape(-1),
            out_gain_acc[0],
            skip_acc,
            head_acc[:2].reshape(-1),
        ]
    )
    small = butterfly_sum(butterfly_sum(small, "ctx"), "fsdp")
    conv_sum = small[: (taps + 1) * wide].reshape(taps + 1, wide)
    rest = small[(taps + 1) * wide :]
    shared = jnp.concatenate(
        [
            w_owned[:, 2 * inner : 2 * inner + 2 * state_size].reshape(-1),
            jnp.sum(packed.astype(F32) * w_owned, 1),
            conv_sum[:, inner:].reshape(-1),
        ]
    )
    shared = butterfly_sum(shared, "tp")
    bc_size = owned * 2 * state_size
    bc_owned = shared[:bc_size].reshape(owned, 2, state_size)
    gain_owned = shared[bc_size : bc_size + owned] / norm_gain.astype(F32)
    conv_bc = shared[bc_size + owned :].reshape(taps + 1, 2, state_size)

    return (
        block_out[None],
        hidden_grad[None],
        gain_owned,
        w_owned[:, : 2 * inner].reshape(owned, 2, inner),
        w_owned[:, 2 * inner + 2 * state_size : 2 * inner + 2 * state_size + heads],
        bc_owned,
        conv_sum[:taps, :inner],
        conv_sum[taps, :inner],
        conv_bc[:taps],
        conv_bc[taps],
        rest[2 * inner : 2 * inner + heads],
        rest[2 * inner + LANES : 2 * inner + LANES + heads],
        jnp.sum(rest[inner : 2 * inner].reshape(heads, head_size), 1),
        rest[:inner],
        wo_owned.T,
    )


def solution(mesh):
    placed = (
        P("fsdp", "ctx", None),
        P("fsdp", "ctx"),
        P("fsdp", "ctx", None),
        P(("fsdp", "ctx")),
        P(("fsdp", "ctx"), None, "tp"),
        P(("fsdp", "ctx"), "tp"),
        P(("fsdp", "ctx"), None, None),
        P(None, "tp"),
        P("tp"),
        P(),
        P(),
        P("tp"),
        P("tp"),
        P("tp"),
        P("tp"),
        P("tp", ("fsdp", "ctx")),
    )
    return jax.shard_map(
        body,
        mesh=mesh,
        in_specs=placed,
        out_specs=(
            P("fsdp", "ctx", None),
            P("fsdp", "ctx", None),
            P(("fsdp", "ctx")),
            P(("fsdp", "ctx"), None, "tp"),
            P(("fsdp", "ctx"), "tp"),
            P(("fsdp", "ctx"), None, None),
            P(None, "tp"),
            P("tp"),
            P(),
            P(),
            P("tp"),
            P("tp"),
            P("tp"),
            P("tp"),
            P("tp", ("fsdp", "ctx")),
        ),
        check_vma=False,
    )
```

```python
import functools

import jax
import jax.numpy as jnp
from jax import lax
from jax.experimental import pallas as pl
from jax.experimental.pallas import tpu as pltpu
from jax.sharding import PartitionSpec as P

CHUNK = 128
STEP = 256
SUB = STEP // CHUNK
LANES = 128
EDGE = 16
GROUPS = 2
EPSILON = 1e-05
EXACT = lax.Precision.HIGHEST
F32 = jnp.float32
BF16 = jnp.bfloat16
NEGATIVE = -1e30
M1, M2, M3, ENTRY, TAIL, SEG, RAW = 16, 17, 18, 19, 20, 21, 24
VMEM_LIMIT = 56 * 1024 * 1024


def nn(a, b):
    return lax.dot_general(a, b, (((1,), (0,)), ((), ())), preferred_element_type=F32)


def nt(a, b):
    return lax.dot_general(a, b, (((1,), (1,)), ((), ())), preferred_element_type=F32)


def tn(a, b):
    return nn(a.T, b)


def exact(a, b):
    return lax.dot_general(
        a, b, (((1,), (0,)), ((), ())), precision=EXACT, preferred_element_type=F32
    )


def lasts(microseconds):
    return pl.CostEstimate(
        flops=0, bytes_accessed=int(microseconds * 3.69e6), transcendentals=0
    )


ANYWHERE = pl.BlockSpec(memory_space=pl.ANY)


def ordered(kernel, inputs, after):
    def run(*refs):
        kernel(*refs[:inputs], *refs[inputs + after :])

    return run


def iota(shape, dim):
    return lax.broadcasted_iota(jnp.int32, shape, dim)


def spread(per_head, pairs):
    rows = per_head.shape[0]
    low = iota((rows, LANES), 1) < LANES // 2
    parts = []
    for j in range(pairs):
        left = jnp.broadcast_to(per_head[:, 2 * j : 2 * j + 1], (rows, LANES))
        right = jnp.broadcast_to(per_head[:, 2 * j + 1 : 2 * j + 2], (rows, LANES))
        parts.append(jnp.where(low, left, right))
    return jnp.concatenate(parts, 1)


def halves(block):
    low = iota(block.shape, 1) < LANES // 2
    zero = jnp.zeros_like(block)
    return jnp.where(low, block, zero), jnp.where(low, zero, block)


def silu(v):
    return v * jax.nn.sigmoid(v)


def rms_unit(x):
    return x * lax.rsqrt(jnp.mean(x * x, -1, keepdims=True) + EPSILON)


def front_kernel(
    gain_lane, starts, hid, edge, tok, cw, dtp, *refs
):
    (normed, gate, pre_out, u_out, rec, st, pdx, fin, pdfin, w, gain_out,
     buf, state, decay) = refs[-14:]
    shards = refs[:-14]
    inner = gate.shape[1]
    wide = pre_out.shape[1]
    pairs = inner // LANES
    at = pl.program_id(0)

    @pl.when(at == 0)
    def _():
        for k, shard in enumerate(shards):
            size = shard.shape[0]
            w[pl.ds(pl.multiple_of(starts[k], 16), size), :] = shard[...]
        for k in range(w.shape[0] // LANES):
            tile = w[k * LANES : (k + 1) * LANES, inner + wide :].astype(F32).T
            gain_out[:, k * LANES : (k + 1) * LANES] = jnp.broadcast_to(
                tile[gain_lane : gain_lane + 1, :], (8, LANES)
            )
        edge_low = (rms_unit(edge[...].astype(F32)) * gain_out[0:1, :]).astype(BF16)
        edge_pre = nn(edge_low, w[:, inner : inner + wide])
        buf[0:8, :] = edge_pre[EDGE - 8 :, :]
        state[...] = jnp.zeros_like(state)
        decay[...] = jnp.ones_like(decay)

    @pl.when(at > 0)
    def _():
        buf[0:8, :] = buf[STEP : STEP + 8, :]

    low = (rms_unit(hid[...].astype(F32)) * gain_out[0:1, :]).astype(BF16)
    normed[...] = low
    gate[...] = nn(low, w[:, :inner])
    pre = nn(low, w[:, inner : inner + wide])
    pre_out[...] = pre
    buf[8 : 8 + STEP, :] = pre
    raw_all = nn(low, w[:, inner + wide :]) + dtp[0:1, :]
    marks = tok[...]
    u = cw[3:4, :] * pre + cw[4:5, :]
    u = u + cw[2:3, :] * (buf[7 : 7 + STEP, :] * marks[:, M1 : M1 + 1])
    u = u + cw[1:2, :] * (buf[6 : 6 + STEP, :] * marks[:, M2 : M2 + 1])
    u = u + cw[0:1, :] * (buf[5 : 5 + STEP, :] * marks[:, M3 : M3 + 1])
    u_out[...] = u
    act = silu(u)
    step_all = jax.nn.softplus(raw_all)
    lane = iota((CHUNK, LANES), 1)
    lower = (iota((CHUNK, CHUNK), 0) >= iota((CHUNK, CHUNK), 1)).astype(F32)
    for i in range(SUB):
        rows = slice(i * CHUNK, (i + 1) * CHUNK)
        step = step_all[rows]
        cum = exact(lower, step * dtp[1:2, :])
        mark = marks[rows]
        rec[rows, :] = jnp.where(
            lane < 8, cum, jnp.where(lane < 16, step, jnp.where(lane < 24, mark, raw_all[rows]))
        )
        last = cum[CHUNK - 1 :, :]
        tail = mark[:, TAIL : TAIL + 1] * jnp.exp(last - cum) * step
        fed = (act[rows, :inner] * spread(tail, pairs)).astype(BF16)
        st[i] = state[...]
        pdx[8 * i : 8 * i + 8, :] = decay[...]
        passed = spread(mark[CHUNK - 1 :, ENTRY : ENTRY + 1] * jnp.exp(last), pairs)
        input_b = act[rows, inner : inner + LANES].T.astype(BF16)
        state[...] = passed * state[...] + nn(input_b, fed)
        decay[...] = decay[...] * passed
    fin[...] = state[...]
    pdfin[...] = decay[...]


def front(hidden, edge, tok, shards, starts, gain_lane, cw, dtp, inner, wide):
    rows, width = hidden.shape
    packed = shards[0].shape[1]
    steps = rows // STEP
    state_size = LANES

    def whole(a):
        return pl.BlockSpec(a.shape, lambda i: (0,) * a.ndim)

    def tall(cols):
        return pl.BlockSpec((STEP, cols), lambda i: (i, 0))

    chunks = rows // CHUNK
    return pl.pallas_call(
        functools.partial(front_kernel, gain_lane),
        grid=(steps,),
        in_specs=[
            pl.BlockSpec(memory_space=pltpu.SMEM),
            tall(width),
            whole(edge),
            tall(LANES),
            whole(cw),
            whole(dtp),
        ]
        + [whole(shard) for shard in shards],
        out_specs=[
            tall(width),
            tall(inner),
            tall(wide),
            tall(wide),
            tall(LANES),
            pl.BlockSpec((SUB, state_size, inner), lambda i: (i, 0, 0)),
            pl.BlockSpec((8 * SUB, inner), lambda i: (i, 0)),
            pl.BlockSpec((state_size, inner), lambda i: (0, 0)),
            pl.BlockSpec((8, inner), lambda i: (0, 0)),
            pl.BlockSpec((width, packed), lambda i: (0, 0)),
            pl.BlockSpec((8, width), lambda i: (0, 0)),
        ],
        out_shape=[
            jax.ShapeDtypeStruct((rows, width), BF16),
            jax.ShapeDtypeStruct((rows, inner), F32),
            jax.ShapeDtypeStruct((rows, wide), F32),
            jax.ShapeDtypeStruct((rows, wide), F32),
            jax.ShapeDtypeStruct((rows, LANES), F32),
            jax.ShapeDtypeStruct((chunks, state_size, inner), F32),
            jax.ShapeDtypeStruct((8 * chunks, inner), F32),
            jax.ShapeDtypeStruct((state_size, inner), F32),
            jax.ShapeDtypeStruct((8, inner), F32),
            jax.ShapeDtypeStruct((width, packed), BF16),
            jax.ShapeDtypeStruct((8, width), F32),
        ],
        scratch_shapes=[
            pltpu.VMEM((STEP + 8, wide), F32),
            pltpu.VMEM((state_size, inner), F32),
            pltpu.VMEM((8, inner), F32),
        ],
        compiler_params=pltpu.CompilerParams(
            dimension_semantics=("arbitrary",), vmem_limit_bytes=VMEM_LIMIT
        ),
        cost_estimate=lasts(0.01),
        name="front",
    )(starts, hidden, edge, tok, cw, dtp, *shards)


def middle_kernel(
    u, rec, gate, st, pdx, sin, og, wo, prm,
    scan, dgate, sums, *parts,
):
    inner = gate.shape[1]
    pairs = inner // LANES
    d_gate = nn(og[...], wo[...])
    dgate[...] = d_gate
    act = silu(u[...])
    below = iota((CHUNK, CHUNK), 0) >= iota((CHUNK, CHUNK), 1)
    for i in range(SUB):
        rows = slice(i * CHUNK, (i + 1) * CHUNK)
        record = rec[rows, :]
        turned = record.T
        state = (st[i] + pdx[8 * i : 8 * i + 1, :] * sin[...]).astype(BF16)
        x = act[rows, :inner]
        input_b = act[rows, inner : inner + LANES].astype(BF16)
        input_c = act[rows, inner + LANES :].astype(BF16)
        scores = nt(input_c, input_b)
        barred = jnp.where(
            below & (record[:, SEG : SEG + 1] == turned[SEG : SEG + 1, :]), 0.0, NEGATIVE
        )
        entry = record[:, ENTRY : ENTRY + 1] * jnp.exp(record)
        outs = []
        for j in range(pairs):
            block = x[:, j * LANES : (j + 1) * LANES].astype(BF16)
            total = None
            for k, side in enumerate(halves(block)):
                h = 2 * j + k
                link = jnp.exp(record[:, h : h + 1] - turned[h : h + 1, :] + barred)
                weight = (scores * link * turned[8 + h : 9 + h, :]).astype(BF16)
                term = nn(weight, side)
                total = term if total is None else total + term
            outs.append(total)
        y = jnp.concatenate(outs, 1)
        y = y + nn(input_c, state) * spread(entry, pairs) + prm[0:1, :] * x
        scan[rows, :] = y
    gated = scan[...] * silu(gate[...])
    scaled = gated * prm[1:2, :]
    squares = jnp.sum(gated * gated, -1, keepdims=True)
    crosses = jnp.sum(scaled * d_gate, -1, keepdims=True)
    lane = iota((STEP, LANES), 1)
    both = jnp.where(lane == 0, squares, jnp.where(lane == 1, crosses, 0.0))
    sums[...] = both.T[0:8, :]
    part_low = nt(scaled.astype(BF16), wo[...]).astype(BF16)
    steps_each = pl.num_programs(0) // len(parts)
    for k, part in enumerate(parts):

        @pl.when(pl.program_id(0) // steps_each == k)
        def _():
            part[...] = part_low


def middle(u, rec, gate, st, pdx, sin, og, wo, prm):
    rows, inner = gate.shape
    width = og.shape[1]
    steps = rows // STEP
    each = steps // GROUPS

    def whole(a):
        return pl.BlockSpec(a.shape, lambda i: (0,) * a.ndim)

    def tall(cols):
        return pl.BlockSpec((STEP, cols), lambda i: (i, 0))

    def part(k):
        return pl.BlockSpec((STEP, width), lambda i: (jnp.clip(i - k * each, 0, each - 1), 0))

    return pl.pallas_call(
        middle_kernel,
        grid=(steps,),
        in_specs=[
            tall(u.shape[1]),
            tall(LANES),
            tall(inner),
            pl.BlockSpec((SUB,) + st.shape[1:], lambda i: (i, 0, 0)),
            pl.BlockSpec((8 * SUB, inner), lambda i: (i, 0)),
            whole(sin),
            tall(width),
            whole(wo),
            whole(prm),
        ],
        out_specs=[
            tall(inner),
            tall(inner),
            pl.BlockSpec((8, STEP), lambda i: (0, i)),
        ]
        + [part(k) for k in range(GROUPS)],
        out_shape=[
            jax.ShapeDtypeStruct((rows, inner), F32),
            jax.ShapeDtypeStruct((rows, inner), F32),
            jax.ShapeDtypeStruct((8, rows), F32),
        ]
        + [jax.ShapeDtypeStruct((rows // GROUPS, width), BF16)] * GROUPS,
        compiler_params=pltpu.CompilerParams(
            dimension_semantics=("arbitrary",), vmem_limit_bytes=VMEM_LIMIT
        ),
        cost_estimate=lasts(0.01),
        name="middle",
    )(u, rec, gate, st, pdx, sin, og, wo, prm)


def turn_kernel(
    inner_total, scan, gate, dgate, sums, upre_c, rec, prm,
    dscan, dgr, glow, adj, psx, fin, gain_grad,
    state, decay,
):
    inner = gate.shape[1]
    pairs = inner // LANES
    at = pl.program_id(0)

    @pl.when(at == 0)
    def _():
        state[...] = jnp.zeros_like(state)
        decay[...] = jnp.ones_like(decay)
        gain_grad[...] = jnp.zeros_like(gain_grad)

    head = sums[...]
    column = jnp.concatenate([head, jnp.zeros((LANES - 8, STEP), F32)], 0).T
    inv = lax.rsqrt(column[:, 0:1] / inner_total + EPSILON)
    cube = inv * inv * inv * (column[:, 1:2] / inner_total)
    raw = gate[...]
    sig = jax.nn.sigmoid(raw)
    sil = raw * sig
    y = scan[...]
    gated = y * sil
    unit = gated * inv
    d_gate = dgate[...]
    gain = prm[1:2, :]
    glow[...] = (unit * gain).astype(BF16)
    gain_grad[...] += jnp.broadcast_to(jnp.sum(d_gate * unit, 0, keepdims=True), gain_grad.shape)
    d_gated = inv * gain * d_gate - gated * cube
    d_scan = d_gated * sil
    dscan[...] = d_scan
    dgr[...] = (d_gated * y * (sig * (1.0 + raw * (1.0 - sig)))).astype(BF16)
    input_c = silu(upre_c[...])
    for i in reversed(range(SUB)):
        rows = slice(i * CHUNK, (i + 1) * CHUNK)
        record = rec[rows, :]
        entry = record[:, ENTRY : ENTRY + 1] * jnp.exp(record)
        adj[i] = state[...]
        psx[8 * i : 8 * i + 8, :] = decay[...]
        passed = spread(entry[CHUNK - 1 :, :], pairs)
        fed = (d_scan[rows] * spread(entry, pairs)).astype(BF16)
        state[...] = passed * state[...] + nn(input_c[rows].T.astype(BF16), fed)
        decay[...] = decay[...] * passed
    fin[...] = state[...]


def turn(scan, gate, dgate, sums, u, rec, prm, inner_total):
    rows, inner = scan.shape
    steps = rows // STEP
    chunks = rows // CHUNK
    state_size = LANES
    c_block = u.shape[1] // LANES - 1

    def whole(a):
        return pl.BlockSpec(a.shape, lambda i: (0,) * a.ndim)

    def tall(cols):
        return pl.BlockSpec((STEP, cols), lambda i: (steps - 1 - i, 0))

    return pl.pallas_call(
        functools.partial(turn_kernel, float(inner_total)),
        grid=(steps,),
        in_specs=[
            tall(inner),
            tall(inner),
            tall(inner),
            pl.BlockSpec((8, STEP), lambda i: (0, steps - 1 - i)),
            pl.BlockSpec((STEP, LANES), lambda i: (steps - 1 - i, c_block)),
            tall(LANES),
            whole(prm),
        ],
        out_specs=[
            tall(inner),
            tall(inner),
            tall(inner),
            pl.BlockSpec((SUB, state_size, inner), lambda i: (steps - 1 - i, 0, 0)),
            pl.BlockSpec((8 * SUB, inner), lambda i: (steps - 1 - i, 0)),
            pl.BlockSpec((state_size, inner), lambda i: (0, 0)),
            pl.BlockSpec((8, inner), lambda i: (0, 0)),
        ],
        out_shape=[
            jax.ShapeDtypeStruct((rows, inner), F32),
            jax.ShapeDtypeStruct((rows, inner), BF16),
            jax.ShapeDtypeStruct((rows, inner), BF16),
            jax.ShapeDtypeStruct((chunks, state_size, inner), F32),
            jax.ShapeDtypeStruct((8 * chunks, inner), F32),
            jax.ShapeDtypeStruct((state_size, inner), F32),
            jax.ShapeDtypeStruct((8, inner), F32),
        ],
        scratch_shapes=[pltpu.VMEM((state_size, inner), F32), pltpu.VMEM((8, inner), F32)],
        compiler_params=pltpu.CompilerParams(
            dimension_semantics=("arbitrary",), vmem_limit_bytes=VMEM_LIMIT
        ),
        cost_estimate=lasts(0.01),
        name="turn",
    )(scan, gate, dgate, sums, u, rec, prm)


def back_kernel(
    u, rec, dscan, st, pdx, sin, adj, psx, ain, prm, dtp,
    dpre, dstep, skip_acc, head_acc,
):
    inner = dscan.shape[1]
    pairs = inner // LANES
    heads = 2 * pairs

    @pl.when(pl.program_id(0) == 0)
    def _():
        skip_acc[...] = jnp.zeros_like(skip_acc)
        head_acc[...] = jnp.zeros_like(head_acc)

    raw = u[...]
    sig = jax.nn.sigmoid(raw)
    act = raw * sig
    slope = sig * (1.0 + raw * (1.0 - sig))
    above = iota((CHUNK, CHUNK), 0) <= iota((CHUNK, CHUNK), 1)
    upper = above.astype(F32)
    lane = iota((CHUNK, LANES), 1)
    gather_heads = (iota((inner, LANES), 0) // (LANES // 2) == iota((inner, LANES), 1)).astype(BF16)
    nega = dtp[1:2, :]
    for i in range(SUB):
        rows = slice(i * CHUNK, (i + 1) * CHUNK)
        record = rec[rows, :]
        turned = record.T
        state = st[i] + pdx[8 * i : 8 * i + 1, :] * sin[...]
        state_low = state.astype(BF16)
        later = adj[i] + psx[8 * i : 8 * i + 1, :] * ain[...]
        later_low = later.astype(BF16)
        x = act[rows, :inner]
        b_wide = act[rows, inner : inner + LANES]
        c_wide = act[rows, inner + LANES :]
        input_b = b_wide.astype(BF16)
        input_c = c_wide.astype(BF16)
        dy = dscan[rows, :]
        scores = nt(input_b, input_c)
        barred = jnp.where(
            above & (record[:, SEG : SEG + 1] == turned[SEG : SEG + 1, :]), 0.0, NEGATIVE
        )
        step = pltpu.roll(record, LANES - 8, axis=1)
        z = pltpu.roll(record, LANES - RAW, axis=1)
        d_scores = jnp.zeros((CHUNK, CHUNK), F32)
        direct = jnp.zeros((CHUNK, LANES), F32)
        arrivals = []
        dxs = []
        for j in range(pairs):
            cols = slice(j * LANES, (j + 1) * LANES)
            x_sides = halves(x[:, cols].astype(BF16))
            dy_pair = dy[:, cols].astype(BF16)
            dy_sides = halves(dy_pair)
            total = None
            for k in range(2):
                h = 2 * j + k
                step_col = record[:, 8 + h : 9 + h]
                link = jnp.exp(turned[h : h + 1, :] - record[:, h : h + 1] + barred)
                d_link = nt(x_sides[k], dy_pair) * link
                d_scaled = d_link * step_col
                d_scores = d_scores + d_scaled
                flow = d_scaled * scores
                arrivals.append(jnp.sum(flow, 0, keepdims=True))
                given = jnp.sum(d_link * scores, 1, keepdims=True)
                direct = jnp.where(lane == h, given, direct)
                weight = (scores * link * step_col).astype(BF16)
                term = nn(weight, dy_sides[k])
                total = term if total is None else total + term
            dxs.append(total)
        dx = jnp.concatenate(dxs, 1)
        arrived = jnp.concatenate(arrivals + [jnp.zeros((CHUNK - heads, CHUNK), F32)], 0).T
        decay_in = record[:, ENTRY : ENTRY + 1] * jnp.exp(record)
        last = record[CHUNK - 1 :, :]
        tail_exp = record[:, TAIL : TAIL + 1] * jnp.exp(last - record)
        tail = tail_exp * step
        tail_wide = spread(jnp.where(lane < 8, tail, 0.0), pairs)
        fed_back = (dy * spread(decay_in, pairs)).astype(BF16)
        fed = (x * tail_wide).astype(BF16)
        from_state = nn(input_c, state_low)
        d_fed = nn(input_b, later_low)
        d_score_low = d_scores.astype(BF16)
        d_c = nt(fed_back, state_low) + nn(d_scores.T.astype(BF16), input_b)
        d_b = nt(fed, later_low) + nn(d_score_low, input_c)
        d_entry = nn((dy * from_state).astype(BF16), gather_heads)
        d_tail = nn((x * d_fed).astype(BF16), gather_heads)
        through = jnp.broadcast_to(jnp.sum(later * state, 0, keepdims=True), (16, inner))
        d_through = nn(through.astype(BF16), gather_heads)[0:1, :]
        dx = dx + d_fed * tail_wide + prm[0:1, :] * dy
        tail_flow = d_tail * tail
        d_cum = arrived - direct * step + d_entry * decay_in - tail_flow
        d_cum = jnp.where(lane < 8, d_cum, 0.0)
        d_last = jnp.sum(tail_flow, 0, keepdims=True) + decay_in[CHUNK - 1 :, :] * d_through
        d_rate = exact(upper, d_cum) + jnp.where(lane < 8, d_last, 0.0)
        d_step = direct + d_tail * tail_exp + nega * d_rate
        d_z = jnp.where(lane < 8, d_step * jax.nn.sigmoid(z), 0.0)
        dstep[rows, :] = d_z.astype(BF16)
        dpre[rows, :] = jnp.concatenate([dx, d_b, d_c], 1) * slope[rows]
        skip_acc[...] += jnp.broadcast_to(jnp.sum(dy * x, 0, keepdims=True), skip_acc.shape)
        head_acc[0:1, :] += jnp.sum(d_z, 0, keepdims=True)
        head_acc[1:2, :] += jnp.sum(
            jnp.where(lane < 8, d_rate * (nega * step), 0.0), 0, keepdims=True
        )


def back(u, rec, dscan, st, pdx, sin, adj, psx, ain, prm, dtp, after, group):
    rows, wide = u.shape
    inner = dscan.shape[1]
    steps = rows // STEP // GROUPS
    first = group * steps

    def whole(a):
        return pl.BlockSpec(a.shape, lambda i: (0,) * a.ndim)

    def tall(cols):
        return pl.BlockSpec((STEP, cols), lambda i: (first + i, 0))

    def out_tall(cols):
        return pl.BlockSpec((STEP, cols), lambda i: (i, 0))

    def states(at):
        return pl.BlockSpec((SUB,) + st.shape[1:], lambda i: (at + i, 0, 0))

    def decays(at):
        return pl.BlockSpec((8 * SUB, inner), lambda i: (at + i, 0))

    return pl.pallas_call(
        ordered(back_kernel, 11, len(after)),
        grid=(steps,),
        in_specs=[
            tall(wide),
            tall(LANES),
            tall(inner),
            states(first),
            decays(first),
            whole(sin),
            states(first),
            decays(first),
            whole(ain),
            whole(prm),
            whole(dtp),
        ]
        + [ANYWHERE] * len(after),
        out_specs=[
            out_tall(wide),
            out_tall(LANES),
            pl.BlockSpec((8, inner), lambda i: (0, 0)),
            pl.BlockSpec((8, LANES), lambda i: (0, 0)),
        ],
        out_shape=[
            jax.ShapeDtypeStruct((steps * STEP, wide), F32),
            jax.ShapeDtypeStruct((steps * STEP, LANES), BF16),
            jax.ShapeDtypeStruct((8, inner), F32),
            jax.ShapeDtypeStruct((8, LANES), F32),
        ],
        compiler_params=pltpu.CompilerParams(
            dimension_semantics=("arbitrary",), vmem_limit_bytes=VMEM_LIMIT
        ),
        cost_estimate=lasts(0.01),
        name="back",
    )(u, rec, dscan, st, pdx, sin, adj, psx, ain, prm, dtp, *after)


def rear_kernel(
    dpre, rec, pre, dgr, dstep, follow, w, cw,
    dproj, dnorm, conv_acc,
    buf, mbuf,
):
    wide = dpre.shape[1]
    inner = dgr.shape[1]

    @pl.when(pl.program_id(0) == 0)
    def _():
        buf[STEP : STEP + 8, :] = follow[:, :wide]
        mbuf[STEP : STEP + 8, :] = follow[:, wide:]
        conv_acc[...] = jnp.zeros_like(conv_acc)

    @pl.when(pl.program_id(0) > 0)
    def _():
        buf[STEP : STEP + 8, :] = buf[0:8, :]
        mbuf[STEP : STEP + 8, :] = mbuf[0:8, :]

    grad = dpre[...]
    buf[0:STEP, :] = grad
    mbuf[0:STEP, :] = rec[...]
    value = pre[...]
    total = cw[3:4, :] * grad
    conv_acc[3:4, :] += jnp.sum(value * grad, 0, keepdims=True)
    conv_acc[4:5, :] += jnp.sum(grad, 0, keepdims=True)
    for shift in (1, 2, 3):
        mark = mbuf[shift : shift + STEP, :][:, M1 + shift - 1 : M1 + shift]
        moved = buf[shift : shift + STEP, :] * mark
        total = total + cw[3 - shift : 4 - shift, :] * moved
        conv_acc[3 - shift : 4 - shift, :] += jnp.sum(value * moved, 0, keepdims=True)
    dproj[:, :inner] = dgr[...]
    dproj[:, inner : inner + wide] = total.astype(BF16)
    dproj[:, inner + wide :] = dstep[...]
    dnorm[...] = nt(dproj[...], w[...]).astype(BF16)


def rear(dpre, rec, pre, dgr, dstep, follow, w, cw, after, group):
    rows, wide = dpre.shape
    steps = rows // STEP
    inner = dgr.shape[1]
    width, packed = w.shape
    first = group * steps

    def whole(a):
        return pl.BlockSpec(a.shape, lambda i: (0,) * a.ndim)

    def tall(cols):
        return pl.BlockSpec((STEP, cols), lambda i: (first + steps - 1 - i, 0))

    def own(cols):
        return pl.BlockSpec((STEP, cols), lambda i: (steps - 1 - i, 0))

    return pl.pallas_call(
        ordered(rear_kernel, 8, len(after)),
        grid=(steps,),
        in_specs=[
            own(wide),
            tall(LANES),
            tall(wide),
            tall(inner),
            own(LANES),
            whole(follow),
            whole(w),
            whole(cw),
        ]
        + [ANYWHERE] * len(after),
        out_specs=[
            own(packed),
            own(width),
            pl.BlockSpec((8, wide), lambda i: (0, 0)),
        ],
        out_shape=[
            jax.ShapeDtypeStruct((rows, packed), BF16),
            jax.ShapeDtypeStruct((rows, width), BF16),
            jax.ShapeDtypeStruct((8, wide), F32),
        ],
        scratch_shapes=[
            pltpu.VMEM((STEP + 8, wide), F32),
            pltpu.VMEM((STEP + 8, LANES), F32),
        ],
        compiler_params=pltpu.CompilerParams(
            dimension_semantics=("arbitrary",), vmem_limit_bytes=VMEM_LIMIT
        ),
        cost_estimate=lasts(0.01),
        name="rear",
    )(dpre, rec, pre, dgr, dstep, follow, w, cw, *after)


def settle_kernel(inner_total, hid, sums, given, held, outer, filled, out, *handed):
    column = jnp.concatenate([sums[...], jnp.zeros((LANES - 8, STEP), F32)], 0).T
    inv = lax.rsqrt(column[:, 0:1] / inner_total + EPSILON)
    total = jnp.where(outer[0:1, 0:1] > 0.0, given[...].astype(F32), held[...].astype(F32))
    out[...] = (hid[...].astype(F32) + inv * total).astype(BF16)


def finish_kernel(hid, cot, gain, given, held, outer, filled, out, *handed):
    x = hid[...].astype(F32)
    inv = lax.rsqrt(jnp.mean(x * x, -1, keepdims=True) + EPSILON)
    total = jnp.where(outer[0:1, 0:1] > 0.0, given[...].astype(F32), held[...].astype(F32))
    scaled = total * gain[0:1, :]
    cross = jnp.mean(scaled * x, -1, keepdims=True)
    out[...] = cot[...].astype(F32) + inv * scaled - x * (inv * inv * inv * cross)


def by_group(kernel, out_like, dtype, group, fresh, operands, filled, after, name, held=()):
    rows, width = out_like.shape
    steps = rows // GROUPS // STEP
    first = group * steps
    specs = {
        "all": lambda a: pl.BlockSpec((STEP, a.shape[1]), lambda i: (first + i, 0)),
        "group": lambda a: pl.BlockSpec((STEP, a.shape[1]), lambda i: (i, 0)),
        "columns": lambda a: pl.BlockSpec((8, STEP), lambda i: (0, first + i)),
        "whole": lambda a: pl.BlockSpec(a.shape, lambda i: (0, 0)),
    }
    count = len(operands) + 1
    aliases = {} if fresh else {count - 1: 0}
    aliases.update({count + len(after) + k: 1 + k for k in range(len(held))})
    out, *handed = pl.pallas_call(
        ordered(kernel, count, len(after) + len(held)),
        grid=(steps,),
        in_specs=[specs[kind](a) for a, kind in operands]
        + [ANYWHERE] * (1 + len(after) + len(held)),
        out_specs=[pl.BlockSpec((STEP, width), lambda i: (first + i, 0))]
        + [ANYWHERE] * len(held),
        out_shape=[jax.ShapeDtypeStruct((rows, width), dtype)]
        + [jax.ShapeDtypeStruct(a.shape, a.dtype) for a in held],
        input_output_aliases=aliases,
        compiler_params=pltpu.CompilerParams(
            dimension_semantics=("arbitrary",), vmem_limit_bytes=VMEM_LIMIT
        ),
        cost_estimate=lasts(0.01),
        name=name,
    )(*[a for a, _ in operands], filled, *after, *held)
    return (out, handed) if held else out


def passed_along(value, axis, steps):
    count = lax.axis_size(axis)
    leading, last = (max(0, -steps), min(count, count - steps))
    return lax.ppermute(value, axis, [(source, source + steps) for source in range(leading, last)])


def chained(own, decay, axis, steps):
    entering = jnp.zeros_like(own)
    for turn_at in range(lax.axis_size(axis) - 1):
        leaving = own if turn_at == 0 else own + decay * entering
        entering = passed_along(leaving, axis, steps)
    return entering


def butterfly_sum(value, axis):
    bit = 1
    while bit < lax.axis_size(axis):
        pairs = [(i, i ^ bit) for i in range(lax.axis_size(axis))]
        value = value + lax.ppermute(value, axis, pairs)
        bit *= 2
    return value


def join_kernel(pairs, *refs):
    outs = refs[2 * pairs :]
    for k in range(pairs):
        left, right, out = refs[2 * k], refs[2 * k + 1], outs[k]
        out[...] = (left[...].astype(F32) + right[...].astype(F32)).astype(out.dtype)


def join(pairs, after, held=()):
    rows, width = pairs[0][0].shape
    spec = pl.BlockSpec((STEP, width), lambda i: (i, 0))
    return pl.pallas_call(
        ordered(
            functools.partial(join_kernel, len(pairs)), 2 * len(pairs), len(after) + len(held)
        ),
        grid=(rows // STEP,),
        in_specs=[spec] * (2 * len(pairs)) + [ANYWHERE] * (len(after) + len(held)),
        out_specs=[spec] * len(pairs) + [ANYWHERE] * len(held),
        out_shape=[jax.ShapeDtypeStruct((rows, width), BF16)] * len(pairs)
        + [jax.ShapeDtypeStruct(a.shape, a.dtype) for a in held],
        input_output_aliases={
            2 * len(pairs) + len(after) + k: len(pairs) + k for k in range(len(held))
        },
        compiler_params=pltpu.CompilerParams(
            dimension_semantics=("arbitrary",), vmem_limit_bytes=VMEM_LIMIT
        ),
        cost_estimate=lasts(0.01),
        name="join",
    )(*[a for pair in pairs for a in pair], *after, *held)


def trade_kernel(pairs, *refs):
    own, outer = refs[2 * pairs], refs[2 * pairs + 1]
    outs = refs[2 * pairs + 2 :]
    for k in range(pairs):
        left, right = refs[2 * k], refs[2 * k + 1]
        total = left[...].astype(F32) + right[...].astype(F32)
        outs[k][...] = total.astype(BF16)
    outs[pairs][...] = jnp.where(outer[0:1, 0:1] > 0.0, own[...].astype(F32), total).astype(BF16)


def trade(pairs, own, outer, after):
    rows, width = own.shape
    spec = pl.BlockSpec((STEP, width), lambda i: (i, 0))
    flag = pl.BlockSpec(outer.shape, lambda i: (0, 0))
    count = len(pairs)
    return pl.pallas_call(
        ordered(functools.partial(trade_kernel, count), 2 * count + 2, len(after)),
        grid=(rows // STEP,),
        in_specs=[spec] * (2 * count + 1) + [flag] + [ANYWHERE] * len(after),
        out_specs=[spec] * (count + 1),
        out_shape=[jax.ShapeDtypeStruct((rows, width), BF16)] * (count + 1),
        compiler_params=pltpu.CompilerParams(
            dimension_semantics=("arbitrary",), vmem_limit_bytes=VMEM_LIMIT
        ),
        cost_estimate=lasts(0.01),
        name="trade",
    )(*[a for pair in pairs for a in pair], own, outer, *after)


class LineSum:
    def __init__(self, value, come=None):
        self.own = value
        self.come = lax.ppermute(value, "tp", [(0, 1), (3, 2)]) if come is None else come
        self.near = self.across = self.given = None

    def pair(self):
        return (self.own if self.near is None else self.near, self.come)

    def joined(self, value):
        if self.near is None:
            self.near = value
            self.come = lax.ppermute(value, "tp", [(1, 2), (2, 1)])
        else:
            self.across = value
            self.given = lax.ppermute(value, "tp", [(1, 0), (2, 3)])


def advance_and_begin(sums, value, outer, after):
    *outs, both = trade([one.pair() for one in sums], value, outer, after)
    for one, out in zip(sums[:-1], outs):
        one.joined(out)
    sums[-1].across = outs[-1]
    come = lax.ppermute(both, "tp", [(0, 1), (1, 0), (2, 3), (3, 2)])
    sums[-1].given = come
    return LineSum(value, come), tuple(outs)


def advance(sums, after, held=()):
    outs = join([one.pair() for one in sums], after, held)
    for one, value in zip(sums, outs):
        one.joined(value)
    return tuple(outs)


def total_kernel(own, one, two, three, *refs):
    out = refs[len(refs) // 2]
    out[...] = (own[...] + one[...]) + (two[...] + three[...])


def total_over_row(own, held):
    others = [lax.ppermute(own, "tp", [(i, i ^ bits) for i in range(4)]) for bits in (1, 2, 3)]
    spec = pl.BlockSpec(own.shape, lambda i: (0, 0))
    return pl.pallas_call(
        total_kernel,
        grid=(1,),
        in_specs=[spec] * 4 + [ANYWHERE] * len(held),
        out_specs=[spec] + [ANYWHERE] * len(held),
        out_shape=[jax.ShapeDtypeStruct(own.shape, own.dtype)]
        + [jax.ShapeDtypeStruct(a.shape, a.dtype) for a in held],
        input_output_aliases={4 + k: 1 + k for k in range(len(held))},
        cost_estimate=lasts(0.01),
        name="total",
    )(own, *others, *held)


def other_core_kernel(place, w, wo, out):
    packed = w.shape[1]
    out[:, :packed] = w[...].astype(BF16)
    out[:, packed:] = wo[...].astype(BF16)


def split_kernel(
    place, w_ka, w_sa, w_kb, w_sb, wo_kb, wo_sb, r_ka, r_sa, r_kb, r_sb,
    keep_a, send_a, keep_b, send_b,
):
    cut, packed = keep_a.shape[1], w_ka.shape[1]
    keep_a[...] = w_ka[:, :cut] + r_ka[:, :cut].astype(F32)
    send_a[...] = (w_sa[:, :cut] + r_sa[:, :cut].astype(F32)).astype(BF16)
    for w, wo, r, out in ((w_kb, wo_kb, r_kb, keep_b), (w_sb, wo_sb, r_sb, send_b)):
        out[:, : packed - cut] = (w[:, cut:] + r[:, cut:packed].astype(F32)).astype(out.dtype)
        out[:, packed - cut :] = (wo[...] + r[:, packed:].astype(F32)).astype(out.dtype)


def second_kernel(place, ka, ra, sa, rsa, kb, rb, sb, rsb, keep_a, send_a, keep_b, send_b):
    keep_a[...] = ka[...] + ra[...].astype(F32)
    send_a[...] = (sa[...] + rsa[...].astype(F32)).astype(BF16)
    keep_b[...] = kb[...] + rb[...].astype(F32)
    send_b[...] = (sb[...] + rsb[...].astype(F32)).astype(BF16)


def placed_call(kernel, steps, place, inputs, outputs, name, after=()):
    return pl.pallas_call(
        ordered(kernel, 1 + len(inputs), len(after)),
        grid_spec=pltpu.PrefetchScalarGridSpec(
            num_scalar_prefetch=1,
            grid=(steps,),
            in_specs=[
                pl.BlockSpec((LANES, a.shape[1]), functools.partial(lambda f, i, p: (f(i, p), 0), f))
                for a, f in inputs
            ]
            + [ANYWHERE] * len(after),
            out_specs=[pl.BlockSpec((LANES, cols), lambda i, p: (i, 0)) for cols, _ in outputs],
        ),
        out_shape=[jax.ShapeDtypeStruct((steps * LANES, cols), kind) for cols, kind in outputs],
        compiler_params=pltpu.CompilerParams(
            dimension_semantics=("arbitrary",), vmem_limit_bytes=VMEM_LIMIT
        ),
        cost_estimate=lasts(0.01),
        name=name,
    )(place, *[a for a, _ in inputs], *after)


def to_owners(w, wo):
    after = yield
    packed, extra = w.shape[1], wo.shape[1]
    if lax.axis_size("fsdp") != 4 or lax.axis_size("ctx") != 2 or w.shape[0] != 8 * LANES:
        both = jnp.concatenate([w, wo], 1)
        summed = lax.psum_scatter(both, ("fsdp", "ctx"), scatter_dimension=0, tiled=True)
        yield w
        yield w
        (summed,) = yield w, [summed]
        yield summed
        return

    def swapped(value, axis, bit):
        count = lax.axis_size(axis)
        return lax.ppermute(value, axis, [(i, i ^ bit) for i in range(count)])

    fsdp = lax.axis_index("fsdp")
    place = jnp.stack([fsdp % 2, fsdp // 2, lax.axis_index("ctx")]).astype(jnp.int32)
    cut = 1024
    rest = packed + extra - cut

    (sent,) = placed_call(
        other_core_kernel, 4, place,
        [(w, lambda i, p: 2 * i + 1 - p[2]), (wo, lambda i, p: 2 * i + 1 - p[2])],
        [(packed + extra, BF16)], "other_core", after,
    )
    come = swapped(sent, "ctx", 1)
    after = yield sent
    of = {
        "ka": lambda i, p: 2 * i + p[0],
        "sa": lambda i, p: 2 * i + 1 - p[0],
        "kb": lambda i, p: 2 * p[1] + i,
        "sb": lambda i, p: 2 * (1 - p[1]) + i,
    }

    def own(key):
        return lambda i, p: 2 * of[key](i, p) + p[2]

    keep_a, send_a, keep_b, send_b = placed_call(
        split_kernel, 2, place,
        [(w, own(key)) for key in ("ka", "sa", "kb", "sb")]
        + [(wo, own(key)) for key in ("kb", "sb")]
        + [(come, of[key]) for key in ("ka", "sa", "kb", "sb")],
        [(cut, F32), (cut, BF16), (rest, F32), (rest, BF16)], "split", after,
    )
    come_a, come_b = swapped(send_a, "fsdp", 1), swapped(send_b, "fsdp", 2)
    after = yield send_a
    y, not_y = (lambda i, p: p[1]), (lambda i, p: 1 - p[1])
    x, not_x = (lambda i, p: p[0]), (lambda i, p: 1 - p[0])
    keep_a, send_a, keep_b, send_b = placed_call(
        second_kernel, 1, place,
        [(keep_a, y), (come_a, y), (keep_a, not_y), (come_a, not_y)]
        + [(keep_b, x), (come_b, x), (keep_b, not_x), (come_b, not_x)],
        [(cut, F32), (cut, BF16), (rest, F32), (rest, BF16)], "second", after,
    )
    come_a, come_b = swapped(send_a, "fsdp", 2), swapped(send_b, "fsdp", 1)
    keep_a, keep_b = yield send_a, [keep_a, keep_b]
    yield jnp.concatenate([keep_a + come_a.astype(F32), keep_b + come_b.astype(F32)], 1)


def flip_kernel(value, out):
    out[...] = value[...].astype(F32).T.astype(out.dtype)


def flipped(value, after):
    rows, cols = value.shape
    return pl.pallas_call(
        ordered(flip_kernel, 1, len(after)),
        grid=(1,),
        in_specs=[pl.BlockSpec((rows, cols), lambda i: (0, 0))] + [ANYWHERE] * len(after),
        out_specs=pl.BlockSpec((cols, rows), lambda i: (0, 0)),
        out_shape=jax.ShapeDtypeStruct((cols, rows), value.dtype),
        cost_estimate=lasts(0.01),
        name="flip",
    )(value, *after)


def gathered_shards(own):
    rows = own.shape[0]
    if lax.axis_size("fsdp") != 4 or lax.axis_size("ctx") != 2:
        return [lax.all_gather(own, ("fsdp", "ctx"), axis=0, tiled=True)], [0]

    def swapped(value, axis, bit):
        count = lax.axis_size(axis)
        return lax.ppermute(value, axis, [(i, i ^ bit) for i in range(count)])

    half = rows // 2
    by_one, by_two = swapped(own, "fsdp", 1), swapped(own, "fsdp", 2)
    upper = swapped(by_two[:half], "fsdp", 1)
    under = swapped(by_one[half:], "fsdp", 2)
    mine = [own, by_one, by_two, upper, under]
    place = lax.axis_index("fsdp")
    core = lax.axis_index("ctx")
    shards, starts = [], []
    for other in (0, 1):
        for value, bits, offset in zip(mine, (0, 1, 2, 3, 3), (0, 0, 0, 0, half)):
            shards.append(swapped(value, "ctx", 1) if other else value)
            starts.append(((place ^ bits) * 2 + (core ^ other)) * rows + offset)
    return shards, starts


def token_marks(segment, before):
    rows = segment.shape[0]
    joined = jnp.concatenate([before, segment])
    marks = [joined[3 - j : 3 - j + rows] == segment for j in (1, 2, 3)]
    blocks = segment.reshape(-1, CHUNK)
    previous = jnp.concatenate([before[2:], blocks[:-1, -1]])
    marks.append((blocks == previous[:, None]).reshape(-1))
    marks.append((blocks == blocks[:, -1:]).reshape(-1))
    marks.append(segment)
    table = jnp.stack([mark.astype(F32) for mark in marks], 1)
    return jnp.pad(table, ((0, 0), (M1, LANES - M1 - len(marks))))


def body(
    hidden, segments, out_grad, norm_gain, w_zx, w_dt, w_bc, conv_x_w, conv_x_b,
    conv_bc_w, conv_bc_b, dt_bias, a_log, skip_d, out_gain, w_out,
):
    _, rows, width = hidden.shape
    inner = w_zx.shape[2]
    heads = w_dt.shape[1]
    head_size = inner // heads
    state_size = w_bc.shape[2]
    wide = inner + 2 * state_size
    taps = conv_x_w.shape[0]
    owned = w_zx.shape[0]
    shards = ("fsdp", "ctx")
    hid = hidden[0]
    cot = out_grad[0]
    segment = segments[0]

    packed = jnp.concatenate(
        [
            w_zx.reshape(owned, 2 * inner),
            w_bc.reshape(owned, 2 * state_size),
            w_dt, w_dt, w_dt, w_dt,
            norm_gain[:, None],
            jnp.zeros((owned, LANES - 4 * heads - 1), BF16),
        ],
        1,
    )
    w_shards, w_starts = gathered_shards(packed)
    w_starts = jnp.stack([jnp.asarray(start, jnp.int32) for start in w_starts])
    wo = lax.all_gather(
        flipped(w_out, tuple(w_shards[3:5])), shards, axis=0, tiled=True
    )

    edge, edge_segment = passed_along((hid[rows - EDGE :], segment[rows - 3 :]), "ctx", 1)
    tok = token_marks(segment, edge_segment)
    conv_rows = jnp.concatenate(
        [
            jnp.concatenate([conv_x_w, conv_bc_w.reshape(taps, -1)], 1),
            jnp.concatenate([conv_x_b, conv_bc_b.reshape(-1)])[None],
            jnp.zeros((8 - taps - 1, wide), F32),
        ],
        0,
    )
    spare = jnp.zeros((LANES - 4 * heads,), F32)
    rate = -jnp.exp(a_log)
    dtp = jnp.concatenate(
        [
            jnp.concatenate([dt_bias] * 4 + [spare])[None],
            jnp.concatenate([rate] * 4 + [spare])[None],
            jnp.zeros((6, LANES), F32),
        ],
        0,
    )
    prm = jnp.concatenate(
        [jnp.repeat(skip_d, head_size)[None], out_gain[None], jnp.zeros((6, inner), F32)], 0
    )

    normed, gate, pre, u, rec, st, pdx, state_end, decay_end, w_in, gain = front(
        hid, edge, tok, w_shards, w_starts, 4 * heads, conv_rows, dtp, inner, wide
    )
    sin = chained(state_end, decay_end[:1], "ctx", 1)
    inner_total = inner * lax.axis_size("tp")
    me = lax.axis_index("tp")
    outer = jnp.full((8, LANES), (me == 0) | (me == lax.axis_size("tp") - 1), F32)

    scan, dgate, sums, *parts = middle(u, rec, gate, st, pdx, sin, cot, wo, prm)
    sums, *parts = total_over_row(sums, parts)
    out_sums = [LineSum(part) for part in parts]
    dscan, dgr, glow, adj, psx, adj_start, out_gain_acc = turn(
        scan, gate, dgate, sums, u, rec, prm, inner_total
    )
    ain = chained(adj_start, decay_end[:1], "ctx", -1)
    contract_rows = (((0,), (0,)), ((), ()))
    wo_grad = lax.dot_general(cot, glow, contract_rows, preferred_element_type=F32)

    group_rows = rows // GROUPS
    backs = [None] * GROUPS
    rears = [None] * GROUPS
    d_normed = [None] * GROUPS
    follows = [None] * GROUPS

    def run_back(group, after):
        backs[group] = back(u, rec, dscan, st, pdx, sin, adj, psx, ain, prm, dtp, after, group)
        start = jnp.concatenate(
            [backs[group][0][:8], rec[group * group_rows : group * group_rows + 8]], 1
        )
        if group == 0:
            follows[GROUPS - 1] = passed_along(start, "ctx", -1)
        else:
            follows[group - 1] = start

    def run_rear(group, after):
        rears[group] = rear(
            backs[group][0], rec, pre, dgr, backs[group][1], follows[group], w_in,
            conv_rows, after, group,
        )

    def settle(group, filled, after=()):
        total = out_sums[group]
        return by_group(
            functools.partial(settle_kernel, float(inner_total)), hid, BF16, group, filled is None,
            [
                (hid, "all"),
                (sums, "columns"),
                (total.given, "group"),
                (total.across, "group"),
                (outer, "whole"),
            ],
            outer if filled is None else filled, after, "settle",
        )

    def finish(group, filled, after, held=()):
        total = d_normed[group]
        return by_group(
            finish_kernel, hid, F32, group, filled is None,
            [
                (hid, "all"),
                (cot, "all"),
                (gain, "whole"),
                (total.given, "group"),
                (total.across, "group"),
                (outer, "whole"),
            ],
            outer if filled is None else filled, after, "finish", held,
        )

    sum_a, sum_b = out_sums
    run_back(0, (wo_grad,))
    done = advance([sum_a], (backs[0][3],))
    run_back(1, done)
    run_rear(0, (backs[1][3],))
    d_normed[0], done = advance_and_begin([sum_b, sum_a], rears[0][1], outer, (rears[0][2],))
    run_rear(1, done)

    conv_acc = sum(r[2] for r in rears)
    skip_acc = sum(b[2][0] for b in backs)
    head_acc = sum(b[3] for b in backs)

    dproj = jnp.concatenate([r[0] for r in rears], 0)
    w_grad = lax.dot_general(normed, dproj, contract_rows, preferred_element_type=F32)
    owners = to_owners(w_grad, wo_grad)
    next(owners)
    d_normed[1], done = advance_and_begin(
        [sum_b], rears[1][1], outer, (w_grad[:8, :LANES],)
    )
    sum_c, sum_d = d_normed
    done = advance([sum_c], done)
    block_out = settle(0, None, done)
    owners.send((block_out,))
    done = advance([sum_c], (block_out,))
    sent = owners.send(done)
    done = advance([sum_d], done + (sent,))
    block_out = settle(1, block_out, done)
    sent, kept = owners.send((block_out,))
    done = advance([sum_d], (sent,))
    hidden_grad, kept = finish(0, None, done, kept)
    both_owned = owners.send(kept)
    hidden_grad = finish(1, hidden_grad, ())
    w_owned, wo_owned = both_owned[:, : w_grad.shape[1]], both_owned[:, w_grad.shape[1] :]

    small = jnp.concatenate(
        [
            conv_acc[: taps + 1].reshape(-1),
            out_gain_acc[0],
            skip_acc,
            head_acc[:2].reshape(-1),
        ]
    )
    small = butterfly_sum(butterfly_sum(small, "ctx"), "fsdp")
    conv_sum = small[: (taps + 1) * wide].reshape(taps + 1, wide)
    rest = small[(taps + 1) * wide :]
    shared = jnp.concatenate(
        [
            w_owned[:, 2 * inner : 2 * inner + 2 * state_size].reshape(-1),
            jnp.sum(packed.astype(F32) * w_owned, 1),
            conv_sum[:, inner:].reshape(-1),
        ]
    )
    shared = butterfly_sum(shared, "tp")
    bc_size = owned * 2 * state_size
    bc_owned = shared[:bc_size].reshape(owned, 2, state_size)
    gain_owned = shared[bc_size : bc_size + owned] / norm_gain.astype(F32)
    conv_bc = shared[bc_size + owned :].reshape(taps + 1, 2, state_size)

    return (
        block_out[None],
        hidden_grad[None],
        gain_owned,
        w_owned[:, : 2 * inner].reshape(owned, 2, inner),
        w_owned[:, 2 * inner + 2 * state_size : 2 * inner + 2 * state_size + heads],
        bc_owned,
        conv_sum[:taps, :inner],
        conv_sum[taps, :inner],
        conv_bc[:taps],
        conv_bc[taps],
        rest[2 * inner : 2 * inner + heads],
        rest[2 * inner + LANES : 2 * inner + LANES + heads],
        jnp.sum(rest[inner : 2 * inner].reshape(heads, head_size), 1),
        rest[:inner],
        wo_owned.T,
    )


def solution(mesh):
    placed = (
        P("fsdp", "ctx", None),
        P("fsdp", "ctx"),
        P("fsdp", "ctx", None),
        P(("fsdp", "ctx")),
        P(("fsdp", "ctx"), None, "tp"),
        P(("fsdp", "ctx"), "tp"),
        P(("fsdp", "ctx"), None, None),
        P(None, "tp"),
        P("tp"),
        P(),
        P(),
        P("tp"),
        P("tp"),
        P("tp"),
        P("tp"),
        P("tp", ("fsdp", "ctx")),
    )
    return jax.shard_map(
        body,
        mesh=mesh,
        in_specs=placed,
        out_specs=(
            P("fsdp", "ctx", None),
            P("fsdp", "ctx", None),
            P(("fsdp", "ctx")),
            P(("fsdp", "ctx"), None, "tp"),
            P(("fsdp", "ctx"), "tp"),
            P(("fsdp", "ctx"), None, None),
            P(None, "tp"),
            P("tp"),
            P(),
            P(),
            P("tp"),
            P("tp"),
            P("tp"),
            P("tp"),
            P("tp", ("fsdp", "ctx")),
        ),
        check_vma=False,
    )
```
